32 devices in a mesh: dp: 8 (over z, x), tensor: 4 (over y, core).
Axes of the slice: x: 2, y: 2, z: 4, core: 2. Of those that a mesh axis runs over, the one named last changes fastest.
Arguments:
- block_input: bfloat16 [16, 512, 768], P('dp')
- segment_lengths: int32 [16, 4], P('dp'), may hold values from 1 to 256, 512 in all within a row
- entry_master: float32 [3, 768, 768], P(None, 'dp', 'tensor')
- mixer_master: float32 [768, 768], P('tensor', 'dp')
- expand_master: float32 [768, 3072], P('dp', 'tensor')
- shrink_master: float32 [3072, 768], P('tensor', 'dp')
- block_vectors: float32 [6, 768], replicated
- block_cotangent: bfloat16 [16, 512, 768], P('dp'), may hold values from -6 to 6
- entry_moment: float32 [3, 768, 768], P(None, 'dp', 'tensor'), may hold values from -0.005859375 to 0.005859375
- entry_square: float32 [3, 768, 768], P(None, 'dp', 'tensor'), may hold values from 7.059658e-08 to 3.8122153e-07
- mixer_moment: float32 [768, 768], P('tensor', 'dp'), may hold values from -0.005859375 to 0.005859375
- mixer_square: float32 [768, 768], P('tensor', 'dp'), may hold values from 7.059658e-08 to 3.8122153e-07
- expand_moment: float32 [768, 3072], P('dp', 'tensor'), may hold values from -0.005859375 to 0.005859375
- expand_square: float32 [768, 3072], P('dp', 'tensor'), may hold values from 7.059658e-08 to 3.8122153e-07
- shrink_moment: float32 [3072, 768], P('tensor', 'dp'), may hold values from -0.005859375 to 0.005859375
- shrink_square: float32 [3072, 768], P('tensor', 'dp'), may hold values from 7.059658e-08 to 3.8122153e-07
- vector_moment: float32 [6, 768], P(None, 'dp'), may hold values from -0.005859375 to 0.005859375
- vector_square: float32 [6, 768], P(None, 'dp'), may hold values from 7.059658e-08 to 3.8122153e-07
Outputs:
- block_output: bfloat16 [16, 512, 768], P('dp')
- input_gradient: float32 [16, 512, 768], P('dp')
- gradient_norm: float32 [], replicated
- entry_drift: float32 [3, 768, 768], P(None, 'dp', 'tensor')
- entry_energy: float32 [3, 768, 768], P(None, 'dp', 'tensor')
- entry_weights: float32 [3, 768, 768], P(None, 'dp', 'tensor')
- entry_bfloat: bfloat16 [3, 768, 768], P(None, 'dp', 'tensor')
- mixer_drift: float32 [768, 768], P('tensor', 'dp')
- mixer_energy: float32 [768, 768], P('tensor', 'dp')
- mixer_weights: float32 [768, 768], P('tensor', 'dp')
- mixer_bfloat: bfloat16 [768, 768], P('tensor', 'dp')
- expand_drift: float32 [768, 3072], P('dp', 'tensor')
- expand_energy: float32 [768, 3072], P('dp', 'tensor')
- expand_weights: float32 [768, 3072], P('dp', 'tensor')
- expand_bfloat: bfloat16 [768, 3072], P('dp', 'tensor')
- shrink_drift: float32 [3072, 768], P('tensor', 'dp')
- shrink_energy: float32 [3072, 768], P('tensor', 'dp')
- shrink_weights: float32 [3072, 768], P('tensor', 'dp')
- shrink_bfloat: bfloat16 [3072, 768], P('tensor', 'dp')
- vector_drift: float32 [6, 768], P(None, 'dp')
- vector_energy: float32 [6, 768], P(None, 'dp')
- vector_values: float32 [6, 768], P(None, 'dp')
The draws below stay inside these ranges and needn't reach their ends.
Inputs may be any that keep to these rules, and one draw needn't show every extreme that they name: `segment_lengths`: each row's segment lengths sum to 512, and in every row the largest is 256.
All inputs are finite; a program needn't handle non-finite values.
Results may differ from the reference program's by a relative error of at most 0.014.
The reference program's roundings to bfloat16 on the way count: a program that leaves them out, or rounds other values in their place, can miss the bound.
Values may be sent and summed in bfloat16 or wider, within the bound.
No kernel may reach another device: no remote copies, remote signals or barrier semaphores. Data moves between devices by JAX's collectives and lax.ppermute only.
A program may use at most 128 MiB of HBM per device.

```python
import math
import jax
import jax.numpy as jnp
import numpy as np
from jax import lax

D = 768
HEADS = 12
HD = 64
FF = 3072
SEQ_LEN = 512
SEGS = 4
ADAM_STEP = 3
ROWS = 16


def ramp(count, low_end, high_end):
    place = jnp.arange(count, dtype=jnp.float32) / max(count - 1, 1)
    return low_end * (high_end / low_end) ** place


def shaped(base, key, axis, fan, low_end, high_end):
    count = base.shape[axis]
    form = [1] * base.ndim
    form[axis] = count
    rough = jax.random.uniform(jax.random.fold_in(key, 7), base.shape, jnp.float32, 0.75, 1.35)
    return base * rough * ramp(count, low_end, high_end).reshape(form) * fan ** (-0.5)


def draw_block_input(key, part):
    key = jax.random.fold_in(key, 15)
    shape = (ROWS, SEQ_LEN, D)
    base = jnp.clip(jax.random.normal(key, shape, jnp.float32), -6.0, 6.0)
    return shaped(base, key, 2, 1.0, 0.6, 1.8).astype(jnp.bfloat16)


def draw_entry_master(key, part):
    key = jax.random.fold_in(key, 11)
    shape = (3, D, HEADS * HD)
    base = jnp.clip(jax.random.normal(key, shape, jnp.float32), -6.0, 6.0)
    return shaped(base, key, 2, D, 0.7, 1.4)


def draw_mixer_master(key, part):
    key = jax.random.fold_in(key, 12)
    shape = (HEADS * HD, D)
    base = jnp.clip(jax.random.normal(key, shape, jnp.float32), -6.0, 6.0)
    return shaped(base, key, 0, HEADS * HD / 16.0, 0.7, 1.4)


def draw_expand_master(key, part):
    key = jax.random.fold_in(key, 13)
    shape = (D, FF)
    base = jnp.clip(jax.random.normal(key, shape, jnp.float32), -6.0, 6.0)
    return shaped(base, key, 1, D, 0.7, 1.4)


def draw_shrink_master(key, part):
    key = jax.random.fold_in(key, 14)
    shape = (FF, D)
    base = jnp.clip(jax.random.normal(key, shape, jnp.float32), -6.0, 6.0)
    return shaped(base, key, 0, FF, 0.7, 1.4)


def draw_block_vectors(key, part):
    key = jax.random.fold_in(key, 16)
    shape = (6, D)
    noise = jnp.clip(jax.random.normal(key, shape, jnp.float32), -6.0, 6.0)
    low_end, high_end = (0.6, 1.8)
    line = ramp(D, low_end, high_end)
    gain_one = line * jax.random.uniform(jax.random.fold_in(key, 1), (D,), jnp.float32, 0.75, 1.35)
    gain_two = line * jax.random.uniform(jax.random.fold_in(key, 2), (D,), jnp.float32, 0.75, 1.35)
    return jnp.stack([0.3 * noise[0], 0.3 * noise[1], gain_one, 0.3 * noise[3], gain_two, 0.3 * noise[5]])


def block_levels(rng, dims, cuts, least, top_value):
    factor_of = 1.0
    for position, blocks in cuts:
        draws = jax.random.uniform(jax.random.fold_in(jax.random.fold_in(rng, 6), position), (blocks,), jnp.float32, least / len(cuts), top_value / len(cuts))
        factor_of = factor_of * jnp.repeat(jnp.exp(draws), dims[position] // blocks).reshape((-1,) + (1,) * (len(dims) - 1 - position))
    return factor_of


def split_up(amount, total, bound, lean):
    portions = [(1 << 20) // math.isqrt(rank ** lean) + 1 for rank in range(2, amount + 1)]
    spare, holding = total - bound - (amount - 1), [1] * (amount - 1)
    while spare > 0:
        movable = [i for i in range(amount - 1) if holding[i] < bound]
        mass, budget = sum([portions[i] for i in movable]), spare
        for i in movable:
            addition = min(bound - holding[i], max(1, budget * portions[i] // mass), spare)
            holding[i] = holding[i] + addition
            spare = spare - addition
    return np.array([bound] + holding)


def uneven_parts(stream_key, number_of, total, bound, skew):
    if number_of == 2:
        one = jax.random.randint(stream_key, (), max(1, total - bound), min(bound, total - 1) + 1)
        return jnp.stack([one, total - one])
    sizes = jnp.asarray(split_up(number_of, total, bound, skew), jnp.int32)
    couples = (number_of - 1) // 2
    donor, sink = sizes[1:1 + 2 * couples:2], sizes[2:2 + 2 * couples:2]
    room = jnp.minimum(donor - 1, bound - sink)
    passed = jax.random.randint(jax.random.fold_in(stream_key, 1), (couples,), 0, 1 << 20) % (room + 1)
    sizes = sizes.at[1:1 + 2 * couples:2].set(donor - passed).at[2:2 + 2 * couples:2].set(sink + passed)
    return sizes[jax.random.permutation(jax.random.fold_in(stream_key, 2), number_of)]


def normal_values(stream_key, dims, width, most, shards=(), kind=jnp.bfloat16):
    entries = width * jax.random.normal(stream_key, dims, jnp.float32)
    if shards:
        entries = entries * block_levels(stream_key, dims, shards, -0.22, 0.18)
    return jnp.clip(entries, -most, most).astype(kind)


def setup_inputs(seed: int = 0) -> dict:
    arg_keys = jax.random.split(jax.random.key(seed), 19)
    block_input = draw_block_input(jax.random.fold_in(arg_keys[18], 71), 0)
    segment_lengths = jax.vmap(lambda own: uneven_parts(own, SEGS, SEQ_LEN, SEQ_LEN // 2, 1))(jax.random.split(arg_keys[1], ROWS)).reshape((ROWS, SEGS)).astype(jnp.int32)
    entry_master = draw_entry_master(jax.random.fold_in(arg_keys[18], 71), 0)
    mixer_master = draw_mixer_master(jax.random.fold_in(arg_keys[18], 71), 0)
    expand_master = draw_expand_master(jax.random.fold_in(arg_keys[18], 71), 0)
    shrink_master = draw_shrink_master(jax.random.fold_in(arg_keys[18], 71), 0)
    block_vectors = draw_block_vectors(jax.random.fold_in(arg_keys[18], 71), 0)
    block_cotangent = normal_values(arg_keys[7], (ROWS, SEQ_LEN, D), 1.0, 6.0, ((0, 8),))
    entry_moment = normal_values(arg_keys[8], (3, D, HEADS * HD), ((4 * D * HEADS * HD + 2 * D * FF + 6 * D) ** -0.5), 0.005859375, ((1, 8), (2, 4)), jnp.float32)
    entry_square = jnp.clip(7.059657747277015e-08 + 3.10624947985616e-07 * jax.random.uniform(arg_keys[9], (3, D, HEADS * HD), jnp.float32) ** block_levels(arg_keys[9], (3, D, HEADS * HD), ((1, 8), (2, 4)), -0.2, 0.2), 7.059657747277015e-08, 3.8122152545838617e-07)
    mixer_moment = normal_values(arg_keys[10], (HEADS * HD, D), ((4 * D * HEADS * HD + 2 * D * FF + 6 * D) ** -0.5), 0.005859375, ((0, 4), (1, 8)), jnp.float32)
    mixer_square = jnp.clip(7.059657747277015e-08 + 3.10624947985616e-07 * jax.random.uniform(arg_keys[11], (HEADS * HD, D), jnp.float32) ** block_levels(arg_keys[11], (HEADS * HD, D), ((0, 4), (1, 8)), -0.2, 0.2), 7.059657747277015e-08, 3.8122152545838617e-07)
    expand_moment = normal_values(arg_keys[12], (D, FF), ((4 * D * HEADS * HD + 2 * D * FF + 6 * D) ** -0.5), 0.005859375, ((0, 8), (1, 4)), jnp.float32)
    expand_square = jnp.clip(7.059657747277015e-08 + 3.10624947985616e-07 * jax.random.uniform(arg_keys[13], (D, FF), jnp.float32) ** block_levels(arg_keys[13], (D, FF), ((0, 8), (1, 4)), -0.2, 0.2), 7.059657747277015e-08, 3.8122152545838617e-07)
    shrink_moment = normal_values(arg_keys[14], (FF, D), ((4 * D * HEADS * HD + 2 * D * FF + 6 * D) ** -0.5), 0.005859375, ((0, 4), (1, 8)), jnp.float32)
    shrink_square = jnp.clip(7.059657747277015e-08 + 3.10624947985616e-07 * jax.random.uniform(arg_keys[15], (FF, D), jnp.float32) ** block_levels(arg_keys[15], (FF, D), ((0, 4), (1, 8)), -0.2, 0.2), 7.059657747277015e-08, 3.8122152545838617e-07)
    vector_moment = normal_values(arg_keys[16], (6, D), ((4 * D * HEADS * HD + 2 * D * FF + 6 * D) ** -0.5), 0.005859375, ((1, 8),), jnp.float32)
    vector_square = jnp.clip(7.059657747277015e-08 + 3.10624947985616e-07 * jax.random.uniform(arg_keys[17], (6, D), jnp.float32) ** block_levels(arg_keys[17], (6, D), ((1, 8),), -0.2, 0.2), 7.059657747277015e-08, 3.8122152545838617e-07)
    return dict(block_input=block_input, segment_lengths=segment_lengths, entry_master=entry_master, mixer_master=mixer_master, expand_master=expand_master, shrink_master=shrink_master, block_vectors=block_vectors, block_cotangent=block_cotangent, entry_moment=entry_moment, entry_square=entry_square, mixer_moment=mixer_moment, mixer_square=mixer_square, expand_moment=expand_moment, expand_square=expand_square, shrink_moment=shrink_moment, shrink_square=shrink_square, vector_moment=vector_moment, vector_square=vector_square)


@jax.custom_vjp
def low(v):
    return lax.optimization_barrier(v.astype(jnp.bfloat16)).astype(jnp.float32)

@jax.custom_vjp
def low_back(v):
    return v

def low_keep(v):
    return (low(v), None)

def low_pass(kept, grad):
    return (grad,)

def back_keep(v):
    return (v, None)

def back_low(kept, grad):
    return (low(grad),)
low.defvjp(low_keep, low_pass)
low_back.defvjp(back_keep, back_low)
norm_eps = 1e-12
clip_bound = 1.0
beta_first = 0.5
beta_second = 0.6
adam_eps = 1e-08
rate_matrix = 0.02
rate_mixer = 0.08
rate_vector = 0.25
decay_matrix = 0.01
group_rows = 8
highest = lax.Precision.HIGHEST

def layer_norm(value, gain, shift):
    mean = lax.optimization_barrier(jnp.mean(value, axis=-1, keepdims=True))
    centered = value - mean
    spread = lax.optimization_barrier(jnp.mean(centered * centered, axis=-1, keepdims=True))
    return centered * lax.rsqrt(spread + norm_eps) * gain + shift

def exact_gelu(value):
    return jax.nn.gelu(value, approximate=False)

def attend_row(packed):
    queries, key_rows, value_rows, segment = packed
    raw = jnp.einsum('qhe,khe->hqk', queries, key_rows, precision=highest) * HD ** (-0.5)
    allowed = segment[:, None] == segment[None, :]
    scores = jnp.where(allowed[None], raw, -1e+30)
    scores = low_back(scores)
    probs = jax.nn.softmax(scores, axis=-1)
    attended = jnp.einsum('hqk,khe->qhe', low(probs), value_rows, precision=highest)
    return attended.reshape(SEQ_LEN, HEADS * HD)

def forward(inputs, segment, entry_w, mixer_w, expand_w, shrink_w, vectors):
    entry_low = low(entry_w)
    mixer_low = low(mixer_w)
    expand_low = low(expand_w)
    shrink_low = low(shrink_w)
    flat = inputs.reshape(-1, D)
    projected = jnp.einsum('nd,cdf->cnf', flat, entry_low, precision=highest)
    projected = low(low_back(projected))
    split = projected.reshape(3, group_rows, SEQ_LEN, HEADS, HD)
    attended = lax.map(jax.checkpoint(attend_row), (split[0], split[1], split[2], segment))
    attended = low(low_back(attended.reshape(-1, HEADS * HD)))
    mixed = low_back(jnp.dot(attended, mixer_low, precision=highest))
    first_in = flat + mixed + vectors[0]
    normed = layer_norm(first_in, vectors[2], vectors[3])
    expanded = low_back(jnp.dot(low(normed), expand_low, precision=highest))
    activated = low(exact_gelu(expanded))
    shrunk = low_back(jnp.dot(activated, shrink_low, precision=highest))
    second_in = normed + shrunk + vectors[1]
    final = layer_norm(second_in, vectors[4], vectors[5])
    return final.reshape(group_rows, SEQ_LEN, D)

def adam_update(grad, moment, square, master, factor, rate, decay):
    clipped = grad * factor
    moment_new = beta_first * moment + (1.0 - beta_first) * clipped
    square_new = beta_second * square + (1.0 - beta_second) * clipped * clipped
    corrected = moment_new / (1.0 - beta_first ** ADAM_STEP)
    scaled = square_new / (1.0 - beta_second ** ADAM_STEP)
    master_new = master - rate * (corrected / (jnp.sqrt(scaled) + adam_eps) + decay * master)
    return (moment_new, square_new, master_new)

def reference(block_input, segment_lengths, entry_master, mixer_master, expand_master, shrink_master, block_vectors, block_cotangent, entry_moment, entry_square, mixer_moment, mixer_square, expand_moment, expand_square, shrink_moment, shrink_square, vector_moment, vector_square):
    ends = jnp.cumsum(segment_lengths, axis=1).astype(jnp.int32)
    positions = jnp.arange(SEQ_LEN, dtype=jnp.int32)
    segment = lax.optimization_barrier(jnp.sum((positions[None, :, None] >= ends[:, None, :]).astype(jnp.int32), axis=-1)).astype(jnp.int32)
    groups = ROWS // group_rows
    inputs = block_input.astype(jnp.float32).reshape(groups, group_rows, SEQ_LEN, D)
    cotangent = block_cotangent.astype(jnp.float32).reshape(groups, group_rows, SEQ_LEN, D)
    segment = segment.reshape(groups, group_rows, SEQ_LEN)
    params = (entry_master, mixer_master, expand_master, shrink_master, block_vectors)

    def group_step(carry, item):
        rows_in, rows_segment, rows_cot = item

        def run(values, entry_w, mixer_w, expand_w, shrink_w, vectors):
            return forward(values, rows_segment, entry_w, mixer_w, expand_w, shrink_w, vectors)
        result, back = jax.vjp(run, rows_in, *params)
        grads = back(rows_cot)
        carry = tuple((total + piece for total, piece in zip(carry, grads[1:])))
        return (carry, (result.astype(jnp.bfloat16), grads[0]))
    start = tuple((jnp.zeros(piece.shape, jnp.float32) for piece in params))
    totals, (outputs, input_grads) = lax.scan(group_step, start, (inputs, segment, cotangent))
    block_output = outputs.reshape(ROWS, SEQ_LEN, D)
    input_gradient = input_grads.reshape(ROWS, SEQ_LEN, D)
    squares = sum((jnp.sum(piece * piece) for piece in totals))
    gradient_norm = jnp.sqrt(squares)
    factor = jnp.minimum(1.0, clip_bound / (gradient_norm + 1e-06))
    entry_drift, entry_energy, entry_weights = adam_update(totals[0], entry_moment, entry_square, entry_master, factor, rate_matrix, decay_matrix)
    mixer_drift, mixer_energy, mixer_weights = adam_update(totals[1], mixer_moment, mixer_square, mixer_master, factor, rate_mixer, decay_matrix)
    expand_drift, expand_energy, expand_weights = adam_update(totals[2], expand_moment, expand_square, expand_master, factor, rate_matrix, decay_matrix)
    shrink_drift, shrink_energy, shrink_weights = adam_update(totals[3], shrink_moment, shrink_square, shrink_master, factor, rate_matrix, decay_matrix)
    vector_drift, vector_energy, vector_values = adam_update(totals[4], vector_moment, vector_square, block_vectors, factor, rate_vector, 0.0)
    return (block_output, input_gradient, gradient_norm, entry_drift, entry_energy, entry_weights, entry_weights.astype(jnp.bfloat16), mixer_drift, mixer_energy, mixer_weights, mixer_weights.astype(jnp.bfloat16), expand_drift, expand_energy, expand_weights, expand_weights.astype(jnp.bfloat16), shrink_drift, shrink_energy, shrink_weights, shrink_weights.astype(jnp.bfloat16), vector_drift, vector_energy, vector_values)
```

```python
import jax
import jax.numpy as jnp
from jax import lax
from jax.sharding import PartitionSpec as P

HD = 64
ADAM_STEP = 3


norm_eps = 1e-12
clip_bound = 1.0
beta_first = 0.5
beta_second = 0.6
adam_eps = 1e-08
rate_matrix = 0.02
rate_mixer = 0.08
rate_vector = 0.25
decay_matrix = 0.01


def layer_norm(value, gain, shift):
    mean = jnp.mean(value, axis=-1, keepdims=True)
    centered = value - mean
    spread = jnp.mean(centered * centered, axis=-1, keepdims=True)
    return centered * lax.rsqrt(spread + norm_eps) * gain + shift


def exact_gelu(value):
    return jax.nn.gelu(value, approximate=False)


def adam_update(grad, moment, square, master, factor, rate, decay):
    clipped = grad * factor
    moment_new = beta_first * moment + (1.0 - beta_first) * clipped
    square_new = beta_second * square + (1.0 - beta_second) * clipped * clipped
    corrected = moment_new / (1.0 - beta_first**ADAM_STEP)
    scaled = square_new / (1.0 - beta_second**ADAM_STEP)
    master_new = master - rate * (corrected / (jnp.sqrt(scaled) + adam_eps) + decay * master)
    return (moment_new, square_new, master_new)


def cores(value):
    size = lax.axis_size("tensor")
    return lax.ppermute(value, "tensor", [(i, i ^ 1) for i in range(size)])


def planes(value):
    size = lax.axis_size("tensor")
    return lax.ppermute(value, "tensor", [(i, i ^ 2) for i in range(size)])


def ring_order(size):
    return list(range(0, size, 2)) + list(range(size - 1, 0, -2))


def turn(value, step):
    size = lax.axis_size("dp")
    ring = ring_order(size)
    pairs = [(ring[i], ring[(i + step) % size]) for i in range(size)]
    return lax.ppermute(value, "dp", pairs)


RING_LIMIT = 16


def owner_at(step):
    size = lax.axis_size("dp")
    place = lax.axis_index("dp")
    seat = jnp.where(place % 2 == 0, place // 2, size - 1 - place // 2)
    return jnp.array(ring_order(size), jnp.int32)[(seat + step) % size]


def ring_gather(block):
    size = lax.axis_size("dp")
    if size > RING_LIMIT:
        every = lax.all_gather(block, "dp", axis=0)
        return [lax.dynamic_index_in_dim(every, owner_at(i), 0, False) for i in range(size)]
    found = {0: block}
    ahead = behind = block
    for step in range(1, size // 2 + 1):
        behind = turn(behind, 1)
        found[size - step] = behind
        if step < size - step:
            ahead = turn(ahead, -1)
            found[step] = ahead
    return [found[i] for i in range(size)]


def ring_scatter(matrix):
    size = lax.axis_size("dp")
    share = matrix.shape[0] // size
    if size > RING_LIMIT:
        return lax.psum_scatter(matrix.astype(jnp.float32), "dp", scatter_dimension=0, tiled=True)

    def part(step):
        rows = lax.dynamic_slice_in_dim(matrix, owner_at(step) * share, share, 0)
        return rows.astype(jnp.float32)

    far = size // 2
    behind = part(far).astype(jnp.bfloat16)
    ahead = part(far + 1).astype(jnp.bfloat16)
    for step in range(1, far):
        behind = (turn(behind, 1).astype(jnp.float32) + part(far - step)).astype(jnp.bfloat16)
        if step < far - 1:
            ahead = turn(ahead, -1).astype(jnp.float32) + part(far + 1 + step)
            ahead = ahead.astype(jnp.bfloat16)
    total = part(0) + turn(behind, 1).astype(jnp.float32)
    return total + turn(ahead, -1).astype(jnp.float32)


def shards(
    block_input,
    segment_lengths,
    entry_master,
    mixer_master,
    expand_master,
    shrink_master,
    block_vectors,
    block_cotangent,
    entry_moment,
    entry_square,
    mixer_moment,
    mixer_square,
    expand_moment,
    expand_square,
    shrink_moment,
    shrink_square,
    vector_moment,
    vector_square,
):
    rows, length, width = block_input.shape
    low = jnp.bfloat16
    wide = jnp.float32
    members = lax.axis_size("dp")
    place = lax.axis_index("dp")
    spot = lax.axis_index("tensor")
    core = spot % 2
    plane = spot // 2
    share = width // members
    heads_width = entry_master.shape[2]

    def assemble(blocks):
        whole = jnp.zeros((width, blocks[0].shape[1]), low)
        for step, block in enumerate(blocks):
            whole = lax.dynamic_update_slice(whole, block, (owner_at(step) * share, 0))
        return whole

    attend_shard = jnp.concatenate(
        [entry_master[0], entry_master[1], entry_master[2], mixer_master.T], axis=1
    ).astype(low)
    feed_shard = jnp.concatenate([expand_master, shrink_master.T], axis=1).astype(low)
    attend_pair = jnp.concatenate([attend_shard, planes(attend_shard)], axis=1)
    attend_w = assemble(ring_gather(attend_pair))
    feed_blocks = ring_gather(feed_shard)
    feed_others = [planes(block) for block in feed_blocks]
    feed_w = assemble([jnp.concatenate(pair, axis=1) for pair in zip(feed_blocks, feed_others)])
    unit = width
    expand_w = jnp.concatenate([feed_w[:, :unit], feed_w[:, 2 * unit : 3 * unit]], axis=1)
    shrink_w = jnp.concatenate([feed_w[:, unit : 2 * unit], feed_w[:, 3 * unit :]], axis=1)
    pieces = [
        [attend_w[:, (4 * p + c) * heads_width : (4 * p + c + 1) * heads_width] for p in (0, 1)]
        for c in range(4)
    ]
    entry_w = jnp.stack([jnp.concatenate(pieces[c], axis=1) for c in range(3)])
    mixer_w = jnp.concatenate(pieces[3], axis=1)

    own_rows = rows // 2
    tokens = own_rows * length
    inputs = lax.dynamic_slice_in_dim(block_input, plane * own_rows, own_rows, 0)
    inputs = inputs.reshape(tokens, width)
    incoming = lax.dynamic_slice_in_dim(block_cotangent, plane * own_rows, own_rows, 0)
    incoming = incoming.reshape(tokens, width).astype(wide)
    lengths = lax.dynamic_slice_in_dim(segment_lengths, plane * own_rows, own_rows, 0)
    local_width = 2 * heads_width
    heads_local = local_width // HD
    scale = HD ** (-0.5)
    projected = jnp.einsum("nd,cdf->cnf", inputs, entry_w, preferred_element_type=wide).astype(low)
    split = projected.reshape(3, own_rows, length, heads_local, HD)
    queries, key_rows, value_rows = (split[0], split[1], split[2])
    ends = jnp.cumsum(lengths, axis=1)
    positions = jnp.arange(length, dtype=jnp.int32)
    segment = jnp.sum((positions[None, :, None] >= ends[:, None, :]).astype(jnp.int32), axis=-1)
    allowed = segment[:, :, None] == segment[:, None, :]

    def scores_of():
        raw = jnp.einsum("rqhe,rkhe->rhqk", queries, key_rows, preferred_element_type=wide) * scale
        return jnp.where(allowed[:, None], raw, -1e30)

    scores = scores_of()
    peak = jnp.max(scores, axis=-1, keepdims=True)
    expd = jnp.exp(scores - peak)
    total = jnp.sum(expd, axis=-1, keepdims=True)
    log_total = peak + jnp.log(total)
    probs_low = (expd / total).astype(low)
    attended = jnp.einsum("rhqk,rkhe->rqhe", probs_low, value_rows, preferred_element_type=wide)
    attended = attended.astype(low).reshape(tokens, local_width)

    def nt(left, right):
        return lax.dot_general(left, right, (((1,), (1,)), ((), ())), preferred_element_type=wide)

    def tn(left, right):
        return lax.dot_general(left, right, (((0,), (0,)), ((), ())), preferred_element_type=wide)

    def both(value):
        return value + cores(value)

    mixed = both(nt(attended, mixer_w))
    first_in = inputs.astype(wide) + mixed + block_vectors[0]
    normed, first_back = jax.vjp(layer_norm, first_in, block_vectors[2], block_vectors[3])
    normed_low = normed.astype(low)
    expanded = jnp.dot(normed_low, expand_w, preferred_element_type=wide)
    activated, gelu_back = jax.vjp(exact_gelu, expanded)
    active_low = activated.astype(low)
    shrunk = both(nt(active_low, shrink_w))
    second_in = normed + shrunk + block_vectors[1]
    final, second_back = jax.vjp(layer_norm, second_in, block_vectors[4], block_vectors[5])
    block_output = final.astype(low).reshape(own_rows, length, width)
    second_grad, gain_two, shift_two = second_back(incoming)
    shrink_low = second_grad.astype(low)
    shrink_grad = tn(shrink_low, active_low).astype(low)
    active_grad = jnp.dot(shrink_low, shrink_w, preferred_element_type=wide)
    expand_low = gelu_back(active_grad)[0].astype(low)
    expand_grad = tn(normed_low, expand_low).astype(low)
    normed_grad = second_grad + both(nt(expand_low, expand_w))
    first_grad, gain_one, shift_one = first_back(normed_grad)
    vector_grad = jnp.stack(
        [
            jnp.sum(first_grad, axis=0),
            jnp.sum(second_grad, axis=0),
            gain_one,
            shift_one,
            gain_two,
            shift_two,
        ]
    )
    mixer_low = first_grad.astype(low)
    mixer_grad = tn(mixer_low, attended).astype(low)
    attended_grad = jnp.dot(mixer_low, mixer_w, preferred_element_type=wide)
    attended_grad = attended_grad.astype(low).reshape(own_rows, length, heads_local, HD)
    weights_again = jnp.exp(scores_of() - log_total)
    probs_again = weights_again.astype(low)
    prob_grad = jnp.einsum("rqhe,rkhe->rhqk", attended_grad, value_rows, preferred_element_type=wide)
    score_grad = weights_again * (
        prob_grad - jnp.sum(weights_again * prob_grad, axis=-1, keepdims=True)
    )
    score_low = score_grad.astype(low)
    query_grad = (
        jnp.einsum("rhqk,rkhe->rqhe", score_low, key_rows, preferred_element_type=wide) * scale
    ).astype(low)
    key_grad = (
        jnp.einsum("rhqk,rqhe->rkhe", score_low, queries, preferred_element_type=wide) * scale
    ).astype(low)
    value_grad = jnp.einsum(
        "rhqk,rqhe->rkhe", probs_again, attended_grad, preferred_element_type=wide
    ).astype(low)
    projected_grad = jnp.stack([query_grad, key_grad, value_grad]).reshape(3, tokens, local_width)
    entry_grad = jnp.einsum(
        "nd,cnf->cdf", inputs, projected_grad, preferred_element_type=wide
    ).astype(low)
    partial = jnp.einsum("cnf,cdf->nd", projected_grad, entry_w, preferred_element_type=wide)
    input_gradient = first_grad + both(partial.astype(low).astype(wide))

    def halves(matrix):
        middle = matrix.shape[-1] // 2
        return matrix[..., :middle], matrix[..., middle:]

    kept, sent = halves(shrink_grad)
    shrink_half = (kept + planes(sent)).astype(low)
    shrink_share = ring_scatter(shrink_half)
    expand_pair = ring_scatter(expand_grad)
    kept, sent = halves(expand_pair)
    expand_share = kept + planes(sent.astype(low)).astype(wide)
    quarters = [halves(entry_grad[c]) for c in range(3)] + [halves(mixer_grad)]
    vector_columns = jnp.pad(vector_grad.T, ((0, 0), (0, 122))).astype(low)
    attend_grad = jnp.concatenate(
        [q[0] for q in quarters] + [q[1] for q in quarters] + [vector_columns], axis=1
    )
    attend_sum = ring_scatter(attend_grad)
    swapped = planes(attend_sum[:, unit:].astype(low)).astype(wide)
    attend_share = attend_sum[:, :unit] + swapped[:, :unit]
    vector_share_grad = (attend_sum[:, 2 * unit :].astype(low).astype(wide) + swapped[:, unit:])[:, :6].T

    entry_share = jnp.stack(
        [attend_share[:, c * heads_width : (c + 1) * heads_width] for c in range(3)]
    )
    mixer_share = attend_share[:, 3 * heads_width :].T
    shares = (entry_share, mixer_share, expand_share, shrink_share.T, vector_share_grad)

    def other_rows(value):
        middle = length // 2
        half = lax.dynamic_slice_in_dim(value, core * middle, middle, 1)
        first = planes(half)
        second = cores(first)
        top = jnp.where(core == 0, first, second)
        bottom = jnp.where(core == 0, second, first)
        return jnp.concatenate([top, bottom], axis=1)

    def whole_rows(own, other):
        return jnp.where(
            plane == 0,
            jnp.concatenate([own, other], axis=0),
            jnp.concatenate([other, own], axis=0),
        )

    block_output = whole_rows(block_output, other_rows(block_output))
    input_gradient = input_gradient.reshape(own_rows, length, width)
    input_gradient = whole_rows(
        input_gradient, other_rows(input_gradient.astype(low)).astype(wide)
    )

    local_squares = jnp.sum(shares[0] * shares[0]) + jnp.sum(shares[1] * shares[1])
    local_squares = local_squares + jnp.sum(shares[2] * shares[2]) + jnp.sum(shares[3] * shares[3])
    local_squares = local_squares + jnp.sum(shares[4] * shares[4]) / lax.axis_size("tensor")
    squares = jnp.full((8, 128), local_squares)
    squares = squares + cores(squares)
    squares = squares + planes(squares)
    hop = 1
    while hop < members:
        squares = squares + lax.ppermute(squares, "dp", [(i, i ^ hop) for i in range(members)])
        hop *= 2
    gradient_norm = jnp.sqrt(squares[0, 0])
    factor = jnp.minimum(1.0, clip_bound / (gradient_norm + 1e-06))
    vector_width = block_vectors.shape[1] // members
    vector_share = lax.dynamic_slice_in_dim(block_vectors, place * vector_width, vector_width, 1)
    entry_drift, entry_energy, entry_weights = adam_update(
        shares[0], entry_moment, entry_square, entry_master, factor, rate_matrix, decay_matrix
    )
    mixer_drift, mixer_energy, mixer_weights = adam_update(
        shares[1], mixer_moment, mixer_square, mixer_master, factor, rate_mixer, decay_matrix
    )
    expand_drift, expand_energy, expand_weights = adam_update(
        shares[2], expand_moment, expand_square, expand_master, factor, rate_matrix, decay_matrix
    )
    shrink_drift, shrink_energy, shrink_weights = adam_update(
        shares[3], shrink_moment, shrink_square, shrink_master, factor, rate_matrix, decay_matrix
    )
    vector_drift, vector_energy, vector_values = adam_update(
        shares[4], vector_moment, vector_square, vector_share, factor, rate_vector, 0.0
    )
    return (
        block_output,
        input_gradient,
        gradient_norm,
        entry_drift,
        entry_energy,
        entry_weights,
        entry_weights.astype(jnp.bfloat16),
        mixer_drift,
        mixer_energy,
        mixer_weights,
        mixer_weights.astype(jnp.bfloat16),
        expand_drift,
        expand_energy,
        expand_weights,
        expand_weights.astype(jnp.bfloat16),
        shrink_drift,
        shrink_energy,
        shrink_weights,
        shrink_weights.astype(jnp.bfloat16),
        vector_drift,
        vector_energy,
        vector_values,
    )


def solution(mesh):
    in_specs = (
        P("dp", None, None),
        P("dp", None),
        P(None, "dp", "tensor"),
        P("tensor", "dp"),
        P("dp", "tensor"),
        P("tensor", "dp"),
        P(),
        P("dp", None, None),
        P(None, "dp", "tensor"),
        P(None, "dp", "tensor"),
        P("tensor", "dp"),
        P("tensor", "dp"),
        P("dp", "tensor"),
        P("dp", "tensor"),
        P("tensor", "dp"),
        P("tensor", "dp"),
        P(None, "dp"),
        P(None, "dp"),
    )
    out_specs = (
        P("dp", None, None),
        P("dp", None, None),
        P(),
        P(None, "dp", "tensor"),
        P(None, "dp", "tensor"),
        P(None, "dp", "tensor"),
        P(None, "dp", "tensor"),
        P("tensor", "dp"),
        P("tensor", "dp"),
        P("tensor", "dp"),
        P("tensor", "dp"),
        P("dp", "tensor"),
        P("dp", "tensor"),
        P("dp", "tensor"),
        P("dp", "tensor"),
        P("tensor", "dp"),
        P("tensor", "dp"),
        P("tensor", "dp"),
        P("tensor", "dp"),
        P(None, "dp"),
        P(None, "dp"),
        P(None, "dp"),
    )
    return jax.shard_map(shards, mesh=mesh, in_specs=in_specs, out_specs=out_specs, check_vma=False)
```

```python
import math

import jax
import jax.numpy as jnp
from jax import lax
from jax.experimental import pallas as pl
from jax.experimental.pallas import tpu as pltpu
from jax.sharding import PartitionSpec as P

HD = 64
ADAM_STEP = 3


norm_eps = 1e-12
clip_bound = 1.0
beta_first = 0.5
beta_second = 0.6
adam_eps = 1e-08
rate_matrix = 0.02
rate_mixer = 0.08
rate_vector = 0.25
decay_matrix = 0.01


low = jnp.bfloat16
wide = jnp.float32
RING_LIMIT = 16
VMEM_LIMIT = 48 * 2**20


def adam_update(grad, moment, square, master, factor, rate, decay):
    clipped = grad * factor
    moment_new = beta_first * moment + (1.0 - beta_first) * clipped
    square_new = beta_second * square + (1.0 - beta_second) * clipped * clipped
    corrected = moment_new / (1.0 - beta_first**ADAM_STEP)
    scaled = square_new / (1.0 - beta_second**ADAM_STEP)
    master_new = master - rate * (corrected / (jnp.sqrt(scaled) + adam_eps) + decay * master)
    return (moment_new, square_new, master_new)


def cores(value):
    size = lax.axis_size("tensor")
    return lax.ppermute(value, "tensor", [(i, i ^ 1) for i in range(size)])


def planes(value):
    size = lax.axis_size("tensor")
    return lax.ppermute(value, "tensor", [(i, i ^ 2) for i in range(size)])


def ring_order(size):
    return list(range(0, size, 2)) + list(range(size - 1, 0, -2))


def owners_here():
    size = lax.axis_size("dp")
    place = lax.axis_index("dp")
    seat = jnp.where(place % 2 == 0, place // 2, size - 1 - place // 2)
    sign = 1 - 2 * (lax.axis_index("tensor") % 2)
    spots = (seat + sign * jnp.arange(size, dtype=jnp.int32) + size) % size
    return jnp.where(spots < size // 2, 2 * spots, 2 * size - 1 - 2 * spots)


def after(value, *earlier):
    if not earlier:
        return value
    return lax.optimization_barrier((value, *earlier))[0]


def turn(value):
    size, inner = lax.axis_size("dp"), lax.axis_size("tensor")
    ring = ring_order(size)
    pairs = []
    for i in range(size):
        for t in range(inner):
            step = 1 if t % 2 == 0 else -1
            pairs.append((ring[i] * inner + t, ring[(i + step) % size] * inner + t))
    return lax.ppermute(value, ("dp", "tensor"), pairs)


def pair(value):
    return jnp.stack([value, cores(value)])


class Gather:
    def __init__(self, shard, load=None):
        self.size = lax.axis_size("dp")
        self.step = 0
        self.load = pair(shard) if load is None else load
        self.blocks = [(shard, (), 0)]
        self.loads = []

    def advance(self, *gates):
        self.step += 1
        if self.step == self.size // 2:
            self.load = turn(after(self.load[0], *gates))
            self.blocks.append((self.load, (), self.step))
        else:
            self.load = turn(after(self.load, *gates))
            self.take(self.load)
        self.loads.append(self.load)
        return self.load

    def take(self, load):
        self.blocks += [(load, (0,), self.size - self.step), (cores(load), (1,), self.step)]


def piece_order(size):
    far = size // 2
    order = [far] if far else []
    for step in range(far - 1, 0, -1):
        order += [step, size - step]
    return [*order, 0]


class Pieces:
    def __init__(self, pieces):
        self.pieces = pieces
        self.step = 0
        self.payload = pieces[0][0]

    def advance(self, *gates):
        self.step += 1
        load = after(turn(self.payload), *gates)
        piece = self.pieces[self.step]
        if piece.shape[0] == 1:
            return piece[0].astype(wide) + load[0].astype(wide) + cores(load)[1].astype(wide)
        theirs = cores(piece)[1]
        if self.step == 1:
            mine = (load.astype(wide) + piece[0].astype(wide)).astype(low)
            self.payload = jnp.stack([mine, theirs])
        else:
            both = jnp.stack([piece[0], theirs]).astype(wide)
            self.payload = (load.astype(wide) + both).astype(low)
        return self.payload


class Forward:
    def __init__(self, shard):
        self.size = lax.axis_size("dp")
        self.loads = [planes(shard)]
        self.blocks = [(self.loads[0], (), 0)]
        self.step = 0

    def take(self, load):
        self.step += 1
        load = planes(load)
        self.loads.append(load)
        if self.step == self.size // 2:
            self.blocks.append((load, (), self.step))
        else:
            self.blocks += [(load, (0,), self.size - self.step), (cores(load), (1,), self.step)]


def deal(owners, held, outs, distances):
    distances = list(distances)
    for out in outs:
        for i in range(out.shape[0]):
            count = out.shape[1]
            start = owners[distances.pop(0)] * count
            if count % 16 == 0:
                start = pl.multiple_of(start, 16)
            out[i] = held[pl.ds(start, count)]


def nn(left, right):
    return lax.dot_general(left, right, (((1,), (0,)), ((), ())), preferred_element_type=wide)


def nt(left, right):
    return lax.dot_general(left, right, (((1,), (1,)), ((), ())), preferred_element_type=wide)


def tn(left, right):
    return lax.dot_general(left, right, (((0,), (0,)), ((), ())), preferred_element_type=wide)


def fetch(picks, owners, blocks, first, target, sems, base):
    copies = []
    split = target.shape[1] // 2
    for i, (index, distance) in enumerate(picks):
        block = blocks[i]
        tall = block.shape[-2]
        start = owners[distance] * tall
        if tall % 16 == 0:
            start = pl.multiple_of(start, 16)
        for at in (0, split):
            source = block.at[(*index, slice(None), slice(first + at, first + at + split))]
            goal = target.at[pl.ds(start, tall), at : at + split]
            copies.append(
                pltpu.make_async_copy(source, goal, sems.at[base + 2 * i + at // split])
            )
    for copy in copies:
        copy.start()
    return copies


def keep(weights, target, half, sems, first):
    split = weights.shape[2] // 2
    copies = []
    for i in range(2):
        part = (half, slice(None), slice(i * split, (i + 1) * split))
        sem = sems.at[first + 2 * half + i]
        copies.append(pltpu.make_async_copy(weights.at[part], target.at[part], sem))
    for copy in copies:
        copy.start()
    return copies


def settle(copies):
    for copy in copies:
        copy.wait()


def whole_mean(value):
    return jnp.mean(value, axis=-1, keepdims=True)


def scores(queries, keys, same):
    return jnp.where(same, nt(queries, keys) * HD ** (-0.5), -1e30)


def attend_kernel(picks, owners, inputs, column, line, *refs):
    many = len(picks[0])
    packed, attended, logs, mixed, kept, weights, sems = refs[2 * many :]
    copies = [
        fetch(picks[p], owners, refs[p * many : p * many + many], 0, weights.at[p], sems, 2 * many * p)
        for p in range(2)
    ]
    leaving = []
    tall = weights.shape[2] // 4
    same = column[...] == line[...]
    values = inputs[...]
    logs[...] = jnp.zeros_like(logs)
    total = None
    for half in range(2):
        settle(copies[half])
        leaving += keep(weights, kept, half, sems, 4 * many)
        packed[half] = nn(values, weights[half]).astype(low)
        for head in range(tall // HD):
            at = head * HD
            raw = scores(
                packed[half, :, at : at + HD], packed[half, :, tall + at : tall + at + HD], same
            )
            peak = jnp.max(raw, axis=-1, keepdims=True)
            grown = jnp.exp(raw - peak)
            mass = jnp.sum(grown, axis=-1, keepdims=True)
            index = half * (tall // HD) + head
            logs[:, index : index + 1] = peak + jnp.log(mass)
            probs = (grown * (1.0 / mass)).astype(low)
            result = nn(probs, packed[half, :, 2 * tall + at : 2 * tall + at + HD])
            attended[half, :, at : at + HD] = result.astype(low)
        term = nt(attended[half], weights[half, :, 3 * tall :])
        total = term if total is None else total + term
    mixed[...] = total
    settle(leaving)


def feed_kernel(picks, owners, inputs, mixed, mixed_other, vectors, *refs):
    many = len(picks[0])
    own, expand_other, shrink_other = (refs[i * many : i * many + many] for i in range(3))
    first_unit, first_scale, active, slope, shrunk, expand_kept, shrink_kept, expand_w, shrink_w, sems = refs[
        3 * many :
    ]
    hidden = expand_w.shape[2]
    copies = [
        fetch(picks[0], owners, own, 0, expand_w.at[0], sems.at[0], 0),
        fetch(picks[1], owners, expand_other, 0, expand_w.at[1], sems.at[0], 2 * many),
    ]
    more = [
        fetch(picks[0], owners, own, hidden, shrink_w.at[0], sems.at[1], 0),
        fetch(picks[2], owners, shrink_other, 2 * hidden, shrink_w.at[1], sems.at[1], 2 * many),
    ]
    leaving = []
    value = inputs[...].astype(wide) + (mixed[...] + mixed_other[...]) + vectors[0:1]
    centered = value - whole_mean(value)
    scale = lax.rsqrt(whole_mean(centered * centered) + norm_eps)
    unit = centered * scale
    first_unit[...] = unit
    first_scale[...] = jnp.broadcast_to(scale, first_scale.shape)
    rounded = (unit * vectors[2:3] + vectors[3:4]).astype(low)
    total = None
    for half in range(2):
        settle(copies[half])
        leaving += keep(expand_w, expand_kept, half, sems.at[0], 4 * many)
        value = nn(rounded, expand_w[half])
        spread = 0.5 * (1.0 + lax.erf(value * math.sqrt(0.5)))
        result = (value * spread).astype(low)
        active[half] = result
        bell = jnp.exp(-0.5 * value * value) * (1.0 / math.sqrt(2.0 * math.pi))
        slope[half] = spread + value * bell
        settle(more[half])
        leaving += keep(shrink_w, shrink_kept, half, sems.at[1], 4 * many)
        term = nt(result, shrink_w[half])
        total = term if total is None else total + term
    shrunk[...] = total
    settle(leaving)


def sum_rows(value):
    return jnp.sum(value, axis=0, keepdims=True)


def norm_back(unit, scale, gain, grad):
    scaled = grad * gain
    back = scaled - whole_mean(scaled) - unit * whole_mean(scaled * unit)
    return back * scale


def second_kernel(
    first_unit, shrunk, shrunk_other, vectors, cotangent, output, grad, grad_low, sums
):
    normed = first_unit[...] * vectors[2:3] + vectors[3:4]
    value = normed + (shrunk[...] + shrunk_other[...]) + vectors[1:2]
    centered = value - whole_mean(value)
    scale = lax.rsqrt(whole_mean(centered * centered) + norm_eps)
    unit = centered * scale
    output[...] = (unit * vectors[4:5] + vectors[5:6]).astype(low)
    incoming = cotangent[...].astype(wide)
    back = norm_back(unit, scale, vectors[4:5], incoming)
    grad[...] = back
    grad_low[...] = back.astype(low)
    sums[...] = jnp.zeros_like(sums)
    sums[1:2] = sum_rows(back)
    sums[4:5] = sum_rows(incoming * unit)
    sums[5:6] = sum_rows(incoming)


def expand_kernel(grad_low, slope, expand_w, shrink_w, hidden_grad, partial):
    total = None
    for half in range(2):
        grad = nn(grad_low[...], shrink_w[half])
        rounded = (grad * slope[half]).astype(low)
        hidden_grad[half] = rounded
        term = nt(rounded, expand_w[half])
        total = term if total is None else total + term
    partial[...] = total


def weights_kernel(owners, grad_low, active, hidden_grad, first_unit, vectors, *refs):
    outs, held = refs[:-1], refs[-1]
    normed = (first_unit[...] * vectors[2:3] + vectors[3:4]).astype(low)
    hidden = active.shape[2]
    for half in range(2):
        at = half * hidden
        held[:, at : at + hidden] = tn(grad_low[...], active[half]).astype(low)
        at += 2 * hidden
        held[:, at : at + hidden] = tn(normed, hidden_grad[half]).astype(low)
    deal(owners, held, outs, piece_order(sum(out.shape[0] for out in outs)))


def first_kernel(
    grad, partial, partial_other, first_unit, first_scale, vectors, attended, second_sums, weights,
    first_grad, sums, mixer_grad, attended_grad
):
    tall = attended.shape[2]
    incoming = grad[...] + (partial[...] + partial_other[...])
    unit = first_unit[...]
    back = norm_back(unit, first_scale[:, 0:1], vectors[2:3], incoming)
    first_grad[...] = back
    sums[...] = second_sums[...]
    sums[0:1] = sum_rows(back)
    sums[2:3] = sum_rows(incoming * unit)
    sums[3:4] = sum_rows(incoming)
    rounded = back.astype(low)
    for half in range(2):
        attended_grad[half] = nn(rounded, weights[half, :, 3 * tall :]).astype(low)
        mixer_grad[half] = tn(rounded, attended[half]).astype(low)


def entry_kernel(half, owners, inputs, column, line, packed, logs, attended_grad, mixer_grad, sums, weights, *refs):
    outs, partial, held, packed_grad = refs[:-3], *refs[-3:]
    tall = attended_grad.shape[2]
    wide_count = 4 * tall
    same = column[...] == line[...]
    turned = logs[...].T
    scale = HD ** (-0.5)
    for head in range(tall // HD):
        at = head * HD
        queries = packed[half, :, at : at + HD]
        keys = packed[half, :, tall + at : tall + at + HD]
        values = packed[half, :, 2 * tall + at : 2 * tall + at + HD]
        outer = attended_grad[half, :, at : at + HD]
        index = half * (tall // HD) + head
        probs = jnp.exp(scores(keys, queries, same) - turned[index : index + 1])
        probs_grad = nt(values, outer)
        rows = jnp.sum(probs * probs_grad, axis=0, keepdims=True)
        score_grad = (probs * (probs_grad - rows)).astype(low)
        packed_grad[:, at : at + HD] = (tn(score_grad, keys) * scale).astype(low)
        packed_grad[:, tall + at : tall + at + HD] = (nn(score_grad, queries) * scale).astype(low)
        packed_grad[:, 2 * tall + at : 2 * tall + at + HD] = nn(probs.astype(low), outer).astype(low)
    held[:, : 3 * tall] = tn(inputs[...], packed_grad[...]).astype(low)
    held[:, 3 * tall : wide_count] = mixer_grad[half]
    extra = held.shape[1] - wide_count
    lines = jnp.concatenate([sums[...], jnp.zeros((extra - sums.shape[0], sums.shape[1]), wide)], axis=0)
    held[:, wide_count:] = lines.T.astype(low)
    deal(owners, held, outs, piece_order(sum(out.shape[0] for out in outs)))
    partial[...] = nt(packed_grad[...], weights[half, :, : 3 * tall])


def fold(value):
    rows, columns = value.shape
    total = jnp.zeros((8, 128), wide)
    for i in range(rows // 8):
        for j in range(columns // 128):
            tile = value[8 * i : 8 * i + 8, 128 * j : 128 * j + 128]
            total = total + tile * tile
    return total


def total_kernel(inner, pair, others, squares):
    count = pair.shape[1] - 128
    squares[...] = others[...] + fold(pair[:, :count]) + fold(pair[:, count:]) * (1.0 / inner)


def adam_kernel(*refs):
    attend, expand, shrink, squares = refs[:4]
    sources, norm, targets = refs[4:19], refs[19], refs[20:39]
    held, made, sems = refs[39:54], refs[54:73], refs[73]
    arriving = [
        pltpu.make_async_copy(s, h, sems.at[i]) for i, (s, h) in enumerate(zip(sources, held))
    ]
    for copy in arriving:
        copy.start()
    found = jnp.sqrt(jnp.sum(squares[...], keepdims=True))
    norm[...] = found
    factor = jnp.minimum(1.0, clip_bound / (found + 1e-06))
    tall = held[0].shape[2]
    start = 3 * tall // 128 * 128
    done = 4 * tall
    grads = [
        jnp.stack([attend[:, c * tall : (c + 1) * tall] for c in range(3)]),
        attend[:, start:done].T[3 * tall - start :],
        expand[...],
        shrink[...],
        attend[:, done:].T[: held[12].shape[0]],
    ]
    rates = [rate_matrix, rate_mixer, rate_matrix, rate_matrix, rate_vector]
    leaving = []
    for i, (grad, rate) in enumerate(zip(grads, rates)):
        settle(arriving[3 * i : 3 * i + 3])
        master, moment, square = (ref[...] for ref in held[3 * i : 3 * i + 3])
        decay = decay_matrix if i < 4 else 0.0
        new = adam_update(grad, moment, square, master, factor, rate, decay)
        new = (*new, new[2].astype(low)) if i < 4 else new
        for j, value in enumerate(new):
            k = 4 * i + j
            made[k][...] = value
            leaving.append(pltpu.make_async_copy(made[k], targets[k], sems.at[15 + k]))
            leaving[-1].start()
    settle(leaving)


def call(kernel, outs, *args, groups=None, owners=None, scratch=(), name=None):
    specs = [pl.BlockSpec(memory_space=pltpu.VMEM)] * len(args)
    if owners is not None and groups is None:
        args = (owners, *args)
        specs = [pl.BlockSpec(memory_space=pltpu.SMEM), *specs]
    if groups is not None:
        picks = [[(index, distance) for _, index, distance in group] for group in groups]
        blocks = [array for group in groups for array, _, _ in group]
        inner = kernel
        kernel = lambda *refs: inner(picks, *refs)
        args = (owners, *args, *blocks)
        specs = [pl.BlockSpec(memory_space=pltpu.SMEM), *specs]
        specs += [pl.BlockSpec(memory_space=pl.ANY)] * len(blocks)
    return pl.pallas_call(
        kernel,
        out_shape=tuple(jax.ShapeDtypeStruct(out[0], out[1]) for out in outs),
        in_specs=specs,
        out_specs=tuple(
            pl.BlockSpec(memory_space=pl.ANY if len(out) > 2 else pltpu.VMEM) for out in outs
        ),
        scratch_shapes=scratch,
        compiler_params=pltpu.CompilerParams(vmem_limit_bytes=VMEM_LIMIT),
        name=name,
    )(*args)


def shards(
    block_input,
    segment_lengths,
    entry_master,
    mixer_master,
    expand_master,
    shrink_master,
    block_vectors,
    block_cotangent,
    entry_moment,
    entry_square,
    mixer_moment,
    mixer_square,
    expand_moment,
    expand_square,
    shrink_moment,
    shrink_square,
    vector_moment,
    vector_square,
):
    rows, length, width = block_input.shape
    members = lax.axis_size("dp")
    place = lax.axis_index("dp")
    spot = lax.axis_index("tensor")
    core = spot % 2
    plane = spot // 2
    share = width // members
    tall = entry_master.shape[2]
    heads = 2 * tall // HD
    hidden = expand_master.shape[1]
    ringed = members <= RING_LIMIT

    attend_shard = jnp.concatenate(
        [entry_master[0], entry_master[1], entry_master[2], mixer_master.T], axis=1
    ).astype(low)
    feed_shard = jnp.concatenate([expand_master, shrink_master.T], axis=1).astype(low)
    def one_row(value):
        return lax.dynamic_index_in_dim(value, plane, 0, False)

    inputs = one_row(block_input)
    cotangent = one_row(block_cotangent)
    ends = jnp.cumsum(one_row(segment_lengths))
    positions = jnp.arange(length, dtype=jnp.int32)
    segment = jnp.sum((positions[:, None] >= ends[None, :]).astype(jnp.int32), axis=-1)
    column, line = segment[:, None], segment[None, :]
    grid = (length, width)

    def weights_of(many, count, columns):
        held = (pltpu.VMEM((2, width, columns), low),) * count
        shape = 4 * many + 4
        return *held, pltpu.SemaphoreType.DMA((count, shape) if count > 1 else (shape,))

    def attend(*groups, wait=None):
        column_here = column if wait is None else after(column, wait)
        return call(
            attend_kernel,
            [
                ((2, length, 4 * tall), low),
                ((2, length, tall), low),
                ((length, 128), wide),
                (grid, wide),
                ((2, width, 4 * tall), low, "far"),
            ],
            inputs, column_here, line, groups=groups, owners=owners,
            scratch=weights_of(len(groups[0]), 1, 4 * tall), name="attend",
        )

    far = members // 2
    if ringed:
        owners = owners_here()
        attend_gather, attend_other = Gather(attend_shard), Forward(attend_shard)
        shrink_far = planes(feed_shard[:, hidden:])
        for step in range(far):
            load = attend_gather.advance(*attend_other.loads[step - 2 : max(step - 1, 0)])
            attend_other.take(load)
        packed, attended, logs, mixed, attend_w = attend(attend_gather.blocks, attend_other.blocks)
        feed_gather = Gather(jnp.concatenate([feed_shard, shrink_far], axis=1))
        expand_other = Forward(feed_shard[:, :hidden])
        for step in range(far):
            gates = {0: (load, attend_other.loads[far - 2]), 1: (mixed,)}.get(step)
            load = feed_gather.advance(*(gates or expand_other.loads[step - 2 : step - 1]))
            expand_other.take(load[..., :hidden])
        feed_groups = (feed_gather.blocks, expand_other.blocks, feed_gather.blocks)
    else:
        owners = jnp.zeros((1,), jnp.int32)

        def gather(block):
            whole = lax.all_gather(block, "dp", axis=0, tiled=True)
            return [(whole, (), 0)], [(planes(whole), (), 0)]

        packed, attended, logs, mixed, attend_w = attend(*gather(attend_shard))
        whole = lax.all_gather(feed_shard, "dp", axis=0, tiled=True)
        other = planes(whole)
        whole = jnp.concatenate([whole, other[:, hidden:]], axis=1)
        feed_groups = ([(whole, (), 0)], [(other, (), 0)], [(whole, (), 0)])
    many = len(feed_groups[0])

    mixed_other = cores(mixed)
    first_unit, first_scale, active, slope, shrunk, expand_w, shrink_w = call(
        feed_kernel,
        [
            (grid, wide),
            ((length, 128), wide),
            ((2, length, hidden), low),
            ((2, length, hidden), wide),
            (grid, wide),
            ((2, width, hidden), low, "far"),
            ((2, width, hidden), low, "far"),
        ],
        inputs, mixed, mixed_other, block_vectors,
        groups=feed_groups, owners=owners, scratch=weights_of(many, 2, hidden), name="feed",
    )
    shrunk_other = cores(shrunk)
    output, second_grad, second_low, second_sums = call(
        second_kernel,
        [(grid, low), (grid, wide), (grid, low), ((8, width), wide)],
        first_unit, shrunk, shrunk_other, block_vectors, cotangent,
        name="second",
    )

    def pieces_of(columns):
        counts = [1, *[2] * (far - 1), 1] if ringed else [1]
        return [((count, share if ringed else width, columns), low) for count in counts]

    def other_row(value):
        middle = length // 2
        half = lax.dynamic_slice_in_dim(value, core * middle, middle, 0)
        first = planes(half)
        second = cores(first)
        top = jnp.where(core == 0, first, second)
        bottom = jnp.where(core == 0, second, first)
        return jnp.concatenate([top, bottom], axis=0)

    def both_rows(own, other):
        return jnp.stack([jnp.where(plane == 0, own, other), jnp.where(plane == 0, other, own)])

    def swap(value):
        return planes(value.astype(low)).astype(wide)

    hidden_grad, partial = call(
        expand_kernel,
        [((2, length, hidden), low), (grid, wide)],
        second_low, slope, expand_w, shrink_w,
        name="expand",
    )
    partial_other = cores(partial)
    feed_pieces = Pieces(
        call(
            weights_kernel,
            pieces_of(4 * hidden),
            second_low, active, after(hidden_grad, partial), first_unit, block_vectors,
            owners=owners, scratch=(pltpu.VMEM((width, 4 * hidden), low),), name="weights",
        )
    )
    block_output = both_rows(output, other_row(output))
    partial_other = after(partial_other, feed_pieces.payload, block_output)
    first_grad, sums, mixer_grad, attended_grad = call(
        first_kernel,
        [(grid, wide), ((8, width), wide), ((2, width, tall), low), ((2, length, tall), low)],
        second_grad, partial, partial_other, first_unit, first_scale, block_vectors, attended, second_sums,
        attend_w, name="first",
    )

    def entry(half, *gates):
        columns = 4 * tall + 128
        *pieces, input_term = call(
            lambda *refs: entry_kernel(half, *refs),
            [*pieces_of(columns), (grid, wide)],
            inputs, column, line, packed, logs, after(attended_grad, *gates), mixer_grad, sums, attend_w,
            owners=owners, name="entry",
            scratch=(pltpu.VMEM((width, columns), low), pltpu.VMEM((length, 3 * tall), low)),
        )
        return pieces, input_term

    def scattered(value):
        return lax.psum_scatter(value[0].astype(wide), "dp", scatter_dimension=0, tiled=True)

    if ringed:
        feed_pieces.advance(attended_grad)
    far_pieces, input_term = entry(1, feed_pieces.payload)
    crossed = [planes(piece) for piece in far_pieces]
    own_pieces, more_term = entry(0, input_term)
    pieces = [
        (own.astype(wide) + other.astype(wide)).astype(low) for own, other in zip(own_pieces, crossed)
    ]
    attend_pieces = Pieces(pieces)
    if ringed:
        feed_pieces.advance(more_term, attend_pieces.payload, *crossed[1:2])
        attend_pieces.advance(feed_pieces.payload)
        feed_pieces.advance(attend_pieces.payload, *crossed[2:3])
        attend_pieces.advance(feed_pieces.payload)
        feed_pair = feed_pieces.advance()
    else:
        feed_pair = scattered(feed_pieces.payload[None])
    input_term = (input_term + more_term).astype(low)
    input_gradient = first_grad + (input_term.astype(wide) + cores(input_term).astype(wide))
    parts = [feed_pair[:, i * hidden : (i + 1) * hidden] for i in range(4)]
    feed_other = swap(jnp.concatenate([parts[1], parts[3]], axis=1))
    shrink_share = parts[0] + feed_other[:, :hidden]
    expand_share = parts[2] + feed_other[:, hidden:]
    other_squares = jnp.sum(shrink_share * shrink_share) + jnp.sum(expand_share * expand_share)
    if ringed:
        attend_pieces.advance(feed_pair)
        attend_pair = attend_pieces.advance(other_squares)
    else:
        attend_pair = scattered(pieces[0])
    input_other = other_row(input_gradient.astype(low)).astype(wide)
    input_gradient = both_rows(input_gradient, input_other)
    inner = lax.axis_size("tensor")

    def reduced(squares):
        squares = squares + cores(squares)
        squares = squares + planes(squares)
        hop = 1
        while hop < members:
            squares = squares + lax.ppermute(squares, "dp", [(i, i ^ hop) for i in range(members)])
            hop *= 2
        return squares

    vector_width = width // members
    vector_master = lax.dynamic_slice_in_dim(block_vectors, place * vector_width, vector_width, 1)
    if ringed:
        others = jnp.where(lax.broadcasted_iota(jnp.int32, (8, 128), 1) == 0, other_squares / 8, 0.0)
        (squares,) = call(
            lambda *refs: total_kernel(inner, *refs),
            [((8, 128), wide)],
            attend_pair, others, name="total",
        )
        groups = [
            (entry_master, entry_moment, entry_square),
            (mixer_master, mixer_moment, mixer_square),
            (expand_master, expand_moment, expand_square),
            (shrink_master.T, shrink_moment.T, shrink_square.T),
            (vector_master, vector_moment, vector_square),
        ]
        sources = [array for group in groups for array in group]
        targets = []
        for i, group in enumerate(groups):
            targets += [(group[0].shape, wide)] * 3 + [(group[0].shape, low)] * (i < 4)
        in_place = pl.BlockSpec(memory_space=pltpu.HBM)
        held = pl.BlockSpec(memory_space=pltpu.VMEM)
        norm, *news = pl.pallas_call(
            adam_kernel,
            out_shape=[
                jax.ShapeDtypeStruct(shape, kind) for shape, kind in [((1, 1), wide), *targets]
            ],
            in_specs=[held] * 4 + [in_place] * 15,
            out_specs=[held] + [in_place] * 19,
            scratch_shapes=[
                *[pltpu.VMEM(array.shape, wide) for array in sources],
                *[pltpu.VMEM(shape, kind) for shape, kind in targets],
                pltpu.SemaphoreType.DMA((34,)),
            ],
            compiler_params=pltpu.CompilerParams(vmem_limit_bytes=VMEM_LIMIT),
            name="adam",
        )(attend_pair, expand_share, shrink_share, reduced(squares), *sources)
        news[12:16] = [array.T for array in news[12:16]]
        return (block_output, input_gradient, norm[0, 0], *news)

    attend_share = attend_pair[:, : 4 * tall]
    vector_sum = attend_pair[:, 4 * tall :]
    entry_share = jnp.stack([attend_share[:, c * tall : (c + 1) * tall] for c in range(3)])
    mixer_share = attend_share[:, 3 * tall :].T
    vector_share = vector_sum[:, :6].T
    squares = other_squares + jnp.sum(attend_share * attend_share)
    squares = squares + jnp.sum(vector_share * vector_share) / inner
    gradient_norm = jnp.sqrt(reduced(jnp.full((8, 128), squares))[0, 0])
    factor = jnp.minimum(1.0, clip_bound / (gradient_norm + 1e-06))
    results = []
    for grad, moment, square, master, rate in (
        (entry_share, entry_moment, entry_square, entry_master, rate_matrix),
        (mixer_share, mixer_moment, mixer_square, mixer_master, rate_mixer),
        (expand_share, expand_moment, expand_square, expand_master, rate_matrix),
        (shrink_share.T, shrink_moment, shrink_square, shrink_master, rate_matrix),
    ):
        new = adam_update(grad, moment, square, master, factor, rate, decay_matrix)
        results += [*new, new[2].astype(low)]
    results += adam_update(
        vector_share, vector_moment, vector_square, vector_master, factor, rate_vector, 0.0
    )
    return (block_output, input_gradient, gradient_norm, *results)


def solution(mesh):
    in_specs = (
        P("dp", None, None),
        P("dp", None),
        P(None, "dp", "tensor"),
        P("tensor", "dp"),
        P("dp", "tensor"),
        P("tensor", "dp"),
        P(),
        P("dp", None, None),
        P(None, "dp", "tensor"),
        P(None, "dp", "tensor"),
        P("tensor", "dp"),
        P("tensor", "dp"),
        P("dp", "tensor"),
        P("dp", "tensor"),
        P("tensor", "dp"),
        P("tensor", "dp"),
        P(None, "dp"),
        P(None, "dp"),
    )
    out_specs = (
        P("dp", None, None),
        P("dp", None, None),
        P(),
        P(None, "dp", "tensor"),
        P(None, "dp", "tensor"),
        P(None, "dp", "tensor"),
        P(None, "dp", "tensor"),
        P("tensor", "dp"),
        P("tensor", "dp"),
        P("tensor", "dp"),
        P("tensor", "dp"),
        P("dp", "tensor"),
        P("dp", "tensor"),
        P("dp", "tensor"),
        P("dp", "tensor"),
        P("tensor", "dp"),
        P("tensor", "dp"),
        P("tensor", "dp"),
        P("tensor", "dp"),
        P(None, "dp"),
        P(None, "dp"),
        P(None, "dp"),
    )
    return jax.shard_map(shards, mesh=mesh, in_specs=in_specs, out_specs=out_specs, check_vma=False)
```

```python
import math

import jax
import jax.numpy as jnp
from jax import lax
from jax.experimental import pallas as pl
from jax.experimental.pallas import tpu as pltpu
from jax.sharding import PartitionSpec as P

HD = 64
ADAM_STEP = 3


norm_eps = 1e-12
clip_bound = 1.0
beta_first = 0.5
beta_second = 0.6
adam_eps = 1e-08
rate_matrix = 0.02
rate_mixer = 0.08
rate_vector = 0.25
decay_matrix = 0.01


low = jnp.bfloat16
wide = jnp.float32
RING_LIMIT = 16
VMEM_LIMIT = 48 * 2**20


def adam_update(grad, moment, square, master, factor, rate, decay):
    clipped = grad * factor
    moment_new = beta_first * moment + (1.0 - beta_first) * clipped
    square_new = beta_second * square + (1.0 - beta_second) * clipped * clipped
    corrected = moment_new / (1.0 - beta_first**ADAM_STEP)
    scaled = square_new / (1.0 - beta_second**ADAM_STEP)
    master_new = master - rate * (corrected / (jnp.sqrt(scaled) + adam_eps) + decay * master)
    return (moment_new, square_new, master_new)


def cores(value):
    size = lax.axis_size("tensor")
    return lax.ppermute(value, "tensor", [(i, i ^ 1) for i in range(size)])


def planes(value):
    size = lax.axis_size("tensor")
    return lax.ppermute(value, "tensor", [(i, i ^ 2) for i in range(size)])


def ring_order(size):
    return list(range(0, size, 2)) + list(range(size - 1, 0, -2))


def owners_here():
    size = lax.axis_size("dp")
    place = lax.axis_index("dp")
    seat = jnp.where(place % 2 == 0, place // 2, size - 1 - place // 2)
    sign = 1 - 2 * (lax.axis_index("tensor") % 2)
    spots = (seat + sign * jnp.arange(size, dtype=jnp.int32) + size) % size
    return jnp.where(spots < size // 2, 2 * spots, 2 * size - 1 - 2 * spots)


def after(value, *earlier):
    if not earlier:
        return value
    return lax.optimization_barrier((value, *earlier))[0]


def turn(value):
    size, inner = lax.axis_size("dp"), lax.axis_size("tensor")
    ring = ring_order(size)
    pairs = []
    for i in range(size):
        for t in range(inner):
            step = 1 if t % 2 == 0 else -1
            pairs.append((ring[i] * inner + t, ring[(i + step) % size] * inner + t))
    return lax.ppermute(value, ("dp", "tensor"), pairs)


def pair(value):
    return jnp.stack([value, cores(value)])


class Gather:
    def __init__(self, shard, load=None):
        self.size = lax.axis_size("dp")
        self.step = 0
        self.load = pair(shard) if load is None else load
        self.blocks = [(shard, (), 0)]
        self.loads = []

    def advance(self, *gates):
        self.step += 1
        if self.step == self.size // 2:
            self.load = turn(after(self.load[0], *gates))
            self.blocks.append((self.load, (), self.step))
        else:
            self.load = turn(after(self.load, *gates))
            self.take(self.load)
        self.loads.append(self.load)
        return self.load

    def take(self, load):
        self.blocks += [(load, (0,), self.size - self.step), (cores(load), (1,), self.step)]


def piece_order(size):
    far = size // 2
    order = [far] if far else []
    for step in range(far - 1, 0, -1):
        order += [step, size - step]
    return [*order, 0]


class Pieces:
    def __init__(self, pieces):
        self.pieces = pieces
        self.step = 0
        self.payload = pieces[0][0]

    def advance(self, *gates):
        self.step += 1
        load = after(turn(self.payload), *gates)
        piece = self.pieces[self.step]
        if not isinstance(piece, tuple):
            return piece[0].astype(wide) + load[0].astype(wide) + cores(load)[1].astype(wide)
        theirs = cores(piece[1])
        if self.step == 1:
            mine = (load.astype(wide) + piece[0][0].astype(wide)).astype(low)
            self.payload = jnp.concatenate([mine[None], theirs], axis=0)
        else:
            both = jnp.concatenate([piece[0], theirs], axis=0).astype(wide)
            self.payload = (load.astype(wide) + both).astype(low)
        return self.payload


class Forward:
    def __init__(self, shard):
        self.size = lax.axis_size("dp")
        self.loads = [planes(shard)]
        self.blocks = [(self.loads[0], (), 0)]
        self.step = 0

    def take(self, load):
        self.step += 1
        load = planes(load)
        self.loads.append(load)
        if self.step == self.size // 2:
            self.blocks.append((load, (), self.step))
        else:
            self.blocks += [(load, (0,), self.size - self.step), (cores(load), (1,), self.step)]


def deal(owners, held, outs, distances):
    distances = list(distances)
    for out in outs:
        for i in range(out.shape[0]):
            count = out.shape[1]
            start = owners[distances.pop(0)] * count
            if count % 16 == 0:
                start = pl.multiple_of(start, 16)
            out[i] = held[pl.ds(start, count)]


def nn(left, right):
    return lax.dot_general(left, right, (((1,), (0,)), ((), ())), preferred_element_type=wide)


def nt(left, right):
    return lax.dot_general(left, right, (((1,), (1,)), ((), ())), preferred_element_type=wide)


def tn(left, right):
    return lax.dot_general(left, right, (((0,), (0,)), ((), ())), preferred_element_type=wide)


def fetch(picks, owners, blocks, first, target, sems, base):
    copies = []
    split = target.shape[1] // 2
    for i, (index, distance) in enumerate(picks):
        block = blocks[i]
        tall = block.shape[-2]
        start = owners[distance] * tall
        if tall % 16 == 0:
            start = pl.multiple_of(start, 16)
        for at in (0, split):
            source = block.at[(*index, slice(None), slice(first + at, first + at + split))]
            goal = target.at[pl.ds(start, tall), at : at + split]
            copies.append(
                pltpu.make_async_copy(source, goal, sems.at[base + 2 * i + at // split])
            )
    for copy in copies:
        copy.start()
    return copies


def keep(weights, target, sems, first):
    split = weights.shape[1] // 2
    copies = []
    for i in range(2):
        part = (slice(None), slice(i * split, (i + 1) * split))
        copies.append(pltpu.make_async_copy(weights.at[part], target.at[part], sems.at[first + i]))
    for copy in copies:
        copy.start()
    return copies


def settle(copies):
    for copy in copies:
        copy.wait()


def whole_mean(value):
    return jnp.mean(value, axis=-1, keepdims=True)


def scores(queries, keys, same):
    return jnp.where(same, nt(queries, keys) * HD ** (-0.5), -1e30)


def half_of(owners, size, other=False):
    which = owners[owners.shape[0] - 2]
    which = 1 - which if other else which
    return pl.ds(pl.multiple_of(which * (size // 2), 16), size // 2)


def row_of(owners, index):
    return jnp.abs(owners[owners.shape[0] - 1] - index)


def attend_kernel(picks, owners, inputs, column, line, *refs):
    many = len(picks[0])
    packed, attended, attended_other, logs, mixer_w, kept, weights, sems = refs[many:]
    copies = fetch(picks[0], owners, refs[:many], 0, weights, sems, 0)
    tall = mixer_w.shape[0]
    logs[...] = jnp.zeros_like(logs)
    settle(copies)
    leaving = keep(weights, kept, sems, 2 * many)
    mixer_w[...] = weights[:, :tall].T
    for index, goal in ((1, attended_other), (0, attended)):
        row = row_of(owners, index)
        same = column[row] == line[row]
        packed[index] = nn(inputs[row], weights[...]).astype(low)
        for head in range(tall // HD):
            at = tall + head * HD
            raw = scores(
                packed[index, :, at : at + HD], packed[index, :, tall + at : tall + at + HD], same
            )
            peak = jnp.max(raw, axis=-1, keepdims=True)
            grown = jnp.exp(raw - peak)
            mass = jnp.sum(grown, axis=-1, keepdims=True)
            logs[index, :, head : head + 1] = peak + jnp.log(mass)
            probs = (grown * (1.0 / mass)).astype(low)
            result = nn(probs, packed[index, :, 2 * tall + at : 2 * tall + at + HD])
            if index:
                goal[head * HD : head * HD + HD] = result.T.astype(low)
            else:
                goal[:, head * HD : head * HD + HD] = result.astype(low)
    settle(leaving)


def mix_kernel(attended, attended_far, mixer_w, mixer_far, mixed):
    mixed[...] = nn(attended[...], mixer_w[...]) + tn(attended_far[...], mixer_far[...])


def feed_kernel(picks, owners, inputs, mixed, mixed_other, vectors, *refs):
    many = len(picks[0])
    first_unit, first_scale, active, slope, shrunk, expand_kept, shrink_kept, expand_w, shrink_w, sems = refs[many:]
    hidden = expand_w.shape[2]
    copies = [
        fetch(picks[0], owners, refs[:many], p * hidden, (expand_w, shrink_w)[p % 2].at[p // 2], sems, 2 * many * p)
        for p in range(4)
    ]
    leaving = []
    value = inputs[...].astype(wide) + (mixed[...] + mixed_other[...]) + vectors[0:1]
    centered = value - whole_mean(value)
    scale = lax.rsqrt(whole_mean(centered * centered) + norm_eps)
    unit = centered * scale
    first_unit[...] = unit
    first_scale[...] = jnp.broadcast_to(scale, first_scale.shape)
    rounded = (unit * vectors[2:3] + vectors[3:4]).astype(low)
    total = None
    for half in range(2):
        settle(copies[2 * half])
        leaving += keep(expand_w.at[half], expand_kept.at[half], sems, 8 * many + 4 * half)
        value = nn(rounded, expand_w[half])
        spread = 0.5 * (1.0 + lax.erf(value * math.sqrt(0.5)))
        result = (value * spread).astype(low)
        active[half] = result
        bell = jnp.exp(-0.5 * value * value) * (1.0 / math.sqrt(2.0 * math.pi))
        slope[half] = (spread + value * bell).astype(slope.dtype)
        settle(copies[2 * half + 1])
        leaving += keep(shrink_w.at[half], shrink_kept.at[half], sems, 8 * many + 4 * half + 2)
        term = nt(result, shrink_w[half])
        total = term if total is None else total + term
    shrunk[...] = total.astype(shrunk.dtype)
    settle(leaving)


def sum_rows(value):
    return jnp.sum(value, axis=0, keepdims=True)


def norm_back(unit, scale, gain, grad):
    scaled = grad * gain
    back = scaled - whole_mean(scaled) - unit * whole_mean(scaled * unit)
    return back * scale


def second_kernel(
    owners, first_unit, shrunk, shrunk_other, vectors, cotangent, output, output_half, grad, grad_low, sums
):
    normed = first_unit[...] * vectors[2:3] + vectors[3:4]
    value = normed + (shrunk[...].astype(wide) + shrunk_other[...].astype(wide)) + vectors[1:2]
    centered = value - whole_mean(value)
    scale = lax.rsqrt(whole_mean(centered * centered) + norm_eps)
    unit = centered * scale
    output[...] = (unit * vectors[4:5] + vectors[5:6]).astype(low)
    output_half[...] = output[half_of(owners, output.shape[0])]
    incoming = cotangent[...].astype(wide)
    back = norm_back(unit, scale, vectors[4:5], incoming)
    grad[...] = back
    grad_low[...] = back.astype(low)
    sums[...] = jnp.zeros_like(sums)
    sums[1:2] = sum_rows(back)
    sums[4:5] = sum_rows(incoming * unit)
    sums[5:6] = sum_rows(incoming)


def expand_kernel(grad_low, slope, expand_w, shrink_w, hidden_grad, partial):
    total = None
    for half in range(2):
        grad = nn(grad_low[...], shrink_w[half])
        rounded = (grad * slope[half].astype(wide)).astype(low)
        hidden_grad[half] = rounded
        term = nt(rounded, expand_w[half])
        total = term if total is None else total + term
    partial[...] = total


def weights_kernel(owners, grad_low, active, hidden_grad, first_unit, vectors, *refs):
    outs, held = refs[:-1], refs[-1]
    normed = (first_unit[...] * vectors[2:3] + vectors[3:4]).astype(low)
    hidden = active.shape[2]
    for half in range(2):
        at = half * hidden
        held[:, at : at + hidden] = tn(grad_low[...], active[half]).astype(low)
        at += 2 * hidden
        held[:, at : at + hidden] = tn(normed, hidden_grad[half]).astype(low)
    deal(owners, held, outs, piece_order(sum(out.shape[0] for out in outs)))


def first_kernel(
    owners, grad, partial, partial_other, first_unit, first_scale, vectors, attended, attended_far, second_sums,
    mixer_w, mixer_far, first_half, sums, mixer_grad, mixer_grad_far, attended_grad, attended_grad_far, held
):
    incoming = grad[...] + (partial[...] + partial_other[...])
    unit = first_unit[...]
    back = norm_back(unit, first_scale[:, 0:1], vectors[2:3], incoming)
    held[...] = back
    first_half[...] = held[half_of(owners, held.shape[0])]
    sums[...] = second_sums[...]
    sums[0:1] = sum_rows(back)
    sums[2:3] = sum_rows(incoming * unit)
    sums[3:4] = sum_rows(incoming)
    rounded = back.astype(low)
    attended_grad_far[...] = nt(mixer_far[...], rounded).astype(low)
    attended_grad[...] = nt(rounded, mixer_w[...]).astype(low)
    mixer_grad_far[...] = nn(attended_far[...], rounded).astype(low)
    mixer_grad[...] = tn(rounded, attended[...]).astype(low)


def entry_kernel(index, owners, column, line, packed, logs, outer, weights, packed_grad, kept, sent, partial):
    tall = weights.shape[1] // 4
    if outer.shape[0] == tall:
        outer = outer[...].T
    row = row_of(owners, index)
    same = column[row] == line[row]
    turned = logs[index].T
    scale = HD ** (-0.5)
    packed_grad[:, :tall] = jnp.zeros((outer.shape[0], tall), low)
    for head in range(tall // HD):
        at = tall + head * HD
        queries = packed[index, :, at : at + HD]
        keys = packed[index, :, tall + at : tall + at + HD]
        values = packed[index, :, 2 * tall + at : 2 * tall + at + HD]
        outward = outer[:, head * HD : head * HD + HD]
        probs = jnp.exp(scores(keys, queries, same) - turned[head : head + 1])
        probs_grad = nt(values, outward)
        rows = jnp.sum(probs * probs_grad, axis=0, keepdims=True)
        score_grad = (probs * (probs_grad - rows)).astype(low)
        packed_grad[:, at : at + HD] = (tn(score_grad, keys) * scale).astype(low)
        packed_grad[:, tall + at : tall + at + HD] = (nn(score_grad, queries) * scale).astype(low)
        packed_grad[:, 2 * tall + at : 2 * tall + at + HD] = nn(probs.astype(low), outward).astype(low)
    partial[...] = nt(packed_grad[...], weights[...])
    kept[...] = partial[half_of(owners, partial.shape[0])]
    sent[...] = partial[half_of(owners, partial.shape[0], True)].astype(low)


def gather_kernel(
    owners, column, line, packed, logs, outer, weights, inputs, packed_grad, mixer_grad, mixer_grad_far, sums,
    sums_far, *refs
):
    outs, kept, sent, held, other_grad, partial = refs[:-5], *refs[-5:]
    entry_kernel(1, owners, column, line, packed, logs, outer, weights, other_grad, kept, sent, partial)
    tall = weights.shape[1] // 4
    done = packed_grad.shape[1]
    own, other = row_of(owners, 0), row_of(owners, 1)
    held[:, :done] = (
        tn(inputs[own], packed_grad[...]) + tn(inputs[other], other_grad[...])
    ).astype(low)
    held[:, :tall] = (mixer_grad[...].astype(wide) + mixer_grad_far[...].T.astype(wide)).astype(low)
    extra = held.shape[1] - done
    total = sums[...] + sums_far[...]
    lines = jnp.concatenate([total, jnp.zeros((extra - total.shape[0], total.shape[1]), wide)], axis=0)
    held[:, done:] = lines.T.astype(low)
    deal(owners, held, outs, piece_order(sum(out.shape[0] for out in outs)))


def fold(value):
    rows, columns = value.shape
    total = jnp.zeros((8, 128), wide)
    for i in range(rows // 8):
        for j in range(columns // 128):
            tile = value[8 * i : 8 * i + 8, 128 * j : 128 * j + 128]
            total = total + tile * tile
    return total


def total_kernel(inner, pair, others, squares):
    count = pair.shape[1] - 128
    squares[...] = others[...] + fold(pair[:, :count]) + fold(pair[:, count:]) * (1.0 / inner)


def adam_kernel(*refs):
    owners, attend, expand, shrink, squares, half, rest = refs[:7]
    sources, norm, targets, placed = refs[7:22], refs[23], refs[24:43], refs[43]
    held, made, other, sems = refs[44:59], refs[59:78], refs[78], refs[79]
    arriving = [
        pltpu.make_async_copy(s, h, sems.at[i]) for i, (s, h) in enumerate(zip(sources, held))
    ]
    for copy in arriving:
        copy.start()
    count = half.shape[0]
    other[half_of(owners, 2 * count)] = half[...].astype(wide)
    other[half_of(owners, 2 * count, True)] = rest[...].astype(wide)
    leaving = [pltpu.make_async_copy(other, placed.at[row_of(owners, 1)], sems.at[34])]
    leaving[0].start()
    found = jnp.sqrt(jnp.sum(squares[...], keepdims=True))
    norm[...] = found
    factor = jnp.minimum(1.0, clip_bound / (found + 1e-06))
    tall = held[0].shape[2]
    done = 4 * tall
    rounded = (tall + 127) // 128 * 128
    grads = [
        jnp.stack([attend[:, c * tall : (c + 1) * tall] for c in range(1, 4)]),
        attend[:, :rounded].T[:tall],
        expand[...],
        shrink[...],
        attend[:, done:].T[: held[12].shape[0]],
    ]
    rates = [rate_matrix, rate_mixer, rate_matrix, rate_matrix, rate_vector]
    for i, (grad, rate) in enumerate(zip(grads, rates)):
        settle(arriving[3 * i : 3 * i + 3])
        master, moment, square = (ref[...] for ref in held[3 * i : 3 * i + 3])
        decay = decay_matrix if i < 4 else 0.0
        new = adam_update(grad, moment, square, master, factor, rate, decay)
        new = (*new, new[2].astype(low)) if i < 4 else new
        for j, value in enumerate(new):
            k = 4 * i + j
            made[k][...] = value
            leaving.append(pltpu.make_async_copy(made[k], targets[k], sems.at[15 + k]))
            leaving[-1].start()
    settle(leaving)


def place_kernel(owners, own, half, rest, result):
    row = row_of(owners, 1)
    result[row_of(owners, 0)] = own[...]
    result[row, half_of(owners, own.shape[0])] = half[...]
    result[row, half_of(owners, own.shape[0], True)] = rest[...]


def own_kernel(owners, half, rest, result, sems):
    row = row_of(owners, 0)
    copies = [
        pltpu.make_async_copy(
            ref, result.at[row, half_of(owners, 2 * ref.shape[0], i == 1)], sems.at[i]
        )
        for i, ref in enumerate((half, rest))
    ]
    for copy in copies:
        copy.start()
    settle(copies)


def in_hbm(array):
    return pltpu.with_memory_space_constraint(array, pltpu.HBM)


def call(kernel, outs, *args, groups=None, owners=None, scratch=(), name=None):
    specs = [pl.BlockSpec(memory_space=pltpu.VMEM)] * len(args)
    if owners is not None and groups is None:
        args = (owners, *args)
        specs = [pl.BlockSpec(memory_space=pltpu.SMEM), *specs]
    if groups is not None:
        picks = [[(index, distance) for _, index, distance in group] for group in groups]
        blocks = [in_hbm(array) for group in groups for array, _, _ in group]
        inner = kernel
        kernel = lambda *refs: inner(picks, *refs)
        args = (owners, *args, *blocks)
        specs = [pl.BlockSpec(memory_space=pltpu.SMEM), *specs]
        specs += [pl.BlockSpec(memory_space=pl.ANY)] * len(blocks)
    return pl.pallas_call(
        kernel,
        out_shape=tuple(jax.ShapeDtypeStruct(out[0], out[1]) for out in outs),
        in_specs=specs,
        out_specs=tuple(
            pl.BlockSpec(memory_space=pl.ANY if len(out) > 2 else pltpu.VMEM) for out in outs
        ),
        scratch_shapes=scratch,
        compiler_params=pltpu.CompilerParams(vmem_limit_bytes=VMEM_LIMIT),
        name=name,
    )(*args)


def shards(
    block_input,
    segment_lengths,
    entry_master,
    mixer_master,
    expand_master,
    shrink_master,
    block_vectors,
    block_cotangent,
    entry_moment,
    entry_square,
    mixer_moment,
    mixer_square,
    expand_moment,
    expand_square,
    shrink_moment,
    shrink_square,
    vector_moment,
    vector_square,
):
    rows, length, width = block_input.shape
    members = lax.axis_size("dp")
    place = lax.axis_index("dp")
    spot = lax.axis_index("tensor")
    core = spot % 2
    plane = spot // 2
    share = width // members
    tall = entry_master.shape[2]
    heads = 2 * tall // HD
    hidden = expand_master.shape[1]
    ringed = members <= RING_LIMIT

    attend_shard = jnp.concatenate(
        [mixer_master.T, entry_master[0], entry_master[1], entry_master[2]], axis=1
    ).astype(low)
    feed_shard = jnp.concatenate([expand_master, shrink_master.T], axis=1).astype(low)

    def one_row(value):
        return lax.dynamic_index_in_dim(value, plane, 0, False)

    inputs = one_row(block_input)
    cotangent = one_row(block_cotangent)
    ends = jnp.cumsum(segment_lengths, axis=1)
    positions = jnp.arange(length, dtype=jnp.int32)
    segment = jnp.sum((positions[None, :, None] >= ends[:, None, :]).astype(jnp.int32), axis=-1)
    column, line = segment[:, :, None], segment[:, None, :]
    grid = (length, width)

    def attend(blocks):
        count = len(blocks)
        return call(
            attend_kernel,
            [
                ((2, length, 4 * tall), low),
                ((length, tall), low),
                ((tall, length), low),
                ((2, length, 128), wide),
                ((tall, width), low),
                ((width, 4 * tall), low, "far"),
            ],
            block_input, column, line, groups=[blocks], owners=owners, name="attend",
            scratch=(
                pltpu.VMEM((width, 4 * tall), low), pltpu.SemaphoreType.DMA((2 * count + 2,))
            ),
        )

    def mix(attended, attended_other, mixer_w):
        attended_far, mixer_far = planes(attended_other), planes(mixer_w)
        (mixed,) = call(
            mix_kernel, [(grid, wide)], attended, attended_far, mixer_w, mixer_far, name="mix"
        )
        return attended_far, mixer_far, mixed

    far = members // 2
    if ringed:
        owners = jnp.concatenate([owners_here(), core[None], plane[None]])
        attend_gather = Gather(attend_shard)
        feed_far = planes(feed_shard)
        for step in range(far):
            attend_gather.advance()
        packed, attended, attended_other, logs, mixer_w, attend_w = attend(attend_gather.blocks)
        attended_far, mixer_far, mixed = mix(attended, attended_other, mixer_w)
        feed_gather = Gather(jnp.concatenate([feed_shard, feed_far], axis=1))
        for step in range(far):
            gates = {0: (attend_gather.load,), 1: (attended,), 2: (attended_far, mixer_far)}.get(step, ())
            feed_gather.advance(*gates)
        feed_blocks = feed_gather.blocks
    else:
        owners = jnp.stack([jnp.zeros((), jnp.int32), core, plane])
        whole = lax.all_gather(attend_shard, "dp", axis=0, tiled=True)
        packed, attended, attended_other, logs, mixer_w, attend_w = attend([(whole, (), 0)])
        attended_far, mixer_far, mixed = mix(attended, attended_other, mixer_w)
        whole = lax.all_gather(feed_shard, "dp", axis=0, tiled=True)
        feed_blocks = [(jnp.concatenate([whole, planes(whole)], axis=1), (), 0)]
    many = len(feed_blocks)

    mixed_other = cores(mixed)
    first_unit, first_scale, active, slope, shrunk, expand_w, shrink_w = call(
        feed_kernel,
        [
            (grid, wide),
            ((length, 128), wide),
            ((2, length, hidden), low),
            ((2, length, hidden), low),
            (grid, low),
            ((2, width, hidden), low, "far"),
            ((2, width, hidden), low, "far"),
        ],
        inputs, mixed, mixed_other, block_vectors,
        groups=[feed_blocks], owners=owners, name="feed",
        scratch=(
            pltpu.VMEM((2, width, hidden), low),
            pltpu.VMEM((2, width, hidden), low),
            pltpu.SemaphoreType.DMA((8 * many + 8,)),
        ),
    )
    shrunk_other = cores(shrunk)
    half = (length // 2, width)
    output, output_half, second_grad, second_low, second_sums = call(
        second_kernel,
        [(grid, low), (half, low), (grid, wide), (grid, low), ((8, width), wide)],
        first_unit, shrunk, shrunk_other, block_vectors, cotangent,
        owners=owners, name="second",
    )

    def pieces_of(columns, counts):
        return [((count, share if ringed else width, columns), low) for count in counts]

    singles = [1] * members if ringed else [1]

    def paired(pieces):
        middle = [tuple(pieces[i : i + 2]) for i in range(1, len(pieces) - 1, 2)]
        return [pieces[0], *middle, pieces[-1]]

    def swap(value):
        return planes(value.astype(low)).astype(wide)

    hidden_grad, partial = call(
        expand_kernel,
        [((2, length, hidden), low), (grid, wide)],
        second_low, slope, expand_w, shrink_w,
        name="expand",
    )
    partial_other = cores(partial)
    feed_pieces = call(
        weights_kernel,
        pieces_of(4 * hidden, singles),
        second_low, active, after(hidden_grad, partial), first_unit, block_vectors,
        owners=owners, scratch=(pltpu.VMEM((width, 4 * hidden), low),), name="weights",
    )
    feed_pieces = Pieces(paired(feed_pieces))
    partial_other = after(partial_other, feed_pieces.payload)
    first_half, sums, mixer_grad, mixer_grad_other, attended_grad, attended_grad_other = call(
        first_kernel,
        [
            (half, wide),
            ((8, width), wide),
            ((width, tall), low),
            ((tall, width), low),
            ((length, tall), low),
            ((tall, length), low),
        ],
        second_grad, partial, partial_other, first_unit, first_scale, block_vectors, attended, attended_far,
        second_sums, mixer_w, mixer_far, owners=owners, name="first", scratch=(pltpu.VMEM(grid, wide),),
    )

    def scattered(value):
        return lax.psum_scatter(value[0].astype(wide), "dp", scatter_dimension=0, tiled=True)

    if ringed:
        feed_pieces.advance(attended_grad)
    attended_grad_far = planes(attended_grad_other)
    mixer_grad_far = planes(mixer_grad_other)
    sums_far = planes(sums)
    halves = [(half, wide), (half, low)]
    packed_grad, kept_own, sent_own = call(
        lambda *refs: entry_kernel(0, *refs),
        [((length, 4 * tall), low), *halves],
        column, line, packed, logs, after(attended_grad, feed_pieces.payload, attended_grad_far), attend_w,
        owners=owners, name="entry", scratch=(pltpu.VMEM(grid, wide),),
    )
    if ringed:
        feed_pieces.advance(packed_grad, mixer_grad_far, sums_far)
    columns = 4 * tall + 128
    *pieces, kept_other, sent_other = call(
        gather_kernel,
        [*pieces_of(columns, singles), *halves],
        column, line, packed, logs, after(attended_grad_far, feed_pieces.payload), attend_w, block_input,
        packed_grad, mixer_grad, mixer_grad_far, sums, sums_far, owners=owners, name="gather",
        scratch=(
            pltpu.VMEM((width, columns), low),
            pltpu.VMEM((length, 4 * tall), low),
            pltpu.VMEM(grid, wide),
        ),
    )
    attend_pieces = Pieces(paired(pieces))
    output_half = planes(after(output_half, mixer_grad_far, sums_far))
    other_half = planes((kept_other + cores(sent_other).astype(wide)).astype(low))
    own_half = first_half + kept_own + cores(sent_own).astype(wide) + other_half.astype(wide)
    if ringed:
        feed_pieces.advance(attend_pieces.advance())
        feed_pair = feed_pieces.advance(output_half)
        attend_pieces.advance(other_half)
    else:
        feed_pair = scattered(feed_pieces.payload[None])
    (block_output,) = call(
        place_kernel, [((2, *grid), low)], output, output_half, cores(output_half), owners=owners, name="place"
    )
    (input_gradient,) = call(
        own_kernel,
        [((2, *grid), wide, "far")],
        own_half, cores(own_half), owners=owners, name="own", scratch=(pltpu.SemaphoreType.DMA((2,)),),
    )
    parts = [feed_pair[:, i * hidden : (i + 1) * hidden] for i in range(4)]
    feed_other = swap(jnp.concatenate([parts[1], parts[3]], axis=1))
    shrink_share = parts[0] + feed_other[:, :hidden]
    expand_share = parts[2] + feed_other[:, hidden:]
    other_squares = jnp.sum(shrink_share * shrink_share) + jnp.sum(expand_share * expand_share)
    if ringed:
        attend_pieces.advance(feed_other, block_output)
        attend_pair = attend_pieces.advance(other_squares)
    else:
        attend_pair = scattered(pieces[0])
    inner = lax.axis_size("tensor")

    def near(squares):
        squares = squares + cores(squares)
        return squares + planes(squares)

    def reduced(squares):
        hop = 1
        while hop < members:
            squares = squares + lax.ppermute(squares, "dp", [(i, i ^ hop) for i in range(members)])
            hop *= 2
        return squares

    vector_width = width // members
    vector_master = lax.dynamic_slice_in_dim(block_vectors, place * vector_width, vector_width, 1)
    if ringed:
        others = jnp.where(lax.broadcasted_iota(jnp.int32, (8, 128), 1) == 0, other_squares / 8, 0.0)
        (squares,) = call(
            lambda *refs: total_kernel(inner, *refs),
            [((8, 128), wide)],
            attend_pair, others, name="total",
        )
        squares = near(squares)
        input_far = planes(after(own_half.astype(low), squares))
        squares = reduced(squares)
        input_far = after(input_far, squares)
        groups = [
            (entry_master, entry_moment, entry_square),
            (mixer_master, mixer_moment, mixer_square),
            (expand_master, expand_moment, expand_square),
            (shrink_master.T, shrink_moment.T, shrink_square.T),
            (vector_master, vector_moment, vector_square),
        ]
        sources = [array for group in groups for array in group]
        targets = []
        for i, group in enumerate(groups):
            targets += [(group[0].shape, wide)] * 3 + [(group[0].shape, low)] * (i < 4)
        in_place = pl.BlockSpec(memory_space=pltpu.HBM)
        held = pl.BlockSpec(memory_space=pltpu.VMEM)
        *rest, input_gradient = pl.pallas_call(
            adam_kernel,
            out_shape=[
                jax.ShapeDtypeStruct(shape, kind)
                for shape, kind in [((1, 1), wide), *targets, ((2, *grid), wide)]
            ],
            in_specs=[pl.BlockSpec(memory_space=pltpu.SMEM)] + [held] * 6 + [in_place] * 16,
            out_specs=[held] + [in_place] * 20,
            scratch_shapes=[
                *[pltpu.VMEM(array.shape, wide) for array in sources],
                *[pltpu.VMEM(shape, kind) for shape, kind in targets],
                pltpu.VMEM(grid, wide),
                pltpu.SemaphoreType.DMA((35,)),
            ],
            input_output_aliases={22: 20},
            compiler_params=pltpu.CompilerParams(vmem_limit_bytes=VMEM_LIMIT),
            name="adam",
        )(
            owners, attend_pair, expand_share, shrink_share, squares, input_far, cores(input_far),
            *map(in_hbm, sources), input_gradient,
        )
        norm, *news = rest
        news[12:16] = [array.T for array in news[12:16]]
        return (block_output, input_gradient, norm[0, 0], *news)

    attend_share = attend_pair[:, : 4 * tall]
    vector_sum = attend_pair[:, 4 * tall :]
    entry_share = jnp.stack([attend_share[:, c * tall : (c + 1) * tall] for c in range(1, 4)])
    mixer_share = attend_share[:, :tall].T
    vector_share = vector_sum[:, :6].T
    squares = other_squares + jnp.sum(attend_share * attend_share)
    squares = squares + jnp.sum(vector_share * vector_share) / inner
    squares = near(jnp.full((8, 128), squares))
    squares = reduced(squares)
    other = planes(own_half.astype(low))
    other, rest = other.astype(wide), cores(other).astype(wide)
    other = jnp.concatenate([jnp.where(core == 0, other, rest), jnp.where(core == 0, rest, other)], axis=0)
    input_gradient = lax.dynamic_update_index_in_dim(input_gradient, other, 1 - plane, 0)
    gradient_norm = jnp.sqrt(squares[0, 0])
    factor = jnp.minimum(1.0, clip_bound / (gradient_norm + 1e-06))
    results = []
    for grad, moment, square, master, rate in (
        (entry_share, entry_moment, entry_square, entry_master, rate_matrix),
        (mixer_share, mixer_moment, mixer_square, mixer_master, rate_mixer),
        (expand_share, expand_moment, expand_square, expand_master, rate_matrix),
        (shrink_share.T, shrink_moment, shrink_square, shrink_master, rate_matrix),
    ):
        new = adam_update(grad, moment, square, master, factor, rate, decay_matrix)
        results += [*new, new[2].astype(low)]
    results += adam_update(
        vector_share, vector_moment, vector_square, vector_master, factor, rate_vector, 0.0
    )
    return (block_output, input_gradient, gradient_norm, *results)


def solution(mesh):
    in_specs = (
        P("dp", None, None),
        P("dp", None),
        P(None, "dp", "tensor"),
        P("tensor", "dp"),
        P("dp", "tensor"),
        P("tensor", "dp"),
        P(),
        P("dp", None, None),
        P(None, "dp", "tensor"),
        P(None, "dp", "tensor"),
        P("tensor", "dp"),
        P("tensor", "dp"),
        P("dp", "tensor"),
        P("dp", "tensor"),
        P("tensor", "dp"),
        P("tensor", "dp"),
        P(None, "dp"),
        P(None, "dp"),
    )
    out_specs = (
        P("dp", None, None),
        P("dp", None, None),
        P(),
        P(None, "dp", "tensor"),
        P(None, "dp", "tensor"),
        P(None, "dp", "tensor"),
        P(None, "dp", "tensor"),
        P("tensor", "dp"),
        P("tensor", "dp"),
        P("tensor", "dp"),
        P("tensor", "dp"),
        P("dp", "tensor"),
        P("dp", "tensor"),
        P("dp", "tensor"),
        P("dp", "tensor"),
        P("tensor", "dp"),
        P("tensor", "dp"),
        P("tensor", "dp"),
        P("tensor", "dp"),
        P(None, "dp"),
        P(None, "dp"),
        P(None, "dp"),
    )
    return jax.shard_map(shards, mesh=mesh, in_specs=in_specs, out_specs=out_specs, check_vma=False)
```

```python
import math

import jax
import jax.numpy as jnp
from jax import lax
from jax.experimental import pallas as pl
from jax.experimental.pallas import tpu as pltpu
from jax.sharding import PartitionSpec as P

HD = 64
ADAM_STEP = 3


norm_eps = 1e-12
clip_bound = 1.0
beta_first = 0.5
beta_second = 0.6
adam_eps = 1e-08
rate_matrix = 0.02
rate_mixer = 0.08
rate_vector = 0.25
decay_matrix = 0.01


low = jnp.bfloat16
wide = jnp.float32
RING_LIMIT = 16
VMEM_LIMIT = 24 * 2**20


def adam_update(grad, moment, square, master, factor, rate, decay):
    clipped = grad * factor
    moment_new = beta_first * moment + (1.0 - beta_first) * clipped
    square_new = beta_second * square + (1.0 - beta_second) * clipped * clipped
    corrected = moment_new / (1.0 - beta_first**ADAM_STEP)
    scaled = square_new / (1.0 - beta_second**ADAM_STEP)
    master_new = master - rate * (corrected / (jnp.sqrt(scaled) + adam_eps) + decay * master)
    return (moment_new, square_new, master_new)


def cores(value):
    size = lax.axis_size("tensor")
    return lax.ppermute(value, "tensor", [(i, i ^ 1) for i in range(size)])


def planes(value):
    size = lax.axis_size("tensor")
    return lax.ppermute(value, "tensor", [(i, i ^ 2) for i in range(size)])


def ring_order(size):
    return list(range(0, size, 2)) + list(range(size - 1, 0, -2))


def owners_here():
    size = lax.axis_size("dp")
    place = lax.axis_index("dp")
    seat = jnp.where(place % 2 == 0, place // 2, size - 1 - place // 2)
    sign = 1 - 2 * (lax.axis_index("tensor") % 2)
    spots = (seat + sign * jnp.arange(size, dtype=jnp.int32) + size) % size
    return jnp.where(spots < size // 2, 2 * spots, 2 * size - 1 - 2 * spots)


def after(value, *earlier):
    if not earlier:
        return value
    return lax.optimization_barrier((value, *earlier))[0]


def turn(value):
    size, inner = lax.axis_size("dp"), lax.axis_size("tensor")
    ring = ring_order(size)
    pairs = []
    for i in range(size):
        for t in range(inner):
            step = 1 if t % 2 == 0 else -1
            pairs.append((ring[i] * inner + t, ring[(i + step) % size] * inner + t))
    return lax.ppermute(value, ("dp", "tensor"), pairs)


def pair(value):
    return jnp.stack([value, cores(value)])


class Gather:
    def __init__(self, shard, load=None):
        self.size = lax.axis_size("dp")
        self.step = 0
        self.load = pair(shard) if load is None else load
        self.blocks = [(shard, (), 0)]
        self.loads = []

    def advance(self, *gates):
        self.step += 1
        if self.step == self.size // 2:
            self.load = turn(after(self.load[0], *gates))
            self.blocks.append((self.load, (), self.step))
        else:
            self.load = turn(after(self.load, *gates))
            self.take(self.load)
        self.loads.append(self.load)
        return self.load

    def take(self, load):
        self.blocks += [(load, (0,), self.size - self.step), (cores(load), (1,), self.step)]


def piece_order(size):
    far = size // 2
    order = [far] if far else []
    for step in range(far - 1, 0, -1):
        order += [step, size - step]
    return [*order, 0]


class TwinPieces:
    def __init__(self, pieces):
        self.near = [piece[0][0] if isinstance(piece, tuple) else piece[0] for piece in pieces]
        self.mine = self.theirs = self.near[0]
        self.step = 0
        if len(pieces) > 2:
            self.away = [cores(piece[1][0]) for piece in pieces[1:-1]]
            self.theirs = self.away[0]
            self.turns = 0

    def advance(self, *gates):
        self.step += 1
        load = after(turn(self.mine), *gates).astype(wide)
        if self.step == len(self.near) - 1:
            return self.near[-1].astype(wide) + load + cores(self.theirs).astype(wide)
        self.mine = (load + self.near[self.step].astype(wide)).astype(low)
        return self.mine

    def follow(self, *gates):
        self.turns += 1
        self.theirs = after(turn(self.theirs), *gates)
        if self.turns < len(self.away):
            self.theirs = (self.theirs.astype(wide) + self.away[self.turns].astype(wide)).astype(low)
        return self.theirs


class Pieces:
    def __init__(self, pieces):
        self.pieces = pieces
        self.step = 0
        self.payload = pieces[0][0]

    def advance(self, *gates):
        self.step += 1
        load = after(turn(self.payload), *gates)
        piece = self.pieces[self.step]
        if not isinstance(piece, tuple):
            return piece[0].astype(wide) + load[0].astype(wide) + cores(load)[1].astype(wide)
        theirs = cores(piece[1])
        if self.step == 1:
            mine = (load.astype(wide) + piece[0][0].astype(wide)).astype(low)
            self.payload = jnp.concatenate([mine[None], theirs], axis=0)
        else:
            both = jnp.concatenate([piece[0], theirs], axis=0).astype(wide)
            self.payload = (load.astype(wide) + both).astype(low)
        return self.payload


class Twin:
    def __init__(self, shard):
        self.size = lax.axis_size("dp")
        self.step = 0
        self.mine, self.theirs = [shard], [cores(shard)]
        self.blocks = [(shard, (), 0)]

    def advance(self, *gates):
        self.step += 1
        self.mine.append(turn(after(self.mine[-1], *gates)))
        self.blocks.append((self.mine[-1], (), (self.size - self.step) % self.size))

    def follow(self, *gates):
        self.theirs.append(turn(after(self.theirs[-1], *gates)))
        self.blocks.append((cores(self.theirs[-1]), (), self.step))


class TwinPieces:
    def __init__(self, pieces):
        self.near = [piece[0][0] if isinstance(piece, tuple) else piece[0] for piece in pieces]
        self.mine = self.theirs = self.near[0]
        self.step = 0
        if len(pieces) > 2:
            self.away = [cores(piece[1][0]) for piece in pieces[1:-1]]
            self.theirs = self.away[0]
            self.turns = 0

    def advance(self, *gates):
        self.step += 1
        load = after(turn(self.mine), *gates).astype(wide)
        if self.step == len(self.near) - 1:
            return self.near[-1].astype(wide) + load + cores(self.theirs).astype(wide)
        self.mine = (load + self.near[self.step].astype(wide)).astype(low)
        return self.mine

    def follow(self, *gates):
        self.turns += 1
        self.theirs = after(turn(self.theirs), *gates)
        if self.turns < len(self.away):
            self.theirs = (self.theirs.astype(wide) + self.away[self.turns].astype(wide)).astype(low)
        return self.theirs


class Pieces:
    def __init__(self, pieces):
        self.pieces = pieces
        self.step = 0
        self.payload = pieces[0][0]

    def advance(self, *gates):
        self.step += 1
        load = after(turn(self.payload), *gates)
        piece = self.pieces[self.step]
        if not isinstance(piece, tuple):
            return piece[0].astype(wide) + load[0].astype(wide) + cores(load)[1].astype(wide)
        theirs = cores(piece[1])
        if self.step == 1:
            mine = (load.astype(wide) + piece[0][0].astype(wide)).astype(low)
            self.payload = jnp.concatenate([mine[None], theirs], axis=0)
        else:
            both = jnp.concatenate([piece[0], theirs], axis=0).astype(wide)
            self.payload = (load.astype(wide) + both).astype(low)
        return self.payload


class Twin:
    def __init__(self, shard):
        self.size = lax.axis_size("dp")
        self.step = 0
        self.mine, self.theirs = [shard], [cores(shard)]
        self.blocks = [(shard, (), 0)]

    def advance(self, *gates):
        self.step += 1
        self.mine.append(turn(after(self.mine[-1], *gates)))
        self.blocks.append((self.mine[-1], (), (self.size - self.step) % self.size))

    def follow(self, *gates):
        self.theirs.append(turn(after(self.theirs[-1], *gates)))
        self.blocks.append((cores(self.theirs[-1]), (), self.step))


class Forward:
    def __init__(self, shard):
        self.size = lax.axis_size("dp")
        self.loads = [planes(shard)]
        self.blocks = [(self.loads[0], (), 0)]
        self.step = 0

    def take(self, load):
        self.step += 1
        load = planes(load)
        self.loads.append(load)
        if self.step == self.size // 2:
            self.blocks.append((load, (), self.step))
        else:
            self.blocks += [(load, (0,), self.size - self.step), (cores(load), (1,), self.step)]


def deal(owners, held, outs, distances):
    distances = list(distances)
    for out in outs:
        for i in range(out.shape[0]):
            count = out.shape[1]
            start = owners[distances.pop(0)] * count
            if count % 16 == 0:
                start = pl.multiple_of(start, 16)
            out[i] = held[pl.ds(start, count)]


def nn(left, right):
    return lax.dot_general(left, right, (((1,), (0,)), ((), ())), preferred_element_type=wide)


def nt(left, right):
    return lax.dot_general(left, right, (((1,), (1,)), ((), ())), preferred_element_type=wide)


def tn(left, right):
    return lax.dot_general(left, right, (((0,), (0,)), ((), ())), preferred_element_type=wide)


def fetch(picks, owners, blocks, first, target, sems, base):
    copies = []
    split = target.shape[1] // 2
    for i, (index, distance) in enumerate(picks):
        block = blocks[i]
        tall = block.shape[-2]
        start = owners[distance] * tall
        if tall % 16 == 0:
            start = pl.multiple_of(start, 16)
        for at in (0, split):
            source = block.at[(*index, slice(None), slice(first + at, first + at + split))]
            goal = target.at[pl.ds(start, tall), at : at + split]
            copies.append(
                pltpu.make_async_copy(source, goal, sems.at[base + 2 * i + at // split])
            )
    for copy in copies:
        copy.start()
    return copies


def keep(weights, target, sems, first):
    split = weights.shape[1] // 2
    copies = []
    for i in range(2):
        part = (slice(None), slice(i * split, (i + 1) * split))
        copies.append(pltpu.make_async_copy(weights.at[part], target.at[part], sems.at[first + i]))
    for copy in copies:
        copy.start()
    return copies


def settle(copies):
    for copy in copies:
        copy.wait()


def whole_mean(value):
    return jnp.mean(value, axis=-1, keepdims=True)


def scores(queries, keys, same):
    return jnp.where(same, nt(queries, keys) * HD ** (-0.5), -1e30)


def half_of(owners, size, other=False):
    which = owners[owners.shape[0] - 2]
    which = 1 - which if other else which
    return pl.ds(pl.multiple_of(which * (size // 2), 16), size // 2)


def row_of(owners, index):
    return jnp.abs(owners[owners.shape[0] - 1] - index)


def same_segment(lengths, row, size):
    column = jnp.zeros((size, 1), jnp.int32)
    line = jnp.zeros((1, size), jnp.int32)
    end = 0
    for k in range(lengths.shape[1]):
        end = end + lengths[row, k]
        column += (lax.broadcasted_iota(jnp.int32, (size, 1), 0) >= end).astype(jnp.int32)
        line += (lax.broadcasted_iota(jnp.int32, (1, size), 1) >= end).astype(jnp.int32)
    return column == line


def attend_kernel(picks, owners, lengths, inputs, *refs):
    many = len(picks[0])
    packed, attended, attended_other, logs, mixer_w, kept, weights, sems = refs[many:]
    copies = fetch(picks[0], owners, refs[:many], 0, weights, sems, 0)
    tall = mixer_w.shape[0]
    logs[...] = jnp.zeros_like(logs)
    settle(copies)
    leaving = keep(weights, kept, sems, 2 * many)
    mixer_w[...] = weights[:, :tall].T
    for index, goal in ((1, attended_other), (0, attended)):
        row = row_of(owners, index)
        same = same_segment(lengths, row, inputs.shape[1])
        packed[index] = nn(inputs[row], weights[...]).astype(low)
        for head in range(tall // HD):
            at = tall + head * HD
            raw = scores(
                packed[index, :, at : at + HD], packed[index, :, tall + at : tall + at + HD], same
            )
            peak = jnp.max(raw, axis=-1, keepdims=True)
            grown = jnp.exp(raw - peak)
            mass = jnp.sum(grown, axis=-1, keepdims=True)
            logs[index, :, head : head + 1] = peak + jnp.log(mass)
            probs = (grown * (1.0 / mass)).astype(low)
            result = nn(probs, packed[index, :, 2 * tall + at : 2 * tall + at + HD])
            if index:
                goal[head * HD : head * HD + HD] = result.T.astype(low)
            else:
                goal[:, head * HD : head * HD + HD] = result.astype(low)
    settle(leaving)


def mix_kernel(attended, attended_far, mixer_w, mixer_far, mixed):
    mixed[...] = (nn(attended[...], mixer_w[...]) + tn(attended_far[...], mixer_far[...])).astype(low)


def feed_kernel(picks, owners, inputs, mixed, mixed_other, vectors, *refs):
    many = len(picks[0])
    first_unit, first_scale, active, slope, shrunk, expand_kept, shrink_kept, expand_w, shrink_w, sems = refs[many:]
    hidden = expand_w.shape[2]
    copies = [
        fetch(picks[0], owners, refs[:many], p * hidden, (expand_w, shrink_w)[p % 2].at[p // 2], sems, 2 * many * p)
        for p in range(4)
    ]
    leaving = []
    value = inputs[...].astype(wide) + (mixed[...].astype(wide) + mixed_other[...].astype(wide)) + vectors[0:1]
    centered = value - whole_mean(value)
    scale = lax.rsqrt(whole_mean(centered * centered) + norm_eps)
    unit = centered * scale
    first_unit[...] = unit
    first_scale[...] = jnp.broadcast_to(scale, first_scale.shape)
    rounded = (unit * vectors[2:3] + vectors[3:4]).astype(low)
    total = None
    for half in range(2):
        settle(copies[2 * half])
        leaving += keep(expand_w.at[half], expand_kept.at[half], sems, 8 * many + 4 * half)
        value = nn(rounded, expand_w[half])
        spread = 0.5 * (1.0 + lax.erf(value * math.sqrt(0.5)))
        result = (value * spread).astype(low)
        active[half] = result
        bell = jnp.exp(-0.5 * value * value) * (1.0 / math.sqrt(2.0 * math.pi))
        slope[half] = (spread + value * bell).astype(slope.dtype)
        settle(copies[2 * half + 1])
        leaving += keep(shrink_w.at[half], shrink_kept.at[half], sems, 8 * many + 4 * half + 2)
        term = nt(result, shrink_w[half])
        total = term if total is None else total + term
    shrunk[...] = total.astype(shrunk.dtype)
    settle(leaving)


def sum_rows(value):
    return jnp.sum(value, axis=0, keepdims=True)


def norm_back(unit, scale, gain, grad):
    scaled = grad * gain
    back = scaled - whole_mean(scaled) - unit * whole_mean(scaled * unit)
    return back * scale


def second_kernel(
    owners, first_unit, shrunk, shrunk_other, vectors, cotangent, output, output_half, grad, grad_low, sums
):
    normed = first_unit[...] * vectors[2:3] + vectors[3:4]
    value = normed + (shrunk[...].astype(wide) + shrunk_other[...].astype(wide)) + vectors[1:2]
    centered = value - whole_mean(value)
    scale = lax.rsqrt(whole_mean(centered * centered) + norm_eps)
    unit = centered * scale
    output[...] = (unit * vectors[4:5] + vectors[5:6]).astype(low)
    output_half[...] = output[half_of(owners, output.shape[0])]
    incoming = cotangent[...].astype(wide)
    back = norm_back(unit, scale, vectors[4:5], incoming)
    grad[...] = back
    grad_low[...] = back.astype(low)
    sums[...] = jnp.zeros_like(sums)
    sums[1:2] = sum_rows(back)
    sums[4:5] = sum_rows(incoming * unit)
    sums[5:6] = sum_rows(incoming)


def expand_kernel(grad_low, slope, expand_w, shrink_w, hidden_grad, partial):
    total = None
    for half in range(2):
        grad = nn(grad_low[...], shrink_w[half])
        rounded = (grad * slope[half].astype(wide)).astype(low)
        hidden_grad[half] = rounded
        term = nt(rounded, expand_w[half])
        total = term if total is None else total + term
    partial[...] = total


def weights_kernel(owners, grad_low, active, hidden_grad, first_unit, vectors, *refs):
    outs, held = refs[:-1], refs[-1]
    normed = (first_unit[...] * vectors[2:3] + vectors[3:4]).astype(low)
    hidden = active.shape[2]
    for half in range(2):
        at = half * hidden
        held[:, at : at + hidden] = tn(grad_low[...], active[half]).astype(low)
        at += 2 * hidden
        held[:, at : at + hidden] = tn(normed, hidden_grad[half]).astype(low)
    deal(owners, held, outs, piece_order(sum(out.shape[0] for out in outs)))


def first_kernel(
    owners, grad, partial, partial_other, first_unit, first_scale, vectors, attended, attended_far, second_sums,
    mixer_w, mixer_far, first_half, sums, mixer_grad, mixer_grad_far, attended_grad, attended_grad_far, held
):
    incoming = grad[...] + (partial[...] + partial_other[...])
    unit = first_unit[...]
    back = norm_back(unit, first_scale[:, 0:1], vectors[2:3], incoming)
    held[...] = back
    first_half[...] = held[half_of(owners, held.shape[0])]
    sums[...] = second_sums[...]
    sums[0:1] = sum_rows(back)
    sums[2:3] = sum_rows(incoming * unit)
    sums[3:4] = sum_rows(incoming)
    rounded = back.astype(low)
    attended_grad_far[...] = nt(mixer_far[...], rounded).astype(low)
    attended_grad[...] = nt(rounded, mixer_w[...]).astype(low)
    mixer_grad_far[...] = nn(attended_far[...], rounded).astype(low)
    mixer_grad[...] = tn(rounded, attended[...]).astype(low)


def entry_kernel(index, owners, lengths, packed, logs, outer, weights, packed_grad, kept, sent, partial):
    tall = weights.shape[1] // 4
    if outer.shape[0] == tall:
        outer = outer[...].T
    row = row_of(owners, index)
    same = same_segment(lengths, row, packed.shape[1])
    turned = logs[index].T
    scale = HD ** (-0.5)
    packed_grad[:, :tall] = jnp.zeros((outer.shape[0], tall), low)
    for head in range(tall // HD):
        at = tall + head * HD
        queries = packed[index, :, at : at + HD]
        keys = packed[index, :, tall + at : tall + at + HD]
        values = packed[index, :, 2 * tall + at : 2 * tall + at + HD]
        outward = outer[:, head * HD : head * HD + HD]
        probs = jnp.exp(scores(keys, queries, same) - turned[head : head + 1])
        probs_grad = nt(values, outward)
        rows = jnp.sum(probs * probs_grad, axis=0, keepdims=True)
        score_grad = (probs * (probs_grad - rows)).astype(low)
        packed_grad[:, at : at + HD] = (tn(score_grad, keys) * scale).astype(low)
        packed_grad[:, tall + at : tall + at + HD] = (nn(score_grad, queries) * scale).astype(low)
        packed_grad[:, 2 * tall + at : 2 * tall + at + HD] = nn(probs.astype(low), outward).astype(low)
    partial[...] = nt(packed_grad[...], weights[...])
    kept[...] = partial[half_of(owners, partial.shape[0])]
    sent[...] = partial[half_of(owners, partial.shape[0], True)].astype(low)


def gather_kernel(
    owners, lengths, packed, logs, outer, weights, inputs, packed_grad, mixer_grad, mixer_grad_far, sums,
    sums_far, *refs
):
    outs, kept, sent, held, other_grad, partial = refs[:-5], *refs[-5:]
    entry_kernel(1, owners, lengths, packed, logs, outer, weights, other_grad, kept, sent, partial)
    tall = weights.shape[1] // 4
    done = packed_grad.shape[1]
    own, other = row_of(owners, 0), row_of(owners, 1)
    held[:, :done] = (
        tn(inputs[own], packed_grad[...]) + tn(inputs[other], other_grad[...])
    ).astype(low)
    held[:, :tall] = (mixer_grad[...].astype(wide) + mixer_grad_far[...].T.astype(wide)).astype(low)
    extra = held.shape[1] - done
    total = sums[...] + sums_far[...]
    lines = jnp.concatenate([total, jnp.zeros((extra - total.shape[0], total.shape[1]), wide)], axis=0)
    held[:, done:] = lines.T.astype(low)
    deal(owners, held, outs, piece_order(sum(out.shape[0] for out in outs)))


def fold(value):
    rows, columns = value.shape
    total = jnp.zeros((8, 128), wide)
    for i in range(rows // 8):
        for j in range(columns // 128):
            tile = value[8 * i : 8 * i + 8, 128 * j : 128 * j + 128]
            total = total + tile * tile
    return total


def total_kernel(inner, pair, others, squares):
    count = pair.shape[1] - 128
    squares[...] = others[...] + fold(pair[:, :count]) + fold(pair[:, count:]) * (1.0 / inner)


def adam_kernel(*refs):
    owners, attend, expand, shrink, squares, half, rest = refs[:7]
    sources, norm, targets, placed = refs[7:22], refs[23], refs[24:43], refs[43]
    held, made, other, sems = refs[44:59], refs[59:78], refs[78], refs[79]
    arriving = [
        pltpu.make_async_copy(s, h, sems.at[i]) for i, (s, h) in enumerate(zip(sources, held))
    ]
    for copy in arriving:
        copy.start()
    count = half.shape[0]
    other[half_of(owners, 2 * count)] = half[...].astype(wide)
    other[half_of(owners, 2 * count, True)] = rest[...].astype(wide)
    leaving = [pltpu.make_async_copy(other, placed.at[row_of(owners, 1)], sems.at[34])]
    leaving[0].start()
    found = jnp.sqrt(jnp.sum(squares[...], keepdims=True))
    norm[...] = found
    factor = jnp.minimum(1.0, clip_bound / (found + 1e-06))
    tall = held[0].shape[2]
    done = 4 * tall
    rounded = (tall + 127) // 128 * 128
    grads = [
        jnp.stack([attend[:, c * tall : (c + 1) * tall] for c in range(1, 4)]),
        attend[:, :rounded].T[:tall],
        expand[...],
        shrink[...],
        attend[:, done:].T[: held[12].shape[0]],
    ]
    rates = [rate_matrix, rate_mixer, rate_matrix, rate_matrix, rate_vector]
    for i, (grad, rate) in enumerate(zip(grads, rates)):
        settle(arriving[3 * i : 3 * i + 3])
        master, moment, square = (ref[...] for ref in held[3 * i : 3 * i + 3])
        decay = decay_matrix if i < 4 else 0.0
        new = adam_update(grad, moment, square, master, factor, rate, decay)
        new = (*new, new[2].astype(low)) if i < 4 else new
        for j, value in enumerate(new):
            k = 4 * i + j
            made[k][...] = value
            leaving.append(pltpu.make_async_copy(made[k], targets[k], sems.at[15 + k]))
            leaving[-1].start()
    settle(leaving)


def place_kernel(owners, own, half, rest, result):
    row = row_of(owners, 1)
    result[row_of(owners, 0)] = own[...]
    result[row, half_of(owners, own.shape[0])] = half[...]
    result[row, half_of(owners, own.shape[0], True)] = rest[...]


def own_kernel(owners, half, rest, result, sems):
    row = row_of(owners, 0)
    copies = [
        pltpu.make_async_copy(
            ref, result.at[row, half_of(owners, 2 * ref.shape[0], i == 1)], sems.at[i]
        )
        for i, ref in enumerate((half, rest))
    ]
    for copy in copies:
        copy.start()
    settle(copies)


def in_hbm(array):
    return pltpu.with_memory_space_constraint(array, pltpu.HBM)


def call(kernel, outs, *args, groups=None, owners=None, lengths=None, scratch=(), name=None):
    specs = [pl.BlockSpec(memory_space=pltpu.VMEM)] * len(args)
    if lengths is not None:
        args = (lengths, *args)
        specs = [pl.BlockSpec(memory_space=pltpu.SMEM), *specs]
    if owners is not None and groups is None:
        args = (owners, *args)
        specs = [pl.BlockSpec(memory_space=pltpu.SMEM), *specs]
    if groups is not None:
        picks = [[(index, distance) for _, index, distance in group] for group in groups]
        blocks = [in_hbm(array) for group in groups for array, _, _ in group]
        inner = kernel
        kernel = lambda *refs: inner(picks, *refs)
        args = (owners, *args, *blocks)
        specs = [pl.BlockSpec(memory_space=pltpu.SMEM), *specs]
        specs += [pl.BlockSpec(memory_space=pl.ANY)] * len(blocks)
    return pl.pallas_call(
        kernel,
        out_shape=tuple(jax.ShapeDtypeStruct(out[0], out[1]) for out in outs),
        in_specs=specs,
        out_specs=tuple(
            pl.BlockSpec(memory_space=pl.ANY if len(out) > 2 else pltpu.VMEM) for out in outs
        ),
        scratch_shapes=scratch,
        compiler_params=pltpu.CompilerParams(vmem_limit_bytes=VMEM_LIMIT),
        name=name,
    )(*args)


def shards(
    block_input,
    segment_lengths,
    entry_master,
    mixer_master,
    expand_master,
    shrink_master,
    block_vectors,
    block_cotangent,
    entry_moment,
    entry_square,
    mixer_moment,
    mixer_square,
    expand_moment,
    expand_square,
    shrink_moment,
    shrink_square,
    vector_moment,
    vector_square,
):
    rows, length, width = block_input.shape
    members = lax.axis_size("dp")
    place = lax.axis_index("dp")
    spot = lax.axis_index("tensor")
    core = spot % 2
    plane = spot // 2
    share = width // members
    tall = entry_master.shape[2]
    heads = 2 * tall // HD
    hidden = expand_master.shape[1]
    ringed = members <= RING_LIMIT

    attend_shard = jnp.concatenate(
        [mixer_master.T, entry_master[0], entry_master[1], entry_master[2]], axis=1
    ).astype(low)
    feed_shard = jnp.concatenate([expand_master, shrink_master.T], axis=1).astype(low)

    def one_row(value):
        return lax.dynamic_index_in_dim(value, plane, 0, False)

    inputs = one_row(block_input)
    cotangent = one_row(block_cotangent)
    grid = (length, width)

    def attend(blocks):
        count = len(blocks)
        return call(
            attend_kernel,
            [
                ((2, length, 4 * tall), low),
                ((length, tall), low),
                ((tall, length), low),
                ((2, length, 128), wide),
                ((tall, width), low),
                ((width, 4 * tall), low, "far"),
            ],
            block_input, groups=[blocks], owners=owners, lengths=segment_lengths, name="attend",
            scratch=(
                pltpu.VMEM((width, 4 * tall), low), pltpu.SemaphoreType.DMA((2 * count + 2,))
            ),
        )

    def mix(attended, attended_other, mixer_w, *gates):
        attended_far, mixer_far = planes(attended_other), planes(mixer_w)
        attended_far = after(attended_far, *gates)
        (mixed,) = call(
            mix_kernel, [(grid, low)], attended, attended_far, mixer_w, mixer_far, name="mix"
        )
        return attended_far, mixer_far, mixed

    far = members // 2
    if ringed:
        owners = jnp.concatenate([owners_here(), core[None], plane[None]])
        attend_gather = Gather(attend_shard)
        feed_far = planes(feed_shard)
        for step in range(far):
            attend_gather.advance()
        packed, attended, attended_other, logs, mixer_w, attend_w = attend(attend_gather.blocks)
        feed_pair = jnp.concatenate([feed_shard, feed_far], axis=1)
        feed_gather = Twin(after(feed_pair, attend_gather.loads[1]))
        M, T = feed_gather.mine, feed_gather.theirs
        for step in range(far):
            feed_gather.advance(*({1: lambda: (*attend_gather.loads[3:], T[1]), 2: lambda: (T[2], attended)}).get(step, tuple)())
            if step + 1 < far:
                feed_gather.follow(*({1: lambda: M[1:2], 2: lambda: M[2:3]}).get(step, tuple)())
            if step == far - 2:
                attended_far, mixer_far, mixed = mix(attended, after(attended_other, attended), mixer_w, M[3], T[3])
        feed_blocks = feed_gather.blocks
    else:
        owners = jnp.stack([jnp.zeros((), jnp.int32), core, plane])
        whole = lax.all_gather(attend_shard, "dp", axis=0, tiled=True)
        packed, attended, attended_other, logs, mixer_w, attend_w = attend([(whole, (), 0)])
        attended_far, mixer_far, mixed = mix(attended, attended_other, mixer_w)
        whole = lax.all_gather(feed_shard, "dp", axis=0, tiled=True)
        feed_blocks = [(jnp.concatenate([whole, planes(whole)], axis=1), (), 0)]
    many = len(feed_blocks)

    mixed_other = cores(mixed)
    first_unit, first_scale, active, slope, shrunk, expand_w, shrink_w = call(
        feed_kernel,
        [
            (grid, wide),
            ((length, 128), wide),
            ((2, length, hidden), low),
            ((2, length, hidden), low),
            (grid, low),
            ((2, width, hidden), low, "far"),
            ((2, width, hidden), low, "far"),
        ],
        inputs, mixed, mixed_other, block_vectors,
        groups=[feed_blocks], owners=owners, name="feed",
        scratch=(
            pltpu.VMEM((2, width, hidden), low),
            pltpu.VMEM((2, width, hidden), low),
            pltpu.SemaphoreType.DMA((8 * many + 8,)),
        ),
    )
    shrunk_other = cores(shrunk)
    half = (length // 2, width)
    output, output_half, second_grad, second_low, second_sums = call(
        second_kernel,
        [(grid, low), (half, low), (grid, wide), (grid, low), ((8, width), wide)],
        first_unit, shrunk, shrunk_other, block_vectors, cotangent,
        owners=owners, name="second",
    )

    def pieces_of(columns, counts):
        return [((count, share if ringed else width, columns), low) for count in counts]

    singles = [1] * members if ringed else [1]

    def paired(pieces):
        middle = [tuple(pieces[i : i + 2]) for i in range(1, len(pieces) - 1, 2)]
        return [pieces[0], *middle, pieces[-1]]

    def swap(value):
        return planes(value.astype(low)).astype(wide)

    hidden_grad, partial = call(
        expand_kernel,
        [((2, length, hidden), low), (grid, wide)],
        second_low, slope, expand_w, shrink_w,
        name="expand",
    )
    partial_other = cores(partial)
    feed_pieces = call(
        weights_kernel,
        pieces_of(4 * hidden, singles),
        second_low, active, after(hidden_grad, partial), first_unit, block_vectors,
        owners=owners, scratch=(pltpu.VMEM((width, 4 * hidden), low),), name="weights",
    )
    feed_pieces = TwinPieces(paired(feed_pieces))
    partial_other = after(partial_other, feed_pieces.mine)
    first_half, sums, mixer_grad, mixer_grad_other, attended_grad, attended_grad_other = call(
        first_kernel,
        [
            (half, wide),
            ((8, width), wide),
            ((width, tall), low),
            ((tall, width), low),
            ((length, tall), low),
            ((tall, length), low),
        ],
        second_grad, partial, partial_other, first_unit, first_scale, block_vectors, attended, attended_far,
        second_sums, mixer_w, mixer_far, owners=owners, name="first", scratch=(pltpu.VMEM(grid, wide),),
    )

    def scattered(value):
        return lax.psum_scatter(value[0].astype(wide), "dp", scatter_dimension=0, tiled=True)

    attended_grad_far = planes(attended_grad_other)
    if ringed:
        feed_pieces.advance(attended_grad_far)
        feed_pieces.follow(attended_grad_far)
    mixer_grad_far = planes(after(mixer_grad_other, attended_grad_far))
    sums_far = planes(after(sums, attended_grad_far))
    halves = [(half, wide), (half, low)]
    packed_grad, kept_own, sent_own = call(
        lambda *refs: entry_kernel(0, *refs),
        [((length, 4 * tall), low), *halves],
        packed, logs, after(attended_grad, feed_pieces.mine, feed_pieces.theirs, attended_grad_far), attend_w,
        owners=owners, lengths=segment_lengths, name="entry", scratch=(pltpu.VMEM(grid, wide),),
    )
    columns = 4 * tall + 128
    *pieces, kept_other, sent_other = call(
        gather_kernel,
        [*pieces_of(columns, singles), *halves],
        packed, logs, after(attended_grad_far, packed_grad), attend_w, block_input,
        packed_grad, mixer_grad, mixer_grad_far, sums, sums_far, owners=owners, lengths=segment_lengths, name="gather",
        scratch=(
            pltpu.VMEM((width, columns), low),
            pltpu.VMEM((length, 4 * tall), low),
            pltpu.VMEM(grid, wide),
        ),
    )
    attend_pieces = Pieces(paired(pieces))
    output_half = planes(after(output_half, mixer_grad_far, sums_far))
    other_half = planes((kept_other + cores(sent_other).astype(wide)).astype(low))
    own_half = first_half + kept_own + cores(sent_own).astype(wide) + other_half.astype(wide)
    if ringed:
        feed_pieces.advance(attend_pieces.payload)
        feed_pieces.follow(attend_pieces.payload)
        fourth = feed_pieces.advance()
        others = feed_pieces.follow()
        attend_pieces.advance(fourth)
        third = attend_pieces.advance()
        feed_pieces.mine = after(feed_pieces.mine, others, third)
        feed_pair = feed_pieces.advance(output_half)
        attend_pieces.advance(other_half)
    else:
        feed_pair = scattered(feed_pieces.mine[None])
    (block_output,) = call(
        place_kernel, [((2, *grid), low)], output, output_half, cores(output_half), owners=owners, name="place"
    )
    (input_gradient,) = call(
        own_kernel,
        [((2, *grid), wide, "far")],
        own_half, cores(own_half), owners=owners, name="own", scratch=(pltpu.SemaphoreType.DMA((2,)),),
    )
    parts = [feed_pair[:, i * hidden : (i + 1) * hidden] for i in range(4)]
    feed_other = swap(jnp.concatenate([parts[1], parts[3]], axis=1))
    shrink_share = parts[0] + feed_other[:, :hidden]
    expand_share = parts[2] + feed_other[:, hidden:]
    other_squares = jnp.sum(shrink_share * shrink_share) + jnp.sum(expand_share * expand_share)
    if ringed:
        attend_pair = attend_pieces.advance(other_squares, block_output)
    else:
        attend_pair = scattered(pieces[0])
    inner = lax.axis_size("tensor")

    def near(squares):
        squares = squares + cores(squares)
        return squares + planes(squares)

    def reduced(squares):
        hop = 1
        while hop < members:
            squares = squares + lax.ppermute(squares, "dp", [(i, i ^ hop) for i in range(members)])
            hop *= 2
        return squares

    vector_width = width // members
    vector_master = lax.dynamic_slice_in_dim(block_vectors, place * vector_width, vector_width, 1)
    if ringed:
        others = jnp.where(lax.broadcasted_iota(jnp.int32, (8, 128), 1) == 0, other_squares / 8, 0.0)
        (squares,) = call(
            lambda *refs: total_kernel(inner, *refs),
            [((8, 128), wide)],
            attend_pair, others, name="total",
        )
        squares = near(squares)
        input_far = planes(after(own_half.astype(low), squares))
        squares = reduced(squares)
        input_far = after(input_far, squares)
        groups = [
            (entry_master, entry_moment, entry_square),
            (mixer_master, mixer_moment, mixer_square),
            (expand_master, expand_moment, expand_square),
            (shrink_master.T, shrink_moment.T, shrink_square.T),
            (vector_master, vector_moment, vector_square),
        ]
        sources = [array for group in groups for array in group]
        targets = []
        for i, group in enumerate(groups):
            targets += [(group[0].shape, wide)] * 3 + [(group[0].shape, low)] * (i < 4)
        in_place = pl.BlockSpec(memory_space=pltpu.HBM)
        held = pl.BlockSpec(memory_space=pltpu.VMEM)
        *rest, input_gradient = pl.pallas_call(
            adam_kernel,
            out_shape=[
                jax.ShapeDtypeStruct(shape, kind)
                for shape, kind in [((1, 1), wide), *targets, ((2, *grid), wide)]
            ],
            in_specs=[pl.BlockSpec(memory_space=pltpu.SMEM)] + [held] * 6 + [in_place] * 16,
            out_specs=[held] + [in_place] * 20,
            scratch_shapes=[
                *[pltpu.VMEM(array.shape, wide) for array in sources],
                *[pltpu.VMEM(shape, kind) for shape, kind in targets],
                pltpu.VMEM(grid, wide),
                pltpu.SemaphoreType.DMA((35,)),
            ],
            input_output_aliases={22: 20},
            compiler_params=pltpu.CompilerParams(vmem_limit_bytes=VMEM_LIMIT),
            name="adam",
        )(
            owners, attend_pair, expand_share, shrink_share, squares, input_far, cores(input_far),
            *map(in_hbm, sources), input_gradient,
        )
        norm, *news = rest
        news[12:16] = [array.T for array in news[12:16]]
        return (block_output, input_gradient, norm[0, 0], *news)

    attend_share = attend_pair[:, : 4 * tall]
    vector_sum = attend_pair[:, 4 * tall :]
    entry_share = jnp.stack([attend_share[:, c * tall : (c + 1) * tall] for c in range(1, 4)])
    mixer_share = attend_share[:, :tall].T
    vector_share = vector_sum[:, :6].T
    squares = other_squares + jnp.sum(attend_share * attend_share)
    squares = squares + jnp.sum(vector_share * vector_share) / inner
    squares = near(jnp.full((8, 128), squares))
    squares = reduced(squares)
    other = planes(own_half.astype(low))
    other, rest = other.astype(wide), cores(other).astype(wide)
    other = jnp.concatenate([jnp.where(core == 0, other, rest), jnp.where(core == 0, rest, other)], axis=0)
    input_gradient = lax.dynamic_update_index_in_dim(input_gradient, other, 1 - plane, 0)
    gradient_norm = jnp.sqrt(squares[0, 0])
    factor = jnp.minimum(1.0, clip_bound / (gradient_norm + 1e-06))
    results = []
    for grad, moment, square, master, rate in (
        (entry_share, entry_moment, entry_square, entry_master, rate_matrix),
        (mixer_share, mixer_moment, mixer_square, mixer_master, rate_mixer),
        (expand_share, expand_moment, expand_square, expand_master, rate_matrix),
        (shrink_share.T, shrink_moment, shrink_square, shrink_master, rate_matrix),
    ):
        new = adam_update(grad, moment, square, master, factor, rate, decay_matrix)
        results += [*new, new[2].astype(low)]
    results += adam_update(
        vector_share, vector_moment, vector_square, vector_master, factor, rate_vector, 0.0
    )
    return (block_output, input_gradient, gradient_norm, *results)


def solution(mesh):
    in_specs = (
        P("dp", None, None),
        P("dp", None),
        P(None, "dp", "tensor"),
        P("tensor", "dp"),
        P("dp", "tensor"),
        P("tensor", "dp"),
        P(),
        P("dp", None, None),
        P(None, "dp", "tensor"),
        P(None, "dp", "tensor"),
        P("tensor", "dp"),
        P("tensor", "dp"),
        P("dp", "tensor"),
        P("dp", "tensor"),
        P("tensor", "dp"),
        P("tensor", "dp"),
        P(None, "dp"),
        P(None, "dp"),
    )
    out_specs = (
        P("dp", None, None),
        P("dp", None, None),
        P(),
        P(None, "dp", "tensor"),
        P(None, "dp", "tensor"),
        P(None, "dp", "tensor"),
        P(None, "dp", "tensor"),
        P("tensor", "dp"),
        P("tensor", "dp"),
        P("tensor", "dp"),
        P("tensor", "dp"),
        P("dp", "tensor"),
        P("dp", "tensor"),
        P("dp", "tensor"),
        P("dp", "tensor"),
        P("tensor", "dp"),
        P("tensor", "dp"),
        P("tensor", "dp"),
        P("tensor", "dp"),
        P(None, "dp"),
        P(None, "dp"),
        P(None, "dp"),
    )
    return jax.shard_map(shards, mesh=mesh, in_specs=in_specs, out_specs=out_specs, check_vma=False)
```

```python
import math

import jax
import jax.numpy as jnp
from jax import lax
from jax.experimental import pallas as pl
from jax.experimental.pallas import tpu as pltpu
from jax.sharding import PartitionSpec as P

HD = 64
ADAM_STEP = 3


norm_eps = 1e-12
clip_bound = 1.0
beta_first = 0.5
beta_second = 0.6
adam_eps = 1e-08
rate_matrix = 0.02
rate_mixer = 0.08
rate_vector = 0.25
decay_matrix = 0.01


low = jnp.bfloat16
wide = jnp.float32
RING_LIMIT = 16
VMEM_LIMIT = 24 * 2**20


def adam_update(grad, moment, square, master, factor, rate, decay):
    clipped = grad * factor
    moment_new = beta_first * moment + (1.0 - beta_first) * clipped
    square_new = beta_second * square + (1.0 - beta_second) * clipped * clipped
    corrected = moment_new / (1.0 - beta_first**ADAM_STEP)
    scaled = square_new / (1.0 - beta_second**ADAM_STEP)
    master_new = master - rate * (corrected / (jnp.sqrt(scaled) + adam_eps) + decay * master)
    return (moment_new, square_new, master_new)


def cores(value):
    size = lax.axis_size("tensor")
    return lax.ppermute(value, "tensor", [(i, i ^ 1) for i in range(size)])


def planes(value):
    size = lax.axis_size("tensor")
    return lax.ppermute(value, "tensor", [(i, i ^ 2) for i in range(size)])


def ring_order(size):
    return list(range(0, size, 2)) + list(range(size - 1, 0, -2))


def owners_here():
    size = lax.axis_size("dp")
    place = lax.axis_index("dp")
    seat = jnp.where(place % 2 == 0, place // 2, size - 1 - place // 2)
    sign = 1 - 2 * (lax.axis_index("tensor") % 2)
    spots = (seat + sign * jnp.arange(size, dtype=jnp.int32) + size) % size
    return jnp.where(spots < size // 2, 2 * spots, 2 * size - 1 - 2 * spots)


def after(value, *earlier):
    if not earlier:
        return value
    return lax.optimization_barrier((value, *earlier))[0]


def turn(value):
    size, inner = lax.axis_size("dp"), lax.axis_size("tensor")
    ring = ring_order(size)
    pairs = []
    for i in range(size):
        for t in range(inner):
            step = 1 if t % 2 == 0 else -1
            pairs.append((ring[i] * inner + t, ring[(i + step) % size] * inner + t))
    return lax.ppermute(value, ("dp", "tensor"), pairs)


def pair(value):
    return jnp.stack([value, cores(value)])


class Gather:
    def __init__(self, shard, load=None):
        self.size = lax.axis_size("dp")
        self.step = 0
        self.load = pair(shard) if load is None else load
        self.blocks = [(shard, (), 0)]
        self.loads = []

    def advance(self, *gates):
        self.step += 1
        if self.step == self.size // 2:
            self.load = turn(after(self.load[0], *gates))
            self.blocks.append((self.load, (), self.step))
        else:
            self.load = turn(after(self.load, *gates))
            self.take(self.load)
        self.loads.append(self.load)
        return self.load

    def take(self, load):
        self.blocks += [(load, (0,), self.size - self.step), (cores(load), (1,), self.step)]


def piece_order(size):
    far = size // 2
    order = [far] if far else []
    for step in range(far - 1, 0, -1):
        order += [step, size - step]
    return [*order, 0]


class TwinPieces:
    def __init__(self, pieces):
        self.near = [piece[0][0] if isinstance(piece, tuple) else piece[0] for piece in pieces]
        self.mine = self.theirs = self.near[0]
        self.step = 0
        if len(pieces) > 2:
            self.away = [cores(piece[1][0]) for piece in pieces[1:-1]]
            self.theirs = self.away[0]
            self.turns = 0

    def advance(self, *gates):
        self.step += 1
        load = after(turn(self.mine), *gates).astype(wide)
        if self.step == len(self.near) - 1:
            return self.near[-1].astype(wide) + load + cores(self.theirs).astype(wide)
        self.mine = (load + self.near[self.step].astype(wide)).astype(low)
        return self.mine

    def follow(self, *gates):
        self.turns += 1
        self.theirs = after(turn(self.theirs), *gates)
        if self.turns < len(self.away):
            self.theirs = (self.theirs.astype(wide) + self.away[self.turns].astype(wide)).astype(low)
        return self.theirs


class Pieces:
    def __init__(self, pieces):
        self.pieces = pieces
        self.step = 0
        self.payload = pieces[0][0]

    def advance(self, *gates):
        self.step += 1
        load = after(turn(self.payload), *gates)
        piece = self.pieces[self.step]
        if not isinstance(piece, tuple):
            return piece[0].astype(wide) + load[0].astype(wide) + cores(load)[1].astype(wide)
        theirs = cores(piece[1])
        if self.step == 1:
            mine = (load.astype(wide) + piece[0][0].astype(wide)).astype(low)
            self.payload = jnp.concatenate([mine[None], theirs], axis=0)
        else:
            both = jnp.concatenate([piece[0], theirs], axis=0).astype(wide)
            self.payload = (load.astype(wide) + both).astype(low)
        return self.payload


class Twin:
    def __init__(self, shard):
        self.size = lax.axis_size("dp")
        self.step = 0
        self.mine, self.theirs = [shard], [cores(shard)]
        self.blocks = [(shard, (), 0)]

    def advance(self, *gates):
        self.step += 1
        self.mine.append(turn(after(self.mine[-1], *gates)))
        self.blocks.append((self.mine[-1], (), (self.size - self.step) % self.size))

    def follow(self, *gates):
        self.theirs.append(turn(after(self.theirs[-1], *gates)))
        self.blocks.append((cores(self.theirs[-1]), (), self.step))


class TwinPieces:
    def __init__(self, pieces):
        self.near = [piece[0][0] if isinstance(piece, tuple) else piece[0] for piece in pieces]
        self.mine = self.theirs = self.near[0]
        self.step = 0
        if len(pieces) > 2:
            self.away = [cores(piece[1][0]) for piece in pieces[1:-1]]
            self.theirs = self.away[0]
            self.turns = 0

    def advance(self, *gates):
        self.step += 1
        load = after(turn(self.mine), *gates).astype(wide)
        if self.step == len(self.near) - 1:
            return self.near[-1].astype(wide) + load + cores(self.theirs).astype(wide)
        self.mine = (load + self.near[self.step].astype(wide)).astype(low)
        return self.mine

    def follow(self, *gates):
        self.turns += 1
        self.theirs = after(turn(self.theirs), *gates)
        if self.turns < len(self.away):
            self.theirs = (self.theirs.astype(wide) + self.away[self.turns].astype(wide)).astype(low)
        return self.theirs


class Pieces:
    def __init__(self, pieces):
        self.pieces = pieces
        self.step = 0
        self.payload = pieces[0][0]

    def advance(self, *gates):
        self.step += 1
        load = after(turn(self.payload), *gates)
        piece = self.pieces[self.step]
        if not isinstance(piece, tuple):
            return piece[0].astype(wide) + load[0].astype(wide) + cores(load)[1].astype(wide)
        theirs = cores(piece[1])
        if self.step == 1:
            mine = (load.astype(wide) + piece[0][0].astype(wide)).astype(low)
            self.payload = jnp.concatenate([mine[None], theirs], axis=0)
        else:
            both = jnp.concatenate([piece[0], theirs], axis=0).astype(wide)
            self.payload = (load.astype(wide) + both).astype(low)
        return self.payload


class Twin:
    def __init__(self, shard):
        self.size = lax.axis_size("dp")
        self.step = 0
        self.mine, self.theirs = [shard], [cores(shard)]
        self.blocks = [(shard, (), 0)]

    def advance(self, *gates):
        self.step += 1
        self.mine.append(turn(after(self.mine[-1], *gates)))
        self.blocks.append((self.mine[-1], (), (self.size - self.step) % self.size))

    def follow(self, *gates):
        self.theirs.append(turn(after(self.theirs[-1], *gates)))
        self.blocks.append((cores(self.theirs[-1]), (), self.step))


class Forward:
    def __init__(self, shard):
        self.size = lax.axis_size("dp")
        self.loads = [planes(shard)]
        self.blocks = [(self.loads[0], (), 0)]
        self.step = 0

    def take(self, load):
        self.step += 1
        load = planes(load)
        self.loads.append(load)
        if self.step == self.size // 2:
            self.blocks.append((load, (), self.step))
        else:
            self.blocks += [(load, (0,), self.size - self.step), (cores(load), (1,), self.step)]


def deal(owners, held, outs, distances):
    distances = list(distances)
    for out in outs:
        for i in range(out.shape[0]):
            count = out.shape[1]
            start = owners[distances.pop(0)] * count
            if count % 16 == 0:
                start = pl.multiple_of(start, 16)
            out[i] = held[pl.ds(start, count)]


def nn(left, right):
    return lax.dot_general(left, right, (((1,), (0,)), ((), ())), preferred_element_type=wide)


def nt(left, right):
    return lax.dot_general(left, right, (((1,), (1,)), ((), ())), preferred_element_type=wide)


def tn(left, right):
    return lax.dot_general(left, right, (((0,), (0,)), ((), ())), preferred_element_type=wide)


def fetch(picks, owners, blocks, first, target, sems, base):
    copies = []
    split = target.shape[1] // 2
    for i, (index, distance) in enumerate(picks):
        block = blocks[i]
        tall = block.shape[-2]
        start = owners[distance] * tall
        if tall % 16 == 0:
            start = pl.multiple_of(start, 16)
        for at in (0, split):
            source = block.at[(*index, slice(None), slice(first + at, first + at + split))]
            goal = target.at[pl.ds(start, tall), at : at + split]
            copies.append(
                pltpu.make_async_copy(source, goal, sems.at[base + 2 * i + at // split])
            )
    for copy in copies:
        copy.start()
    return copies


def keep(weights, target, sems, first):
    split = weights.shape[1] // 2
    copies = []
    for i in range(2):
        part = (slice(None), slice(i * split, (i + 1) * split))
        copies.append(pltpu.make_async_copy(weights.at[part], target.at[part], sems.at[first + i]))
    for copy in copies:
        copy.start()
    return copies


def settle(copies):
    for copy in copies:
        copy.wait()


def whole_mean(value):
    return jnp.mean(value, axis=-1, keepdims=True)


def scores(queries, keys, same):
    return jnp.where(same, nt(queries, keys) * HD ** (-0.5), -1e30)


def half_of(owners, size, other=False):
    which = owners[owners.shape[0] - 2]
    which = 1 - which if other else which
    return pl.ds(pl.multiple_of(which * (size // 2), 16), size // 2)


def row_of(owners, index):
    return jnp.abs(owners[owners.shape[0] - 1] - index)


def same_segment(lengths, row, size):
    column = jnp.zeros((size, 1), jnp.int32)
    line = jnp.zeros((1, size), jnp.int32)
    end = 0
    for k in range(lengths.shape[1]):
        end = end + lengths[row, k]
        column += (lax.broadcasted_iota(jnp.int32, (size, 1), 0) >= end).astype(jnp.int32)
        line += (lax.broadcasted_iota(jnp.int32, (1, size), 1) >= end).astype(jnp.int32)
    return column == line


def attend_kernel(picks, owners, lengths, inputs, *refs):
    many = len(picks[0])
    packed, attended, attended_other, logs, mixer_w, kept, weights, sems = refs[many:]
    copies = fetch(picks[0], owners, refs[:many], 0, weights, sems, 0)
    tall = mixer_w.shape[0]
    logs[...] = jnp.zeros_like(logs)
    settle(copies)
    leaving = keep(weights, kept, sems, 2 * many)
    mixer_w[...] = weights[:, :tall].T
    for index, goal in ((1, attended_other), (0, attended)):
        row = row_of(owners, index)
        same = same_segment(lengths, row, inputs.shape[1])
        packed[index] = nn(inputs[row], weights[...]).astype(low)
        for head in range(tall // HD):
            at = tall + head * HD
            raw = scores(
                packed[index, :, at : at + HD], packed[index, :, tall + at : tall + at + HD], same
            )
            peak = jnp.max(raw, axis=-1, keepdims=True)
            grown = jnp.exp(raw - peak)
            mass = jnp.sum(grown, axis=-1, keepdims=True)
            logs[index, :, head : head + 1] = peak + jnp.log(mass)
            probs = (grown * (1.0 / mass)).astype(low)
            result = nn(probs, packed[index, :, 2 * tall + at : 2 * tall + at + HD])
            if index:
                goal[head * HD : head * HD + HD] = result.T.astype(low)
            else:
                goal[:, head * HD : head * HD + HD] = result.astype(low)
    settle(leaving)


def mix_kernel(attended, attended_far, mixer_w, mixer_far, mixed):
    mixed[...] = (nn(attended[...], mixer_w[...]) + tn(attended_far[...], mixer_far[...])).astype(low)


def feed_kernel(picks, owners, inputs, mixed, mixed_other, vectors, *refs):
    many = len(picks[0])
    first_unit, first_scale, active, slope, shrunk, expand_kept, shrink_kept, expand_w, shrink_w, sems = refs[many:]
    hidden = expand_w.shape[2]
    copies = [
        fetch(picks[0], owners, refs[:many], p * hidden, (expand_w, shrink_w)[p % 2].at[p // 2], sems, 2 * many * p)
        for p in range(4)
    ]
    leaving = []
    value = inputs[...].astype(wide) + (mixed[...].astype(wide) + mixed_other[...].astype(wide)) + vectors[0:1]
    centered = value - whole_mean(value)
    scale = lax.rsqrt(whole_mean(centered * centered) + norm_eps)
    unit = centered * scale
    first_unit[...] = unit
    first_scale[...] = jnp.broadcast_to(scale, first_scale.shape)
    rounded = (unit * vectors[2:3] + vectors[3:4]).astype(low)
    total = None
    for half in range(2):
        settle(copies[2 * half])
        leaving += keep(expand_w.at[half], expand_kept.at[half], sems, 8 * many + 4 * half)
        value = nn(rounded, expand_w[half])
        spread = 0.5 * (1.0 + lax.erf(value * math.sqrt(0.5)))
        result = (value * spread).astype(low)
        active[half] = result
        bell = jnp.exp(-0.5 * value * value) * (1.0 / math.sqrt(2.0 * math.pi))
        slope[half] = (spread + value * bell).astype(slope.dtype)
        settle(copies[2 * half + 1])
        leaving += keep(shrink_w.at[half], shrink_kept.at[half], sems, 8 * many + 4 * half + 2)
        term = nt(result, shrink_w[half])
        total = term if total is None else total + term
    shrunk[...] = total.astype(shrunk.dtype)
    settle(leaving)


def sum_rows(value):
    return jnp.sum(value, axis=0, keepdims=True)


def norm_back(unit, scale, gain, grad):
    scaled = grad * gain
    back = scaled - whole_mean(scaled) - unit * whole_mean(scaled * unit)
    return back * scale


def second_kernel(
    owners, first_unit, shrunk, shrunk_other, vectors, cotangent, output, output_half, grad, grad_low, sums
):
    normed = first_unit[...] * vectors[2:3] + vectors[3:4]
    value = normed + (shrunk[...].astype(wide) + shrunk_other[...].astype(wide)) + vectors[1:2]
    centered = value - whole_mean(value)
    scale = lax.rsqrt(whole_mean(centered * centered) + norm_eps)
    unit = centered * scale
    output[...] = (unit * vectors[4:5] + vectors[5:6]).astype(low)
    output_half[...] = output[half_of(owners, output.shape[0])]
    incoming = cotangent[...].astype(wide)
    back = norm_back(unit, scale, vectors[4:5], incoming)
    grad[...] = back
    grad_low[...] = back.astype(low)
    sums[...] = jnp.zeros_like(sums)
    sums[1:2] = sum_rows(back)
    sums[4:5] = sum_rows(incoming * unit)
    sums[5:6] = sum_rows(incoming)


def expand_kernel(grad_low, slope, expand_w, shrink_w, hidden_grad, partial):
    total = None
    for half in range(2):
        grad = nn(grad_low[...], shrink_w[half])
        rounded = (grad * slope[half].astype(wide)).astype(low)
        hidden_grad[half] = rounded
        term = nt(rounded, expand_w[half])
        total = term if total is None else total + term
    partial[...] = total


def weights_kernel(owners, grad_low, active, hidden_grad, first_unit, vectors, *refs):
    outs, held = refs[:-1], refs[-1]
    normed = (first_unit[...] * vectors[2:3] + vectors[3:4]).astype(low)
    hidden = active.shape[2]
    for half in range(2):
        at = half * hidden
        held[:, at : at + hidden] = tn(grad_low[...], active[half]).astype(low)
        at += 2 * hidden
        held[:, at : at + hidden] = tn(normed, hidden_grad[half]).astype(low)
    deal(owners, held, outs, piece_order(sum(out.shape[0] for out in outs)))


def first_kernel(
    owners, grad, partial, partial_other, first_unit, first_scale, vectors, attended, attended_far, second_sums,
    mixer_w, mixer_far, first_half, sums, mixer_grad, mixer_grad_far, attended_grad, attended_grad_far, held
):
    incoming = grad[...] + (partial[...] + partial_other[...])
    unit = first_unit[...]
    back = norm_back(unit, first_scale[:, 0:1], vectors[2:3], incoming)
    held[...] = back
    first_half[...] = held[half_of(owners, held.shape[0])]
    sums[...] = second_sums[...]
    sums[0:1] = sum_rows(back)
    sums[2:3] = sum_rows(incoming * unit)
    sums[3:4] = sum_rows(incoming)
    rounded = back.astype(low)
    attended_grad_far[...] = nt(mixer_far[...], rounded).astype(low)
    attended_grad[...] = nt(rounded, mixer_w[...]).astype(low)
    mixer_grad_far[...] = nn(attended_far[...], rounded).astype(low)
    mixer_grad[...] = tn(rounded, attended[...]).astype(low)


def entry_kernel(index, owners, lengths, packed, logs, outer, weights, packed_grad, kept, sent, partial):
    tall = weights.shape[1] // 4
    if outer.shape[0] == tall:
        outer = outer[...].T
    row = row_of(owners, index)
    same = same_segment(lengths, row, packed.shape[1])
    turned = logs[index].T
    scale = HD ** (-0.5)
    packed_grad[:, :tall] = jnp.zeros((outer.shape[0], tall), low)
    for head in range(tall // HD):
        at = tall + head * HD
        queries = packed[index, :, at : at + HD]
        keys = packed[index, :, tall + at : tall + at + HD]
        values = packed[index, :, 2 * tall + at : 2 * tall + at + HD]
        outward = outer[:, head * HD : head * HD + HD]
        probs = jnp.exp(scores(keys, queries, same) - turned[head : head + 1])
        probs_grad = nt(values, outward)
        rows = jnp.sum(probs * probs_grad, axis=0, keepdims=True)
        score_grad = (probs * (probs_grad - rows)).astype(low)
        packed_grad[:, at : at + HD] = (tn(score_grad, keys) * scale).astype(low)
        packed_grad[:, tall + at : tall + at + HD] = (nn(score_grad, queries) * scale).astype(low)
        packed_grad[:, 2 * tall + at : 2 * tall + at + HD] = nn(probs.astype(low), outward).astype(low)
    partial[...] = nt(packed_grad[...], weights[...])
    kept[...] = partial[half_of(owners, partial.shape[0])]
    sent[...] = partial[half_of(owners, partial.shape[0], True)].astype(low)


def gather_kernel(
    owners, lengths, packed, logs, outer, weights, inputs, packed_grad, mixer_grad, mixer_grad_far, sums,
    sums_far, *refs
):
    outs, kept, sent, held, other_grad, partial = refs[:-5], *refs[-5:]
    entry_kernel(1, owners, lengths, packed, logs, outer, weights, other_grad, kept, sent, partial)
    tall = weights.shape[1] // 4
    done = packed_grad.shape[1]
    own, other = row_of(owners, 0), row_of(owners, 1)
    held[:, :done] = (
        tn(inputs[own], packed_grad[...]) + tn(inputs[other], other_grad[...])
    ).astype(low)
    held[:, :tall] = (mixer_grad[...].astype(wide) + mixer_grad_far[...].T.astype(wide)).astype(low)
    extra = held.shape[1] - done
    total = sums[...] + sums_far[...]
    lines = jnp.concatenate([total, jnp.zeros((extra - total.shape[0], total.shape[1]), wide)], axis=0)
    held[:, done:] = lines.T.astype(low)
    deal(owners, held, outs, piece_order(sum(out.shape[0] for out in outs)))


def fold(value):
    rows, columns = value.shape
    total = jnp.zeros((8, 128), wide)
    for i in range(rows // 8):
        for j in range(columns // 128):
            tile = value[8 * i : 8 * i + 8, 128 * j : 128 * j + 128]
            total = total + tile * tile
    return total


def total_kernel(inner, pair, others, squares):
    count = pair.shape[1] - 128
    squares[...] = others[...] + fold(pair[:, :count]) + fold(pair[:, count:]) * (1.0 / inner)


def adam_kernel(*refs):
    owners, attend, expand, shrink, squares, half, rest = refs[:7]
    sources, norm, targets, placed = refs[7:22], refs[23], refs[24:43], refs[43]
    held, made, other, sems = refs[44:59], refs[59:78], refs[78], refs[79]
    arriving = [
        pltpu.make_async_copy(s, h, sems.at[i]) for i, (s, h) in enumerate(zip(sources, held))
    ]
    for copy in arriving:
        copy.start()
    count = half.shape[0]
    other[half_of(owners, 2 * count)] = half[...].astype(wide)
    other[half_of(owners, 2 * count, True)] = rest[...].astype(wide)
    leaving = [pltpu.make_async_copy(other, placed.at[row_of(owners, 1)], sems.at[34])]
    leaving[0].start()
    found = jnp.sqrt(jnp.sum(squares[...], keepdims=True))
    norm[...] = found
    factor = jnp.minimum(1.0, clip_bound / (found + 1e-06))
    tall = held[0].shape[2]
    done = 4 * tall
    rounded = (tall + 127) // 128 * 128
    grads = [
        jnp.stack([attend[:, c * tall : (c + 1) * tall] for c in range(1, 4)]),
        attend[:, :rounded].T[:tall],
        expand[...],
        shrink[...],
        attend[:, done:].T[: held[12].shape[0]],
    ]
    rates = [rate_matrix, rate_mixer, rate_matrix, rate_matrix, rate_vector]
    for i, (grad, rate) in enumerate(zip(grads, rates)):
        settle(arriving[3 * i : 3 * i + 3])
        master, moment, square = (ref[...] for ref in held[3 * i : 3 * i + 3])
        decay = decay_matrix if i < 4 else 0.0
        new = adam_update(grad, moment, square, master, factor, rate, decay)
        new = (*new, new[2].astype(low)) if i < 4 else new
        for j, value in enumerate(new):
            k = 4 * i + j
            made[k][...] = value
            leaving.append(pltpu.make_async_copy(made[k], targets[k], sems.at[15 + k]))
            leaving[-1].start()
    settle(leaving)


def place_kernel(owners, own, half, rest, result):
    row = row_of(owners, 1)
    result[row_of(owners, 0)] = own[...]
    result[row, half_of(owners, own.shape[0])] = half[...]
    result[row, half_of(owners, own.shape[0], True)] = rest[...]


def own_kernel(owners, half, rest, result, sems):
    row = row_of(owners, 0)
    copies = [
        pltpu.make_async_copy(
            ref, result.at[row, half_of(owners, 2 * ref.shape[0], i == 1)], sems.at[i]
        )
        for i, ref in enumerate((half, rest))
    ]
    for copy in copies:
        copy.start()
    settle(copies)


def in_hbm(array):
    return pltpu.with_memory_space_constraint(array, pltpu.HBM)


def call(kernel, outs, *args, groups=None, owners=None, lengths=None, scratch=(), name=None):
    specs = [pl.BlockSpec(memory_space=pltpu.VMEM)] * len(args)
    if lengths is not None:
        args = (lengths, *args)
        specs = [pl.BlockSpec(memory_space=pltpu.SMEM), *specs]
    if owners is not None and groups is None:
        args = (owners, *args)
        specs = [pl.BlockSpec(memory_space=pltpu.SMEM), *specs]
    if groups is not None:
        picks = [[(index, distance) for _, index, distance in group] for group in groups]
        blocks = [in_hbm(array) for group in groups for array, _, _ in group]
        inner = kernel
        kernel = lambda *refs: inner(picks, *refs)
        args = (owners, *args, *blocks)
        specs = [pl.BlockSpec(memory_space=pltpu.SMEM), *specs]
        specs += [pl.BlockSpec(memory_space=pl.ANY)] * len(blocks)
    return pl.pallas_call(
        kernel,
        out_shape=tuple(jax.ShapeDtypeStruct(out[0], out[1]) for out in outs),
        in_specs=specs,
        out_specs=tuple(
            pl.BlockSpec(memory_space=pl.ANY if len(out) > 2 else pltpu.VMEM) for out in outs
        ),
        scratch_shapes=scratch,
        compiler_params=pltpu.CompilerParams(vmem_limit_bytes=VMEM_LIMIT),
        name=name,
    )(*args)


def shards(
    block_input,
    segment_lengths,
    entry_master,
    mixer_master,
    expand_master,
    shrink_master,
    block_vectors,
    block_cotangent,
    entry_moment,
    entry_square,
    mixer_moment,
    mixer_square,
    expand_moment,
    expand_square,
    shrink_moment,
    shrink_square,
    vector_moment,
    vector_square,
):
    rows, length, width = block_input.shape
    members = lax.axis_size("dp")
    place = lax.axis_index("dp")
    spot = lax.axis_index("tensor")
    core = spot % 2
    plane = spot // 2
    share = width // members
    tall = entry_master.shape[2]
    heads = 2 * tall // HD
    hidden = expand_master.shape[1]
    ringed = members <= RING_LIMIT

    attend_shard = jnp.concatenate(
        [mixer_master.T, entry_master[0], entry_master[1], entry_master[2]], axis=1
    ).astype(low)
    feed_shard = jnp.concatenate([expand_master, shrink_master.T], axis=1).astype(low)

    def one_row(value):
        return lax.dynamic_index_in_dim(value, plane, 0, False)

    inputs = one_row(block_input)
    cotangent = one_row(block_cotangent)
    grid = (length, width)

    def attend(blocks):
        count = len(blocks)
        return call(
            attend_kernel,
            [
                ((2, length, 4 * tall), low),
                ((length, tall), low),
                ((tall, length), low),
                ((2, length, 128), wide),
                ((tall, width), low),
                ((width, 4 * tall), low, "far"),
            ],
            block_input, groups=[blocks], owners=owners, lengths=segment_lengths, name="attend",
            scratch=(
                pltpu.VMEM((width, 4 * tall), low), pltpu.SemaphoreType.DMA((2 * count + 2,))
            ),
        )

    def mix(attended, attended_far, mixer_w, mixer_far, *gates):
        (mixed,) = call(
            mix_kernel, [(grid, low)], attended, after(attended_far, *gates), mixer_w, mixer_far, name="mix"
        )
        return mixed

    far = members // 2
    if ringed:
        owners = jnp.concatenate([owners_here(), core[None], plane[None]])
        attend_gather = Gather(attend_shard)
        feed_far = planes(feed_shard)
        for step in range(far):
            attend_gather.advance()
        packed, attended, attended_other, logs, mixer_w, attend_w = attend(attend_gather.blocks)
        feed_pair = jnp.concatenate([feed_shard, feed_far], axis=1)
        feed_gather = Twin(after(feed_pair, attend_gather.loads[1]))
        M, T = feed_gather.mine, feed_gather.theirs
        attended_far, mixer_far = planes(attended_other), planes(mixer_w)
        for step in range(far):
            feed_gather.advance(*({1: lambda: (*attend_gather.loads[3:], T[1]), 2: lambda: (T[2], attended), 3: lambda: (attended_far, mixer_far)}).get(step, tuple)())
            if step + 1 < far:
                feed_gather.follow(*({1: lambda: M[1:2], 2: lambda: M[2:3]}).get(step, tuple)())
            if step == far - 2:
                mixed = mix(attended, attended_far, mixer_w, mixer_far)
        feed_blocks = feed_gather.blocks
    else:
        owners = jnp.stack([jnp.zeros((), jnp.int32), core, plane])
        whole = lax.all_gather(attend_shard, "dp", axis=0, tiled=True)
        packed, attended, attended_other, logs, mixer_w, attend_w = attend([(whole, (), 0)])
        attended_far, mixer_far = planes(attended_other), planes(mixer_w)
        mixed = mix(attended, attended_far, mixer_w, mixer_far)
        whole = lax.all_gather(feed_shard, "dp", axis=0, tiled=True)
        feed_blocks = [(jnp.concatenate([whole, planes(whole)], axis=1), (), 0)]
    many = len(feed_blocks)

    mixed_other = cores(mixed)
    first_unit, first_scale, active, slope, shrunk, expand_w, shrink_w = call(
        feed_kernel,
        [
            (grid, wide),
            ((length, 128), wide),
            ((2, length, hidden), low),
            ((2, length, hidden), low),
            (grid, low),
            ((2, width, hidden), low, "far"),
            ((2, width, hidden), low, "far"),
        ],
        inputs, mixed, mixed_other, block_vectors,
        groups=[feed_blocks], owners=owners, name="feed",
        scratch=(
            pltpu.VMEM((2, width, hidden), low),
            pltpu.VMEM((2, width, hidden), low),
            pltpu.SemaphoreType.DMA((8 * many + 8,)),
        ),
    )
    shrunk_other = cores(shrunk)
    half = (length // 2, width)
    output, output_half, second_grad, second_low, second_sums = call(
        second_kernel,
        [(grid, low), (half, low), (grid, wide), (grid, low), ((8, width), wide)],
        first_unit, shrunk, shrunk_other, block_vectors, cotangent,
        owners=owners, name="second",
    )

    def pieces_of(columns, counts):
        return [((count, share if ringed else width, columns), low) for count in counts]

    singles = [1] * members if ringed else [1]

    def paired(pieces):
        middle = [tuple(pieces[i : i + 2]) for i in range(1, len(pieces) - 1, 2)]
        return [pieces[0], *middle, pieces[-1]]

    def swap(value):
        return planes(value.astype(low)).astype(wide)

    hidden_grad, partial = call(
        expand_kernel,
        [((2, length, hidden), low), (grid, wide)],
        second_low, slope, expand_w, shrink_w,
        name="expand",
    )
    partial_other = cores(partial)
    feed_pieces = call(
        weights_kernel,
        pieces_of(4 * hidden, singles),
        second_low, active, after(hidden_grad, partial), first_unit, block_vectors,
        owners=owners, scratch=(pltpu.VMEM((width, 4 * hidden), low),), name="weights",
    )
    feed_pieces = TwinPieces(paired(feed_pieces))
    partial_other = after(partial_other, feed_pieces.mine)
    first_half, sums, mixer_grad, mixer_grad_other, attended_grad, attended_grad_other = call(
        first_kernel,
        [
            (half, wide),
            ((8, width), wide),
            ((width, tall), low),
            ((tall, width), low),
            ((length, tall), low),
            ((tall, length), low),
        ],
        second_grad, partial, partial_other, first_unit, first_scale, block_vectors, attended, attended_far,
        second_sums, mixer_w, mixer_far, owners=owners, name="first", scratch=(pltpu.VMEM(grid, wide),),
    )

    def scattered(value):
        return lax.psum_scatter(value[0].astype(wide), "dp", scatter_dimension=0, tiled=True)

    attended_grad_far = planes(attended_grad_other)
    if ringed:
        feed_pieces.advance(attended_grad_far)
        feed_pieces.follow(attended_grad_far)
    mixer_grad_far = planes(after(mixer_grad_other, attended_grad_far))
    sums_far = planes(after(sums, attended_grad_far))
    halves = [(half, wide), (half, low)]
    packed_grad, kept_own, sent_own = call(
        lambda *refs: entry_kernel(0, *refs),
        [((length, 4 * tall), low), *halves],
        packed, logs, after(attended_grad, attended_grad_far), attend_w,
        owners=owners, lengths=segment_lengths, name="entry", scratch=(pltpu.VMEM(grid, wide),),
    )
    columns = 4 * tall + 128
    *pieces, kept_other, sent_other = call(
        gather_kernel,
        [*pieces_of(columns, singles), *halves],
        packed, logs, after(attended_grad_far, packed_grad), attend_w, block_input,
        packed_grad, mixer_grad, mixer_grad_far, sums, sums_far, owners=owners, lengths=segment_lengths, name="gather",
        scratch=(
            pltpu.VMEM((width, columns), low),
            pltpu.VMEM((length, 4 * tall), low),
            pltpu.VMEM(grid, wide),
        ),
    )
    attend_pieces = Pieces(paired(pieces))
    output_half = planes(after(output_half, mixer_grad_far, sums_far))
    other_half = planes((kept_other + cores(sent_other).astype(wide)).astype(low))
    own_half = first_half + kept_own + cores(sent_own).astype(wide) + other_half.astype(wide)
    if ringed:
        feed_pieces.advance(attend_pieces.payload)
        feed_pieces.follow(attend_pieces.payload)
        fourth = feed_pieces.advance()
        others = feed_pieces.follow()
        attend_pieces.advance(fourth)
        third = attend_pieces.advance()
        feed_pieces.mine = after(feed_pieces.mine, others, third)
        feed_pair = feed_pieces.advance(output_half)
        attend_pieces.advance(other_half)
    else:
        feed_pair = scattered(feed_pieces.mine[None])
    (block_output,) = call(
        place_kernel, [((2, *grid), low)], output, output_half, cores(output_half), owners=owners, name="place"
    )
    (input_gradient,) = call(
        own_kernel,
        [((2, *grid), wide, "far")],
        own_half, cores(own_half), owners=owners, name="own", scratch=(pltpu.SemaphoreType.DMA((2,)),),
    )
    parts = [feed_pair[:, i * hidden : (i + 1) * hidden] for i in range(4)]
    feed_other = swap(jnp.concatenate([parts[1], parts[3]], axis=1))
    shrink_share = parts[0] + feed_other[:, :hidden]
    expand_share = parts[2] + feed_other[:, hidden:]
    other_squares = jnp.sum(shrink_share * shrink_share) + jnp.sum(expand_share * expand_share)
    if ringed:
        attend_pair = attend_pieces.advance(other_squares, block_output)
    else:
        attend_pair = scattered(pieces[0])
    inner = lax.axis_size("tensor")

    def near(squares):
        squares = squares + cores(squares)
        return squares + planes(squares)

    def reduced(squares):
        hop = 1
        while hop < members:
            squares = squares + lax.ppermute(squares, "dp", [(i, i ^ hop) for i in range(members)])
            hop *= 2
        return squares

    vector_width = width // members
    vector_master = lax.dynamic_slice_in_dim(block_vectors, place * vector_width, vector_width, 1)
    if ringed:
        others = jnp.where(lax.broadcasted_iota(jnp.int32, (8, 128), 1) == 0, other_squares / 8, 0.0)
        (squares,) = call(
            lambda *refs: total_kernel(inner, *refs),
            [((8, 128), wide)],
            attend_pair, others, name="total",
        )
        squares = near(squares)
        input_far = planes(after(own_half.astype(low), squares))
        squares = reduced(squares)
        input_far = after(input_far, squares)
        groups = [
            (entry_master, entry_moment, entry_square),
            (mixer_master, mixer_moment, mixer_square),
            (expand_master, expand_moment, expand_square),
            (shrink_master.T, shrink_moment.T, shrink_square.T),
            (vector_master, vector_moment, vector_square),
        ]
        sources = [array for group in groups for array in group]
        targets = []
        for i, group in enumerate(groups):
            targets += [(group[0].shape, wide)] * 3 + [(group[0].shape, low)] * (i < 4)
        in_place = pl.BlockSpec(memory_space=pltpu.HBM)
        held = pl.BlockSpec(memory_space=pltpu.VMEM)
        *rest, input_gradient = pl.pallas_call(
            adam_kernel,
            out_shape=[
                jax.ShapeDtypeStruct(shape, kind)
                for shape, kind in [((1, 1), wide), *targets, ((2, *grid), wide)]
            ],
            in_specs=[pl.BlockSpec(memory_space=pltpu.SMEM)] + [held] * 6 + [in_place] * 16,
            out_specs=[held] + [in_place] * 20,
            scratch_shapes=[
                *[pltpu.VMEM(array.shape, wide) for array in sources],
                *[pltpu.VMEM(shape, kind) for shape, kind in targets],
                pltpu.VMEM(grid, wide),
                pltpu.SemaphoreType.DMA((35,)),
            ],
            input_output_aliases={22: 20},
            compiler_params=pltpu.CompilerParams(vmem_limit_bytes=VMEM_LIMIT),
            name="adam",
        )(
            owners, attend_pair, expand_share, shrink_share, squares, input_far, cores(input_far),
            *map(in_hbm, sources), input_gradient,
        )
        norm, *news = rest
        news[12:16] = [array.T for array in news[12:16]]
        return (block_output, input_gradient, norm[0, 0], *news)

    attend_share = attend_pair[:, : 4 * tall]
    vector_sum = attend_pair[:, 4 * tall :]
    entry_share = jnp.stack([attend_share[:, c * tall : (c + 1) * tall] for c in range(1, 4)])
    mixer_share = attend_share[:, :tall].T
    vector_share = vector_sum[:, :6].T
    squares = other_squares + jnp.sum(attend_share * attend_share)
    squares = squares + jnp.sum(vector_share * vector_share) / inner
    squares = near(jnp.full((8, 128), squares))
    squares = reduced(squares)
    other = planes(own_half.astype(low))
    other, rest = other.astype(wide), cores(other).astype(wide)
    other = jnp.concatenate([jnp.where(core == 0, other, rest), jnp.where(core == 0, rest, other)], axis=0)
    input_gradient = lax.dynamic_update_index_in_dim(input_gradient, other, 1 - plane, 0)
    gradient_norm = jnp.sqrt(squares[0, 0])
    factor = jnp.minimum(1.0, clip_bound / (gradient_norm + 1e-06))
    results = []
    for grad, moment, square, master, rate in (
        (entry_share, entry_moment, entry_square, entry_master, rate_matrix),
        (mixer_share, mixer_moment, mixer_square, mixer_master, rate_mixer),
        (expand_share, expand_moment, expand_square, expand_master, rate_matrix),
        (shrink_share.T, shrink_moment, shrink_square, shrink_master, rate_matrix),
    ):
        new = adam_update(grad, moment, square, master, factor, rate, decay_matrix)
        results += [*new, new[2].astype(low)]
    results += adam_update(
        vector_share, vector_moment, vector_square, vector_master, factor, rate_vector, 0.0
    )
    return (block_output, input_gradient, gradient_norm, *results)


def solution(mesh):
    in_specs = (
        P("dp", None, None),
        P("dp", None),
        P(None, "dp", "tensor"),
        P("tensor", "dp"),
        P("dp", "tensor"),
        P("tensor", "dp"),
        P(),
        P("dp", None, None),
        P(None, "dp", "tensor"),
        P(None, "dp", "tensor"),
        P("tensor", "dp"),
        P("tensor", "dp"),
        P("dp", "tensor"),
        P("dp", "tensor"),
        P("tensor", "dp"),
        P("tensor", "dp"),
        P(None, "dp"),
        P(None, "dp"),
    )
    out_specs = (
        P("dp", None, None),
        P("dp", None, None),
        P(),
        P(None, "dp", "tensor"),
        P(None, "dp", "tensor"),
        P(None, "dp", "tensor"),
        P(None, "dp", "tensor"),
        P("tensor", "dp"),
        P("tensor", "dp"),
        P("tensor", "dp"),
        P("tensor", "dp"),
        P("dp", "tensor"),
        P("dp", "tensor"),
        P("dp", "tensor"),
        P("dp", "tensor"),
        P("tensor", "dp"),
        P("tensor", "dp"),
        P("tensor", "dp"),
        P("tensor", "dp"),
        P(None, "dp"),
        P(None, "dp"),
        P(None, "dp"),
    )
    return jax.shard_map(shards, mesh=mesh, in_specs=in_specs, out_specs=out_specs, check_vma=False)
```

```python
import math

import jax
import jax.numpy as jnp
from jax import lax
from jax.experimental import pallas as pl
from jax.experimental.pallas import tpu as pltpu
from jax.sharding import PartitionSpec as P

HD = 64
ADAM_STEP = 3


norm_eps = 1e-12
clip_bound = 1.0
beta_first = 0.5
beta_second = 0.6
adam_eps = 1e-08
rate_matrix = 0.02
rate_mixer = 0.08
rate_vector = 0.25
decay_matrix = 0.01


low = jnp.bfloat16
wide = jnp.float32
RING_LIMIT = 16
VMEM_LIMIT = 24 * 2**20


def adam_update(grad, moment, square, master, factor, rate, decay):
    clipped = grad * factor
    moment_new = beta_first * moment + (1.0 - beta_first) * clipped
    square_new = beta_second * square + (1.0 - beta_second) * clipped * clipped
    corrected = moment_new / (1.0 - beta_first**ADAM_STEP)
    scaled = square_new / (1.0 - beta_second**ADAM_STEP)
    master_new = master - rate * (corrected / (jnp.sqrt(scaled) + adam_eps) + decay * master)
    return (moment_new, square_new, master_new)


def cores(value):
    size = lax.axis_size("tensor")
    return lax.ppermute(value, "tensor", [(i, i ^ 1) for i in range(size)])


def planes(value):
    size = lax.axis_size("tensor")
    return lax.ppermute(value, "tensor", [(i, i ^ 2) for i in range(size)])


def ring_order(size):
    return list(range(0, size, 2)) + list(range(size - 1, 0, -2))


def owners_here():
    size = lax.axis_size("dp")
    place = lax.axis_index("dp")
    seat = jnp.where(place % 2 == 0, place // 2, size - 1 - place // 2)
    sign = 1 - 2 * (lax.axis_index("tensor") % 2)
    spots = (seat + sign * jnp.arange(size, dtype=jnp.int32) + size) % size
    return jnp.where(spots < size // 2, 2 * spots, 2 * size - 1 - 2 * spots)


def after(value, *earlier):
    if not earlier:
        return value
    return lax.optimization_barrier((value, *earlier))[0]


def turn(value):
    size, inner = lax.axis_size("dp"), lax.axis_size("tensor")
    ring = ring_order(size)
    pairs = []
    for i in range(size):
        for t in range(inner):
            step = 1 if t % 2 == 0 else -1
            pairs.append((ring[i] * inner + t, ring[(i + step) % size] * inner + t))
    return lax.ppermute(value, ("dp", "tensor"), pairs)


def pair(value):
    return jnp.stack([value, cores(value)])


class Gather:
    def __init__(self, shard, load=None):
        self.size = lax.axis_size("dp")
        self.step = 0
        self.load = pair(shard) if load is None else load
        self.blocks = [(shard, (), 0)]
        self.loads = []

    def advance(self, *gates):
        self.step += 1
        if self.step == self.size // 2:
            self.load = turn(after(self.load[0], *gates))
            self.blocks.append((self.load, (), self.step))
        else:
            self.load = turn(after(self.load, *gates))
            self.take(self.load)
        self.loads.append(self.load)
        return self.load

    def take(self, load):
        self.blocks += [(load, (0,), self.size - self.step), (cores(load), (1,), self.step)]


def piece_order(size):
    far = size // 2
    order = [far] if far else []
    for step in range(far - 1, 0, -1):
        order += [step, size - step]
    return [*order, 0]


class TwinPieces:
    def __init__(self, pieces):
        self.near = [piece[0][0] if isinstance(piece, tuple) else piece[0] for piece in pieces]
        self.mine = self.theirs = self.near[0]
        self.step = 0
        if len(pieces) > 2:
            self.away = [cores(piece[1][0]) for piece in pieces[1:-1]]
            self.theirs = self.away[0]
            self.turns = 0

    def advance(self, *gates):
        self.step += 1
        load = after(turn(self.mine), *gates).astype(wide)
        if self.step == len(self.near) - 1:
            return self.near[-1].astype(wide) + load + cores(self.theirs).astype(wide)
        self.mine = (load + self.near[self.step].astype(wide)).astype(low)
        return self.mine

    def follow(self, *gates):
        self.turns += 1
        self.theirs = after(turn(self.theirs), *gates)
        if self.turns < len(self.away):
            self.theirs = (self.theirs.astype(wide) + self.away[self.turns].astype(wide)).astype(low)
        return self.theirs


class Pieces:
    def __init__(self, pieces):
        self.pieces = pieces
        self.step = 0
        self.payload = pieces[0][0]

    def advance(self, *gates):
        self.step += 1
        load = after(turn(self.payload), *gates)
        piece = self.pieces[self.step]
        if not isinstance(piece, tuple):
            return piece, load, cores(load)
        theirs = cores(piece[1])
        if self.step == 1:
            mine = (load.astype(wide) + piece[0][0].astype(wide)).astype(low)
            self.payload = jnp.concatenate([mine[None], theirs], axis=0)
        else:
            both = jnp.concatenate([piece[0], theirs], axis=0).astype(wide)
            self.payload = (load.astype(wide) + both).astype(low)
        return self.payload


class Twin:
    def __init__(self, shard):
        self.size = lax.axis_size("dp")
        self.step = 0
        self.mine, self.theirs = [shard], [cores(shard)]
        self.blocks = [(shard, (), 0)]

    def advance(self, *gates):
        self.step += 1
        self.mine.append(turn(after(self.mine[-1], *gates)))
        self.blocks.append((self.mine[-1], (), (self.size - self.step) % self.size))

    def follow(self, *gates):
        self.theirs.append(turn(after(self.theirs[-1], *gates)))
        self.blocks.append((cores(self.theirs[-1]), (), self.step))


class TwinPieces:
    def __init__(self, pieces):
        self.near = [piece[0][0] if isinstance(piece, tuple) else piece[0] for piece in pieces]
        self.mine = self.theirs = self.near[0]
        self.step = 0
        if len(pieces) > 2:
            self.away = [cores(piece[1][0]) for piece in pieces[1:-1]]
            self.theirs = self.away[0]
            self.turns = 0

    def advance(self, *gates):
        self.step += 1
        load = after(turn(self.mine), *gates).astype(wide)
        if self.step == len(self.near) - 1:
            return self.near[-1].astype(wide) + load + cores(self.theirs).astype(wide)
        self.mine = (load + self.near[self.step].astype(wide)).astype(low)
        return self.mine

    def follow(self, *gates):
        self.turns += 1
        self.theirs = after(turn(self.theirs), *gates)
        if self.turns < len(self.away):
            self.theirs = (self.theirs.astype(wide) + self.away[self.turns].astype(wide)).astype(low)
        return self.theirs


class Pieces:
    def __init__(self, pieces):
        self.pieces = pieces
        self.step = 0
        self.payload = pieces[0][0]

    def advance(self, *gates):
        self.step += 1
        load = after(turn(self.payload), *gates)
        piece = self.pieces[self.step]
        if not isinstance(piece, tuple):
            return piece, load, cores(load)
        theirs = cores(piece[1])
        if self.step == 1:
            mine = (load.astype(wide) + piece[0][0].astype(wide)).astype(low)
            self.payload = jnp.concatenate([mine[None], theirs], axis=0)
        else:
            both = jnp.concatenate([piece[0], theirs], axis=0).astype(wide)
            self.payload = (load.astype(wide) + both).astype(low)
        return self.payload


class Twin:
    def __init__(self, shard):
        self.size = lax.axis_size("dp")
        self.step = 0
        self.mine, self.theirs = [shard], [cores(shard)]
        self.blocks = [(shard, (), 0)]

    def advance(self, *gates):
        self.step += 1
        self.mine.append(turn(after(self.mine[-1], *gates)))
        self.blocks.append((self.mine[-1], (), (self.size - self.step) % self.size))

    def follow(self, *gates):
        self.theirs.append(turn(after(self.theirs[-1], *gates)))
        self.blocks.append((cores(self.theirs[-1]), (), self.step))


class Forward:
    def __init__(self, shard):
        self.size = lax.axis_size("dp")
        self.loads = [planes(shard)]
        self.blocks = [(self.loads[0], (), 0)]
        self.step = 0

    def take(self, load):
        self.step += 1
        load = planes(load)
        self.loads.append(load)
        if self.step == self.size // 2:
            self.blocks.append((load, (), self.step))
        else:
            self.blocks += [(load, (0,), self.size - self.step), (cores(load), (1,), self.step)]


def deal(owners, held, outs, distances):
    distances = list(distances)
    for out in outs:
        for i in range(out.shape[0]):
            count = out.shape[1]
            start = owners[distances.pop(0)] * count
            if count % 16 == 0:
                start = pl.multiple_of(start, 16)
            out[i] = held[pl.ds(start, count)]


def nn(left, right):
    return lax.dot_general(left, right, (((1,), (0,)), ((), ())), preferred_element_type=wide)


def nt(left, right):
    return lax.dot_general(left, right, (((1,), (1,)), ((), ())), preferred_element_type=wide)


def tn(left, right):
    return lax.dot_general(left, right, (((0,), (0,)), ((), ())), preferred_element_type=wide)


def fetch(picks, owners, blocks, first, target, sems, base):
    copies = []
    split = target.shape[1] // 2
    for i, (index, distance) in enumerate(picks):
        block = blocks[i]
        tall = block.shape[-2]
        start = owners[distance] * tall
        if tall % 16 == 0:
            start = pl.multiple_of(start, 16)
        for at in (0, split):
            source = block.at[(*index, slice(None), slice(first + at, first + at + split))]
            goal = target.at[pl.ds(start, tall), at : at + split]
            copies.append(
                pltpu.make_async_copy(source, goal, sems.at[base + 2 * i + at // split])
            )
    for copy in copies:
        copy.start()
    return copies


def keep(weights, target, sems, first):
    split = weights.shape[1] // 2
    copies = []
    for i in range(2):
        part = (slice(None), slice(i * split, (i + 1) * split))
        copies.append(pltpu.make_async_copy(weights.at[part], target.at[part], sems.at[first + i]))
    for copy in copies:
        copy.start()
    return copies


def settle(copies):
    for copy in copies:
        copy.wait()


def whole_mean(value):
    return jnp.mean(value, axis=-1, keepdims=True)


def scores(queries, keys, same):
    return jnp.where(same, nt(queries, keys) * HD ** (-0.5), -1e30)


def half_of(owners, size, other=False):
    which = owners[owners.shape[0] - 2]
    which = 1 - which if other else which
    return pl.ds(pl.multiple_of(which * (size // 2), 16), size // 2)


def row_of(owners, index):
    return jnp.abs(owners[owners.shape[0] - 1] - index)


def same_segment(lengths, row, size):
    column = jnp.zeros((size, 1), jnp.int32)
    line = jnp.zeros((1, size), jnp.int32)
    end = 0
    for k in range(lengths.shape[1]):
        end = end + lengths[row, k]
        column += (lax.broadcasted_iota(jnp.int32, (size, 1), 0) >= end).astype(jnp.int32)
        line += (lax.broadcasted_iota(jnp.int32, (1, size), 1) >= end).astype(jnp.int32)
    return column == line


def mixer_kernel(picks, owners, *refs):
    many = len(picks[0])
    mixer_w, weights, sems = refs[many:]
    settle(fetch(picks[0], owners, refs[:many], 0, weights, sems, 0))
    mixer_w[...] = weights[:, : mixer_w.shape[0]].T


def attend_kernel(picks, owners, lengths, inputs, *refs):
    many = len(picks[0])
    packed, attended, attended_other, logs, kept, weights, sems = refs[many:]
    copies = fetch(picks[0], owners, refs[:many], 0, weights, sems, 0)
    tall = weights.shape[1] // 4
    logs[...] = jnp.zeros_like(logs)
    settle(copies)
    leaving = keep(weights, kept, sems, 2 * many)
    for index, goal in ((1, attended_other), (0, attended)):
        row = row_of(owners, index)
        same = same_segment(lengths, row, inputs.shape[1])
        packed[index] = nn(inputs[row], weights[...]).astype(low)
        for head in range(tall // HD):
            at = tall + head * HD
            raw = scores(
                packed[index, :, at : at + HD], packed[index, :, tall + at : tall + at + HD], same
            )
            peak = jnp.max(raw, axis=-1, keepdims=True)
            grown = jnp.exp(raw - peak)
            mass = jnp.sum(grown, axis=-1, keepdims=True)
            logs[index, :, head : head + 1] = peak + jnp.log(mass)
            probs = (grown * (1.0 / mass)).astype(low)
            result = nn(probs, packed[index, :, 2 * tall + at : 2 * tall + at + HD])
            if index:
                goal[head * HD : head * HD + HD] = result.T.astype(low)
            else:
                goal[:, head * HD : head * HD + HD] = result.astype(low)
    settle(leaving)


def mix_kernel(attended, attended_far, mixer_w, mixer_far, mixed):
    mixed[...] = (nn(attended[...], mixer_w[...]) + tn(attended_far[...], mixer_far[...])).astype(low)


def feed_kernel(picks, owners, inputs, mixed, mixed_other, vectors, *refs):
    many = len(picks[0])
    first_unit, first_scale, active, slope, shrunk, expand_kept, shrink_kept, expand_w, shrink_w, sems = refs[many:]
    hidden = expand_w.shape[2]
    copies = [
        fetch(picks[0], owners, refs[:many], p * hidden, (expand_w, shrink_w)[p % 2].at[p // 2], sems, 2 * many * p)
        for p in range(4)
    ]
    leaving = []
    value = inputs[...].astype(wide) + (mixed[...].astype(wide) + mixed_other[...].astype(wide)) + vectors[0:1]
    centered = value - whole_mean(value)
    scale = lax.rsqrt(whole_mean(centered * centered) + norm_eps)
    unit = centered * scale
    first_unit[...] = unit
    first_scale[...] = jnp.broadcast_to(scale, first_scale.shape)
    rounded = (unit * vectors[2:3] + vectors[3:4]).astype(low)
    total = None
    for half in range(2):
        settle(copies[2 * half])
        leaving += keep(expand_w.at[half], expand_kept.at[half], sems, 8 * many + 4 * half)
        value = nn(rounded, expand_w[half])
        spread = 0.5 * (1.0 + lax.erf(value * math.sqrt(0.5)))
        result = (value * spread).astype(low)
        active[half] = result
        bell = jnp.exp(-0.5 * value * value) * (1.0 / math.sqrt(2.0 * math.pi))
        slope[half] = (spread + value * bell).astype(slope.dtype)
        settle(copies[2 * half + 1])
        leaving += keep(shrink_w.at[half], shrink_kept.at[half], sems, 8 * many + 4 * half + 2)
        term = nt(result, shrink_w[half])
        total = term if total is None else total + term
    shrunk[...] = total.astype(shrunk.dtype)
    settle(leaving)


def sum_rows(value):
    return jnp.sum(value, axis=0, keepdims=True)


def norm_back(unit, scale, gain, grad):
    scaled = grad * gain
    back = scaled - whole_mean(scaled) - unit * whole_mean(scaled * unit)
    return back * scale


def second_kernel(
    owners, first_unit, shrunk, shrunk_other, vectors, cotangent, output, output_half, grad, grad_low, sums
):
    normed = first_unit[...] * vectors[2:3] + vectors[3:4]
    value = normed + (shrunk[...].astype(wide) + shrunk_other[...].astype(wide)) + vectors[1:2]
    centered = value - whole_mean(value)
    scale = lax.rsqrt(whole_mean(centered * centered) + norm_eps)
    unit = centered * scale
    output[...] = (unit * vectors[4:5] + vectors[5:6]).astype(low)
    output_half[...] = output[half_of(owners, output.shape[0])]
    incoming = cotangent[...].astype(wide)
    back = norm_back(unit, scale, vectors[4:5], incoming)
    grad[...] = back
    grad_low[...] = back.astype(low)
    sums[...] = jnp.zeros_like(sums)
    sums[1:2] = sum_rows(back)
    sums[4:5] = sum_rows(incoming * unit)
    sums[5:6] = sum_rows(incoming)


def expand_kernel(grad_low, slope, expand_w, shrink_w, hidden_grad, partial):
    total = None
    for half in range(2):
        grad = nn(grad_low[...], shrink_w[half])
        rounded = (grad * slope[half].astype(wide)).astype(low)
        hidden_grad[half] = rounded
        term = nt(rounded, expand_w[half])
        total = term if total is None else total + term
    partial[...] = total


def weights_kernel(owners, grad_low, active, hidden_grad, first_unit, vectors, *refs):
    outs, held = refs[:-1], refs[-1]
    normed = (first_unit[...] * vectors[2:3] + vectors[3:4]).astype(low)
    hidden = active.shape[2]
    for half in range(2):
        at = half * hidden
        held[:, at : at + hidden] = tn(grad_low[...], active[half]).astype(low)
        at += 2 * hidden
        held[:, at : at + hidden] = tn(normed, hidden_grad[half]).astype(low)
    deal(owners, held, outs, piece_order(sum(out.shape[0] for out in outs)))


def first_kernel(
    owners, grad, partial, partial_other, first_unit, first_scale, vectors, attended, attended_far, second_sums,
    mixer_w, mixer_far, first_half, sums, mixer_grad, mixer_grad_far, attended_grad, attended_grad_far, held
):
    incoming = grad[...] + (partial[...] + partial_other[...])
    unit = first_unit[...]
    back = norm_back(unit, first_scale[:, 0:1], vectors[2:3], incoming)
    held[...] = back
    first_half[...] = held[half_of(owners, held.shape[0])]
    sums[...] = second_sums[...]
    sums[0:1] = sum_rows(back)
    sums[2:3] = sum_rows(incoming * unit)
    sums[3:4] = sum_rows(incoming)
    rounded = back.astype(low)
    attended_grad_far[...] = nt(mixer_far[...], rounded).astype(low)
    attended_grad[...] = nt(rounded, mixer_w[...]).astype(low)
    mixer_grad_far[...] = nn(attended_far[...], rounded).astype(low)
    mixer_grad[...] = tn(rounded, attended[...]).astype(low)


def entry_kernel(index, owners, lengths, packed, logs, outer, weights, packed_grad, kept, sent, partial):
    tall = weights.shape[1] // 4
    if outer.shape[0] == tall:
        outer = outer[...].T
    row = row_of(owners, index)
    same = same_segment(lengths, row, packed.shape[1])
    turned = logs[index].T
    scale = HD ** (-0.5)
    packed_grad[:, :tall] = jnp.zeros((outer.shape[0], tall), low)
    for head in range(tall // HD):
        at = tall + head * HD
        queries = packed[index, :, at : at + HD]
        keys = packed[index, :, tall + at : tall + at + HD]
        values = packed[index, :, 2 * tall + at : 2 * tall + at + HD]
        outward = outer[:, head * HD : head * HD + HD]
        probs = jnp.exp(scores(keys, queries, same) - turned[head : head + 1])
        probs_grad = nt(values, outward)
        rows = jnp.sum(probs * probs_grad, axis=0, keepdims=True)
        score_grad = (probs * (probs_grad - rows)).astype(low)
        packed_grad[:, at : at + HD] = (tn(keys, score_grad) * scale).astype(low).T
        packed_grad[:, tall + at : tall + at + HD] = (nn(score_grad, queries) * scale).astype(low)
        packed_grad[:, 2 * tall + at : 2 * tall + at + HD] = nn(probs.astype(low), outward).astype(low)
    partial[...] = nt(packed_grad[...], weights[...])
    kept[...] = partial[half_of(owners, partial.shape[0])]
    sent[...] = partial[half_of(owners, partial.shape[0], True)].astype(low)


def gather_kernel(
    owners, lengths, packed, logs, outer, weights, inputs, packed_grad, mixer_grad, mixer_grad_far, sums,
    sums_far, *refs
):
    outs, kept, sent, held, other_grad, partial = refs[:-5], *refs[-5:]
    entry_kernel(1, owners, lengths, packed, logs, outer, weights, other_grad, kept, sent, partial)
    tall = weights.shape[1] // 4
    done = packed_grad.shape[1]
    own, other = row_of(owners, 0), row_of(owners, 1)
    held[:, :done] = (
        tn(inputs[own], packed_grad[...]) + tn(inputs[other], other_grad[...])
    ).astype(low)
    held[:, :tall] = (mixer_grad[...].astype(wide) + mixer_grad_far[...].T.astype(wide)).astype(low)
    extra = held.shape[1] - done
    total = sums[...] + sums_far[...]
    lines = jnp.concatenate([total, jnp.zeros((extra - total.shape[0], total.shape[1]), wide)], axis=0)
    held[:, done:] = lines.T.astype(low)
    deal(owners, held, outs, piece_order(sum(out.shape[0] for out in outs)))


def fold(value):
    rows, columns = value.shape
    total = jnp.zeros((8, 128), wide)
    for i in range(rows // 8):
        for j in range(columns // 128):
            tile = value[8 * i : 8 * i + 8, 128 * j : 128 * j + 128]
            total = total + tile * tile
    return total


def total_kernel(inner, piece, load, crossed, others, pair, squares):
    pair[...] = piece[0].astype(wide) + load[0].astype(wide) + crossed[1].astype(wide)
    count = pair.shape[1] - 128
    squares[...] = others[...] + fold(pair[:, :count]) + fold(pair[:, count:]) * (1.0 / inner)


def adam_kernel(*refs):
    owners, attend, expand, shrink, squares, half, rest = refs[:7]
    sources, norm, targets, placed = refs[7:22], refs[23], refs[24:43], refs[43]
    held, made, other, sems = refs[44:59], refs[59:78], refs[78], refs[79]
    arriving = [
        pltpu.make_async_copy(s, h, sems.at[i]) for i, (s, h) in enumerate(zip(sources, held))
    ]
    for copy in arriving:
        copy.start()
    count = half.shape[0]
    other[half_of(owners, 2 * count)] = half[...].astype(wide)
    other[half_of(owners, 2 * count, True)] = rest[...].astype(wide)
    leaving = [pltpu.make_async_copy(other, placed.at[row_of(owners, 1)], sems.at[34])]
    leaving[0].start()
    found = jnp.sqrt(jnp.sum(squares[...], keepdims=True))
    norm[...] = found
    factor = jnp.minimum(1.0, clip_bound / (found + 1e-06))
    tall = held[0].shape[2]
    done = 4 * tall
    rounded = (tall + 127) // 128 * 128
    grads = [
        jnp.stack([attend[:, c * tall : (c + 1) * tall] for c in range(1, 4)]),
        attend[:, :rounded].T[:tall],
        expand[...],
        shrink[...],
        attend[:, done:].T[: held[12].shape[0]],
    ]
    rates = [rate_matrix, rate_mixer, rate_matrix, rate_matrix, rate_vector]
    for i, (grad, rate) in enumerate(zip(grads, rates)):
        settle(arriving[3 * i : 3 * i + 3])
        master, moment, square = (ref[...] for ref in held[3 * i : 3 * i + 3])
        decay = decay_matrix if i < 4 else 0.0
        new = adam_update(grad, moment, square, master, factor, rate, decay)
        new = (*new, new[2].astype(low)) if i < 4 else new
        for j, value in enumerate(new):
            k = 4 * i + j
            made[k][...] = value
            leaving.append(pltpu.make_async_copy(made[k], targets[k], sems.at[15 + k]))
            leaving[-1].start()
    settle(leaving)


def place_kernel(owners, own, half, rest, result):
    row = row_of(owners, 1)
    result[row_of(owners, 0)] = own[...]
    result[row, half_of(owners, own.shape[0])] = half[...]
    result[row, half_of(owners, own.shape[0], True)] = rest[...]


def own_kernel(owners, half, rest, result, sems):
    row = row_of(owners, 0)
    copies = [
        pltpu.make_async_copy(
            ref, result.at[row, half_of(owners, 2 * ref.shape[0], i == 1)], sems.at[i]
        )
        for i, ref in enumerate((half, rest))
    ]
    for copy in copies:
        copy.start()
    settle(copies)


def in_hbm(array):
    return pltpu.with_memory_space_constraint(array, pltpu.HBM)


def call(kernel, outs, *args, groups=None, owners=None, lengths=None, scratch=(), name=None):
    specs = [pl.BlockSpec(memory_space=pltpu.VMEM)] * len(args)
    if lengths is not None:
        args = (lengths, *args)
        specs = [pl.BlockSpec(memory_space=pltpu.SMEM), *specs]
    if owners is not None and groups is None:
        args = (owners, *args)
        specs = [pl.BlockSpec(memory_space=pltpu.SMEM), *specs]
    if groups is not None:
        picks = [[(index, distance) for _, index, distance in group] for group in groups]
        blocks = [in_hbm(array) if name in ('attend', 'mixer') else array for group in groups for array, _, _ in group]
        inner = kernel
        kernel = lambda *refs: inner(picks, *refs)
        args = (owners, *args, *blocks)
        specs = [pl.BlockSpec(memory_space=pltpu.SMEM), *specs]
        specs += [pl.BlockSpec(memory_space=pl.ANY)] * len(blocks)
    return pl.pallas_call(
        kernel,
        out_shape=tuple(jax.ShapeDtypeStruct(out[0], out[1]) for out in outs),
        in_specs=specs,
        out_specs=tuple(
            pl.BlockSpec(memory_space=pl.ANY if len(out) > 2 else pltpu.VMEM) for out in outs
        ),
        scratch_shapes=scratch,
        compiler_params=pltpu.CompilerParams(vmem_limit_bytes=VMEM_LIMIT),
        name=name,
    )(*args)


def shards(
    block_input,
    segment_lengths,
    entry_master,
    mixer_master,
    expand_master,
    shrink_master,
    block_vectors,
    block_cotangent,
    entry_moment,
    entry_square,
    mixer_moment,
    mixer_square,
    expand_moment,
    expand_square,
    shrink_moment,
    shrink_square,
    vector_moment,
    vector_square,
):
    rows, length, width = block_input.shape
    members = lax.axis_size("dp")
    place = lax.axis_index("dp")
    spot = lax.axis_index("tensor")
    core = spot % 2
    plane = spot // 2
    share = width // members
    tall = entry_master.shape[2]
    heads = 2 * tall // HD
    hidden = expand_master.shape[1]
    ringed = members <= RING_LIMIT

    attend_shard = jnp.concatenate(
        [mixer_master.T, entry_master[0], entry_master[1], entry_master[2]], axis=1
    ).astype(low)
    feed_shard = jnp.concatenate([expand_master, shrink_master.T], axis=1).astype(low)

    def one_row(value):
        return lax.dynamic_index_in_dim(value, plane, 0, False)

    inputs = one_row(block_input)
    cotangent = one_row(block_cotangent)
    grid = (length, width)

    def mixer(blocks):
        rounded = (tall + 127) // 128 * 128
        return call(
            mixer_kernel, [((tall, width), low)], groups=[blocks], owners=owners, name="mixer",
            scratch=(
                pltpu.VMEM((width, rounded), low), pltpu.SemaphoreType.DMA((2 * len(blocks),))
            ),
        )[0]

    def attend(blocks, *gates):
        count = len(blocks)
        return call(
            attend_kernel,
            [
                ((2, length, 4 * tall), low),
                ((length, tall), low),
                ((tall, length), low),
                ((2, length, 128), wide),
                ((width, 4 * tall), low, "far"),
            ],
            after(block_input, *gates), groups=[blocks], owners=owners, lengths=segment_lengths, name="attend",
            scratch=(
                pltpu.VMEM((width, 4 * tall), low), pltpu.SemaphoreType.DMA((2 * count + 2,))
            ),
        )

    def mix(attended, attended_far, mixer_w, mixer_far, *gates):
        (mixed,) = call(
            mix_kernel, [(grid, low)], attended, after(attended_far, *gates), mixer_w, mixer_far, name="mix"
        )
        return mixed

    far = members // 2
    if ringed:
        owners = jnp.concatenate([owners_here(), core[None], plane[None]])
        attend_gather = Gather(attend_shard)
        feed_far = planes(feed_shard)
        for step in range(far):
            attend_gather.advance()
        mixer_w = mixer(attend_gather.blocks)
        packed, attended, attended_other, logs, attend_w = attend(attend_gather.blocks, mixer_w)
        feed_pair = jnp.concatenate([feed_shard, feed_far], axis=1)
        feed_gather = Twin(after(feed_pair, attend_gather.loads[1]))
        M, T = feed_gather.mine, feed_gather.theirs
        mixer_far = planes(mixer_w)
        attended_far = planes(after(attended_other, mixer_far))
        for step in range(far):
            feed_gather.advance(*({1: lambda: (*attend_gather.loads[3:], T[1]), 2: lambda: (T[2], attended), 3: lambda: (attended_far, mixer_far)}).get(step, tuple)())
            if step + 1 < far:
                feed_gather.follow(*({1: lambda: M[1:2], 2: lambda: M[2:3]}).get(step, tuple)())
            if step == far - 2:
                mixed = mix(attended, attended_far, mixer_w, mixer_far)
        feed_blocks = feed_gather.blocks
    else:
        owners = jnp.stack([jnp.zeros((), jnp.int32), core, plane])
        whole = lax.all_gather(attend_shard, "dp", axis=0, tiled=True)
        mixer_w = mixer([(whole, (), 0)])
        packed, attended, attended_other, logs, attend_w = attend([(whole, (), 0)])
        attended_far, mixer_far = planes(attended_other), planes(mixer_w)
        mixed = mix(attended, attended_far, mixer_w, mixer_far)
        whole = lax.all_gather(feed_shard, "dp", axis=0, tiled=True)
        feed_blocks = [(jnp.concatenate([whole, planes(whole)], axis=1), (), 0)]
    many = len(feed_blocks)

    mixed_other = cores(mixed)
    first_unit, first_scale, active, slope, shrunk, expand_w, shrink_w = call(
        feed_kernel,
        [
            (grid, wide),
            ((length, 128), wide),
            ((2, length, hidden), low),
            ((2, length, hidden), low),
            (grid, low),
            ((2, width, hidden), low, "far"),
            ((2, width, hidden), low, "far"),
        ],
        inputs, mixed, mixed_other, block_vectors,
        groups=[feed_blocks], owners=owners, name="feed",
        scratch=(
            pltpu.VMEM((2, width, hidden), low),
            pltpu.VMEM((2, width, hidden), low),
            pltpu.SemaphoreType.DMA((8 * many + 8,)),
        ),
    )
    shrunk_other = cores(shrunk)
    half = (length // 2, width)
    output, output_half, second_grad, second_low, second_sums = call(
        second_kernel,
        [(grid, low), (half, low), (grid, wide), (grid, low), ((8, width), wide)],
        first_unit, shrunk, shrunk_other, block_vectors, cotangent,
        owners=owners, name="second",
    )

    def pieces_of(columns, counts):
        return [((count, share if ringed else width, columns), low) for count in counts]

    singles = [1] * members if ringed else [1]

    def paired(pieces):
        middle = [tuple(pieces[i : i + 2]) for i in range(1, len(pieces) - 1, 2)]
        return [pieces[0], *middle, pieces[-1]]

    def swap(value):
        return planes(value.astype(low)).astype(wide)

    hidden_grad, partial = call(
        expand_kernel,
        [((2, length, hidden), low), (grid, wide)],
        second_low, slope, expand_w, shrink_w,
        name="expand",
    )
    partial_other = cores(partial)
    feed_pieces = call(
        weights_kernel,
        pieces_of(4 * hidden, singles),
        second_low, active, after(hidden_grad, partial), first_unit, block_vectors,
        owners=owners, scratch=(pltpu.VMEM((width, 4 * hidden), low),), name="weights",
    )
    feed_pieces = TwinPieces(paired(feed_pieces))
    partial_other = after(partial_other, feed_pieces.mine)
    first_half, sums, mixer_grad, mixer_grad_other, attended_grad, attended_grad_other = call(
        first_kernel,
        [
            (half, wide),
            ((8, width), wide),
            ((width, tall), low),
            ((tall, width), low),
            ((length, tall), low),
            ((tall, length), low),
        ],
        second_grad, partial, partial_other, first_unit, first_scale, block_vectors, attended, attended_far,
        second_sums, mixer_w, mixer_far, owners=owners, name="first", scratch=(pltpu.VMEM(grid, wide),),
    )

    def scattered(value):
        return lax.psum_scatter(value[0].astype(wide), "dp", scatter_dimension=0, tiled=True)

    attended_grad_far = planes(attended_grad_other)
    mixer_grad_far = planes(after(mixer_grad_other, attended_grad_far))
    sums_far = planes(after(sums, attended_grad_far))
    halves = [(half, wide), (half, low)]
    packed_grad, kept_own, sent_own = call(
        lambda *refs: entry_kernel(0, *refs),
        [((length, 4 * tall), low), *halves],
        packed, logs, after(attended_grad, attended_grad_far), attend_w,
        owners=owners, lengths=segment_lengths, name="entry", scratch=(pltpu.VMEM(grid, wide),),
    )
    if ringed:
        feed_pieces.advance(packed_grad, mixer_grad_far)
        feed_pieces.follow(packed_grad)
    columns = 4 * tall + 128
    *pieces, kept_other, sent_other = call(
        gather_kernel,
        [*pieces_of(columns, singles), *halves],
        packed, logs, after(attended_grad_far, packed_grad), attend_w, block_input,
        packed_grad, mixer_grad, mixer_grad_far, sums, sums_far, owners=owners, lengths=segment_lengths, name="gather",
        scratch=(
            pltpu.VMEM((width, columns), low),
            pltpu.VMEM((length, 4 * tall), low),
            pltpu.VMEM(grid, wide),
        ),
    )
    attend_pieces = Pieces(paired(pieces))
    output_half = planes(after(output_half, mixer_grad_far, sums_far))
    other_half = planes((kept_other + cores(sent_other).astype(wide)).astype(low))
    own_half = first_half + kept_own + cores(sent_own).astype(wide) + other_half.astype(wide)
    if ringed:
        feed_pieces.advance(attend_pieces.payload)
        feed_pieces.follow(attend_pieces.payload)
        fourth = feed_pieces.advance()
        others = feed_pieces.follow()
        attend_pieces.advance(fourth)
        third = attend_pieces.advance()
        feed_pieces.mine = after(feed_pieces.mine, others, third)
        feed_pair = feed_pieces.advance(output_half)
        attend_pieces.advance(other_half)
    else:
        feed_pair = scattered(feed_pieces.mine[None])
    (block_output,) = call(
        place_kernel, [((2, *grid), low)], output, output_half, cores(output_half), owners=owners, name="place"
    )
    (input_gradient,) = call(
        own_kernel,
        [((2, *grid), wide, "far")],
        own_half, cores(own_half), owners=owners, name="own", scratch=(pltpu.SemaphoreType.DMA((2,)),),
    )
    parts = [feed_pair[:, i * hidden : (i + 1) * hidden] for i in range(4)]
    feed_other = swap(jnp.concatenate([parts[1], parts[3]], axis=1))
    shrink_share = parts[0] + feed_other[:, :hidden]
    expand_share = parts[2] + feed_other[:, hidden:]
    other_squares = jnp.sum(shrink_share * shrink_share) + jnp.sum(expand_share * expand_share)
    if ringed:
        attend_pair = attend_pieces.advance(other_squares, block_output)
    else:
        attend_pair = scattered(pieces[0])
    inner = lax.axis_size("tensor")

    def near(squares):
        squares = squares + cores(squares)
        return squares + planes(squares)

    def reduced(squares):
        hop = 1
        while hop < members:
            squares = squares + lax.ppermute(squares, "dp", [(i, i ^ hop) for i in range(members)])
            hop *= 2
        return squares

    vector_width = width // members
    vector_master = lax.dynamic_slice_in_dim(block_vectors, place * vector_width, vector_width, 1)
    if ringed:
        others = jnp.where(lax.broadcasted_iota(jnp.int32, (8, 128), 1) == 0, other_squares / 8, 0.0)
        attend_pair, squares = call(
            lambda *refs: total_kernel(inner, *refs),
            [((share, columns), wide), ((8, 128), wide)],
            *attend_pair, others, name="total",
        )
        squares = near(squares)
        input_far = planes(after(own_half.astype(low), squares))
        squares = reduced(squares)
        input_far = after(input_far, squares)
        groups = [
            (entry_master, entry_moment, entry_square),
            (mixer_master, mixer_moment, mixer_square),
            (expand_master, expand_moment, expand_square),
            (shrink_master.T, shrink_moment.T, shrink_square.T),
            (vector_master, vector_moment, vector_square),
        ]
        sources = [array for group in groups for array in group]
        targets = []
        for i, group in enumerate(groups):
            targets += [(group[0].shape, wide)] * 3 + [(group[0].shape, low)] * (i < 4)
        in_place = pl.BlockSpec(memory_space=pltpu.HBM)
        held = pl.BlockSpec(memory_space=pltpu.VMEM)
        *rest, input_gradient = pl.pallas_call(
            adam_kernel,
            out_shape=[
                jax.ShapeDtypeStruct(shape, kind)
                for shape, kind in [((1, 1), wide), *targets, ((2, *grid), wide)]
            ],
            in_specs=[pl.BlockSpec(memory_space=pltpu.SMEM)] + [held] * 6 + [in_place] * 16,
            out_specs=[held] + [in_place] * 20,
            scratch_shapes=[
                *[pltpu.VMEM(array.shape, wide) for array in sources],
                *[pltpu.VMEM(shape, kind) for shape, kind in targets],
                pltpu.VMEM(grid, wide),
                pltpu.SemaphoreType.DMA((35,)),
            ],
            input_output_aliases={22: 20},
            compiler_params=pltpu.CompilerParams(vmem_limit_bytes=VMEM_LIMIT),
            name="adam",
        )(
            owners, attend_pair, expand_share, shrink_share, squares, input_far, cores(input_far),
            *map(in_hbm, sources), input_gradient,
        )
        norm, *news = rest
        news[12:16] = [array.T for array in news[12:16]]
        return (block_output, input_gradient, norm[0, 0], *news)

    attend_share = attend_pair[:, : 4 * tall]
    vector_sum = attend_pair[:, 4 * tall :]
    entry_share = jnp.stack([attend_share[:, c * tall : (c + 1) * tall] for c in range(1, 4)])
    mixer_share = attend_share[:, :tall].T
    vector_share = vector_sum[:, :6].T
    squares = other_squares + jnp.sum(attend_share * attend_share)
    squares = squares + jnp.sum(vector_share * vector_share) / inner
    squares = near(jnp.full((8, 128), squares))
    squares = reduced(squares)
    other = planes(own_half.astype(low))
    other, rest = other.astype(wide), cores(other).astype(wide)
    other = jnp.concatenate([jnp.where(core == 0, other, rest), jnp.where(core == 0, rest, other)], axis=0)
    input_gradient = lax.dynamic_update_index_in_dim(input_gradient, other, 1 - plane, 0)
    gradient_norm = jnp.sqrt(squares[0, 0])
    factor = jnp.minimum(1.0, clip_bound / (gradient_norm + 1e-06))
    results = []
    for grad, moment, square, master, rate in (
        (entry_share, entry_moment, entry_square, entry_master, rate_matrix),
        (mixer_share, mixer_moment, mixer_square, mixer_master, rate_mixer),
        (expand_share, expand_moment, expand_square, expand_master, rate_matrix),
        (shrink_share.T, shrink_moment, shrink_square, shrink_master, rate_matrix),
    ):
        new = adam_update(grad, moment, square, master, factor, rate, decay_matrix)
        results += [*new, new[2].astype(low)]
    results += adam_update(
        vector_share, vector_moment, vector_square, vector_master, factor, rate_vector, 0.0
    )
    return (block_output, input_gradient, gradient_norm, *results)


def solution(mesh):
    in_specs = (
        P("dp", None, None),
        P("dp", None),
        P(None, "dp", "tensor"),
        P("tensor", "dp"),
        P("dp", "tensor"),
        P("tensor", "dp"),
        P(),
        P("dp", None, None),
        P(None, "dp", "tensor"),
        P(None, "dp", "tensor"),
        P("tensor", "dp"),
        P("tensor", "dp"),
        P("dp", "tensor"),
        P("dp", "tensor"),
        P("tensor", "dp"),
        P("tensor", "dp"),
        P(None, "dp"),
        P(None, "dp"),
    )
    out_specs = (
        P("dp", None, None),
        P("dp", None, None),
        P(),
        P(None, "dp", "tensor"),
        P(None, "dp", "tensor"),
        P(None, "dp", "tensor"),
        P(None, "dp", "tensor"),
        P("tensor", "dp"),
        P("tensor", "dp"),
        P("tensor", "dp"),
        P("tensor", "dp"),
        P("dp", "tensor"),
        P("dp", "tensor"),
        P("dp", "tensor"),
        P("dp", "tensor"),
        P("tensor", "dp"),
        P("tensor", "dp"),
        P("tensor", "dp"),
        P("tensor", "dp"),
        P(None, "dp"),
        P(None, "dp"),
        P(None, "dp"),
    )
    return jax.shard_map(shards, mesh=mesh, in_specs=in_specs, out_specs=out_specs, check_vma=False)
```

```python
import math

import jax
import jax.numpy as jnp
from jax import lax
from jax.experimental import pallas as pl
from jax.experimental.pallas import tpu as pltpu
from jax.sharding import PartitionSpec as P

HD = 64
ADAM_STEP = 3


norm_eps = 1e-12
clip_bound = 1.0
beta_first = 0.5
beta_second = 0.6
adam_eps = 1e-08
rate_matrix = 0.02
rate_mixer = 0.08
rate_vector = 0.25
decay_matrix = 0.01


low = jnp.bfloat16
wide = jnp.float32
RING_LIMIT = 16
VMEM_LIMIT = 24 * 2**20


def adam_update(grad, moment, square, master, factor, rate, decay):
    clipped = grad * factor
    moment_new = beta_first * moment + (1.0 - beta_first) * clipped
    square_new = beta_second * square + (1.0 - beta_second) * clipped * clipped
    corrected = moment_new / (1.0 - beta_first**ADAM_STEP)
    scaled = square_new / (1.0 - beta_second**ADAM_STEP)
    master_new = master - rate * (corrected / (jnp.sqrt(scaled) + adam_eps) + decay * master)
    return (moment_new, square_new, master_new)


def cores(value):
    size = lax.axis_size("tensor")
    return lax.ppermute(value, "tensor", [(i, i ^ 1) for i in range(size)])


def planes(value):
    size = lax.axis_size("tensor")
    return lax.ppermute(value, "tensor", [(i, i ^ 2) for i in range(size)])


def ring_order(size):
    return list(range(0, size, 2)) + list(range(size - 1, 0, -2))


def owners_here():
    size = lax.axis_size("dp")
    place = lax.axis_index("dp")
    seat = jnp.where(place % 2 == 0, place // 2, size - 1 - place // 2)
    sign = 1 - 2 * (lax.axis_index("tensor") % 2)
    spots = (seat + sign * jnp.arange(size, dtype=jnp.int32) + size) % size
    return jnp.where(spots < size // 2, 2 * spots, 2 * size - 1 - 2 * spots)


def after(value, *earlier):
    if not earlier:
        return value
    return lax.optimization_barrier((value, *earlier))[0]


def turn(value):
    size, inner = lax.axis_size("dp"), lax.axis_size("tensor")
    ring = ring_order(size)
    pairs = []
    for i in range(size):
        for t in range(inner):
            step = 1 if t % 2 == 0 else -1
            pairs.append((ring[i] * inner + t, ring[(i + step) % size] * inner + t))
    return lax.ppermute(value, ("dp", "tensor"), pairs)


def pair(value):
    return jnp.stack([value, cores(value)])


class Gather:
    def __init__(self, shard, load=None):
        self.size = lax.axis_size("dp")
        self.step = 0
        self.load = pair(shard) if load is None else load
        self.blocks = [(shard, (), 0)]
        self.loads = []

    def advance(self, *gates):
        self.step += 1
        if self.step == self.size // 2:
            self.load = turn(after(self.load[0], *gates))
            self.blocks.append((self.load, (), self.step))
        else:
            self.load = turn(after(self.load, *gates))
            self.take(self.load)
        self.loads.append(self.load)
        return self.load

    def take(self, load):
        self.blocks += [(load, (0,), self.size - self.step), (cores(load), (1,), self.step)]


def piece_order(size):
    far = size // 2
    order = [far] if far else []
    for step in range(far - 1, 0, -1):
        order += [step, size - step]
    return [*order, 0]


class TwinPieces:
    def __init__(self, pieces):
        self.near = [piece[0][0] if isinstance(piece, tuple) else piece[0] for piece in pieces]
        self.mine = self.theirs = self.near[0]
        self.step = 0
        if len(pieces) > 2:
            self.away = [cores(piece[1][0]) for piece in pieces[1:-1]]
            self.theirs = self.away[0]
            self.turns = 0

    def advance(self, *gates):
        self.step += 1
        load = after(turn(self.mine), *gates).astype(wide)
        if self.step == len(self.near) - 1:
            return self.near[-1].astype(wide) + load + cores(self.theirs).astype(wide)
        self.mine = (load + self.near[self.step].astype(wide)).astype(low)
        return self.mine

    def follow(self, *gates):
        self.turns += 1
        self.theirs = after(turn(self.theirs), *gates)
        if self.turns < len(self.away):
            self.theirs = (self.theirs.astype(wide) + self.away[self.turns].astype(wide)).astype(low)
        return self.theirs


class Pieces:
    def __init__(self, pieces):
        self.pieces = pieces
        self.step = 0
        self.payload = pieces[0][0]

    def advance(self, *gates):
        self.step += 1
        load = after(turn(self.payload), *gates)
        piece = self.pieces[self.step]
        if not isinstance(piece, tuple):
            return piece, load, cores(load)
        theirs = cores(piece[1])
        if self.step == 1:
            mine = (load.astype(wide) + piece[0][0].astype(wide)).astype(low)
            self.payload = jnp.concatenate([mine[None], theirs], axis=0)
        else:
            both = jnp.concatenate([piece[0], theirs], axis=0).astype(wide)
            self.payload = (load.astype(wide) + both).astype(low)
        return self.payload


class Twin:
    def __init__(self, shard):
        self.size = lax.axis_size("dp")
        self.step = 0
        self.mine, self.theirs = [shard], [cores(shard)]
        self.blocks = [(shard, (), 0)]

    def advance(self, *gates):
        self.step += 1
        self.mine.append(turn(after(self.mine[-1], *gates)))
        self.blocks.append((self.mine[-1], (), (self.size - self.step) % self.size))

    def follow(self, *gates):
        self.theirs.append(turn(after(self.theirs[-1], *gates)))
        self.blocks.append((cores(self.theirs[-1]), (), self.step))


class TwinPieces:
    def __init__(self, pieces):
        self.near = [piece[0][0] if isinstance(piece, tuple) else piece[0] for piece in pieces]
        self.mine = self.theirs = self.near[0]
        self.step = 0
        if len(pieces) > 2:
            self.away = [cores(piece[1][0]) for piece in pieces[1:-1]]
            self.theirs = self.away[0]
            self.turns = 0

    def advance(self, *gates):
        self.step += 1
        load = after(turn(self.mine), *gates).astype(wide)
        if self.step == len(self.near) - 1:
            return self.near[-1].astype(wide) + load + cores(self.theirs).astype(wide)
        self.mine = (load + self.near[self.step].astype(wide)).astype(low)
        return self.mine

    def follow(self, *gates):
        self.turns += 1
        self.theirs = after(turn(self.theirs), *gates)
        if self.turns < len(self.away):
            self.theirs = (self.theirs.astype(wide) + self.away[self.turns].astype(wide)).astype(low)
        return self.theirs


class Pieces:
    def __init__(self, pieces):
        self.pieces = pieces
        self.step = 0
        self.payload = pieces[0][0]

    def advance(self, *gates):
        self.step += 1
        load = after(turn(self.payload), *gates)
        piece = self.pieces[self.step]
        if not isinstance(piece, tuple):
            return piece, load, cores(load)
        theirs = cores(piece[1])
        if self.step == 1:
            mine = (load.astype(wide) + piece[0][0].astype(wide)).astype(low)
            self.payload = jnp.concatenate([mine[None], theirs], axis=0)
        else:
            both = jnp.concatenate([piece[0], theirs], axis=0).astype(wide)
            self.payload = (load.astype(wide) + both).astype(low)
        return self.payload


class Twin:
    def __init__(self, shard):
        self.size = lax.axis_size("dp")
        self.step = 0
        self.mine, self.theirs = [shard], [cores(shard)]
        self.blocks = [(shard, (), 0)]

    def advance(self, *gates):
        self.step += 1
        self.mine.append(turn(after(self.mine[-1], *gates)))
        self.blocks.append((self.mine[-1], (), (self.size - self.step) % self.size))

    def follow(self, *gates):
        self.theirs.append(turn(after(self.theirs[-1], *gates)))
        self.blocks.append((cores(self.theirs[-1]), (), self.step))


class Forward:
    def __init__(self, shard):
        self.size = lax.axis_size("dp")
        self.loads = [planes(shard)]
        self.blocks = [(self.loads[0], (), 0)]
        self.step = 0

    def take(self, load):
        self.step += 1
        load = planes(load)
        self.loads.append(load)
        if self.step == self.size // 2:
            self.blocks.append((load, (), self.step))
        else:
            self.blocks += [(load, (0,), self.size - self.step), (cores(load), (1,), self.step)]


def deal(owners, held, outs, distances):
    distances = list(distances)
    for out in outs:
        for i in range(out.shape[0]):
            count = out.shape[1]
            start = owners[distances.pop(0)] * count
            if count % 16 == 0:
                start = pl.multiple_of(start, 16)
            out[i] = held[pl.ds(start, count)]


def nn(left, right):
    return lax.dot_general(left, right, (((1,), (0,)), ((), ())), preferred_element_type=wide)


def nt(left, right):
    return lax.dot_general(left, right, (((1,), (1,)), ((), ())), preferred_element_type=wide)


def tn(left, right):
    return lax.dot_general(left, right, (((0,), (0,)), ((), ())), preferred_element_type=wide)


def fetch(picks, owners, blocks, first, target, sems, base):
    copies = []
    split = target.shape[1] // 2
    for i, (index, distance) in enumerate(picks):
        block = blocks[i]
        tall = block.shape[-2]
        start = owners[distance] * tall
        if tall % 16 == 0:
            start = pl.multiple_of(start, 16)
        for at in (0, split):
            source = block.at[(*index, slice(None), slice(first + at, first + at + split))]
            goal = target.at[pl.ds(start, tall), at : at + split]
            copies.append(
                pltpu.make_async_copy(source, goal, sems.at[base + 2 * i + at // split])
            )
    for copy in copies:
        copy.start()
    return copies


def keep(weights, target, sems, first):
    split = weights.shape[1] // 2
    copies = []
    for i in range(2):
        part = (slice(None), slice(i * split, (i + 1) * split))
        copies.append(pltpu.make_async_copy(weights.at[part], target.at[part], sems.at[first + i]))
    for copy in copies:
        copy.start()
    return copies


def settle(copies):
    for copy in copies:
        copy.wait()


def whole_mean(value):
    return jnp.mean(value, axis=-1, keepdims=True)


def scores(queries, keys, same):
    return jnp.where(same, nt(queries, keys) * HD ** (-0.5), -1e30)


def half_of(owners, size, other=False):
    which = owners[owners.shape[0] - 2]
    which = 1 - which if other else which
    return pl.ds(pl.multiple_of(which * (size // 2), 16), size // 2)


def row_of(owners, index):
    return jnp.abs(owners[owners.shape[0] - 1] - index)


def same_segment(lengths, row, size):
    column = jnp.zeros((size, 1), jnp.int32)
    line = jnp.zeros((1, size), jnp.int32)
    end = 0
    for k in range(lengths.shape[1]):
        end = end + lengths[row, k]
        column += (lax.broadcasted_iota(jnp.int32, (size, 1), 0) >= end).astype(jnp.int32)
        line += (lax.broadcasted_iota(jnp.int32, (1, size), 1) >= end).astype(jnp.int32)
    return column == line


def pack_kernel(entry, mixer, packed):
    tall = entry.shape[2]
    packed[:, :tall] = mixer[...].T.astype(low)
    for c in range(3):
        packed[:, (c + 1) * tall : (c + 2) * tall] = entry[c].astype(low)


def join_kernel(expand, shrink, joined):
    count = expand.shape[1]
    joined[:, :count] = expand[...].astype(low)
    joined[:, count:] = shrink[...].astype(low)


def mixer_kernel(picks, owners, *refs):
    many = len(picks[0])
    mixer_w, weights, sems = refs[many:]
    settle(fetch(picks[0], owners, refs[:many], 0, weights, sems, 0))
    mixer_w[...] = weights[:, : mixer_w.shape[0]].T


def attend_kernel(picks, owners, lengths, inputs, *refs):
    many = len(picks[0])
    packed, attended, attended_other, logs, kept, weights, sems = refs[many:]
    copies = fetch(picks[0], owners, refs[:many], 0, weights, sems, 0)
    tall = weights.shape[1] // 4
    logs[...] = jnp.zeros_like(logs)
    settle(copies)
    leaving = keep(weights, kept, sems, 2 * many)
    for index, goal in ((1, attended_other), (0, attended)):
        row = row_of(owners, index)
        same = same_segment(lengths, row, inputs.shape[1])
        packed[index] = nn(inputs[row], weights[...]).astype(low)
        for head in range(tall // HD):
            at = tall + head * HD
            raw = scores(
                packed[index, :, at : at + HD], packed[index, :, tall + at : tall + at + HD], same
            )
            peak = jnp.max(raw, axis=-1, keepdims=True)
            grown = jnp.exp(raw - peak)
            mass = jnp.sum(grown, axis=-1, keepdims=True)
            logs[index, :, head : head + 1] = peak + jnp.log(mass)
            probs = (grown * (1.0 / mass)).astype(low)
            result = nn(probs, packed[index, :, 2 * tall + at : 2 * tall + at + HD])
            if index:
                goal[head * HD : head * HD + HD] = result.T.astype(low)
            else:
                goal[:, head * HD : head * HD + HD] = result.astype(low)
    settle(leaving)


def mix_kernel(attended, attended_far, mixer_w, mixer_far, mixed):
    mixed[...] = (nn(attended[...], mixer_w[...]) + tn(attended_far[...], mixer_far[...])).astype(low)


def feed_kernel(picks, owners, inputs, mixed, mixed_other, vectors, *refs):
    many = len(picks[0])
    first_unit, first_scale, active, slope, shrunk, expand_kept, shrink_kept, expand_w, shrink_w, sems = refs[many:]
    hidden = expand_w.shape[2]
    copies = [
        fetch(picks[0], owners, refs[:many], p * hidden, (expand_w, shrink_w)[p % 2].at[p // 2], sems, 2 * many * p)
        for p in range(4)
    ]
    leaving = []
    value = inputs[...].astype(wide) + (mixed[...].astype(wide) + mixed_other[...].astype(wide)) + vectors[0:1]
    centered = value - whole_mean(value)
    scale = lax.rsqrt(whole_mean(centered * centered) + norm_eps)
    unit = centered * scale
    first_unit[...] = unit
    first_scale[...] = jnp.broadcast_to(scale, first_scale.shape)
    rounded = (unit * vectors[2:3] + vectors[3:4]).astype(low)
    total = None
    for half in range(2):
        settle(copies[2 * half])
        leaving += keep(expand_w.at[half], expand_kept.at[half], sems, 8 * many + 4 * half)
        value = nn(rounded, expand_w[half])
        spread = 0.5 * (1.0 + lax.erf(value * math.sqrt(0.5)))
        result = (value * spread).astype(low)
        active[half] = result
        bell = jnp.exp(-0.5 * value * value) * (1.0 / math.sqrt(2.0 * math.pi))
        slope[half] = (spread + value * bell).astype(slope.dtype)
        settle(copies[2 * half + 1])
        leaving += keep(shrink_w.at[half], shrink_kept.at[half], sems, 8 * many + 4 * half + 2)
        term = nt(result, shrink_w[half])
        total = term if total is None else total + term
    shrunk[...] = total.astype(shrunk.dtype)
    settle(leaving)


def sum_rows(value):
    return jnp.sum(value, axis=0, keepdims=True)


def norm_back(unit, scale, gain, grad):
    scaled = grad * gain
    back = scaled - whole_mean(scaled) - unit * whole_mean(scaled * unit)
    return back * scale


def second_kernel(
    owners, first_unit, shrunk, shrunk_other, vectors, cotangent, output, output_half, grad, grad_low, sums
):
    normed = first_unit[...] * vectors[2:3] + vectors[3:4]
    value = normed + (shrunk[...].astype(wide) + shrunk_other[...].astype(wide)) + vectors[1:2]
    centered = value - whole_mean(value)
    scale = lax.rsqrt(whole_mean(centered * centered) + norm_eps)
    unit = centered * scale
    output[...] = (unit * vectors[4:5] + vectors[5:6]).astype(low)
    output_half[...] = output[half_of(owners, output.shape[0])]
    incoming = cotangent[...].astype(wide)
    back = norm_back(unit, scale, vectors[4:5], incoming)
    grad[...] = back
    grad_low[...] = back.astype(low)
    sums[...] = jnp.zeros_like(sums)
    sums[1:2] = sum_rows(back)
    sums[4:5] = sum_rows(incoming * unit)
    sums[5:6] = sum_rows(incoming)


def expand_kernel(grad_low, slope, expand_w, shrink_w, hidden_grad, partial):
    total = None
    for half in range(2):
        grad = nn(grad_low[...], shrink_w[half])
        rounded = (grad * slope[half].astype(wide)).astype(low)
        hidden_grad[half] = rounded
        term = nt(rounded, expand_w[half])
        total = term if total is None else total + term
    partial[...] = total


def weights_kernel(owners, grad_low, active, hidden_grad, first_unit, vectors, *refs):
    outs, held = refs[:-1], refs[-1]
    normed = (first_unit[...] * vectors[2:3] + vectors[3:4]).astype(low)
    hidden = active.shape[2]
    for half in range(2):
        at = half * hidden
        held[:, at : at + hidden] = tn(grad_low[...], active[half]).astype(low)
        at += 2 * hidden
        held[:, at : at + hidden] = tn(normed, hidden_grad[half]).astype(low)
    deal(owners, held, outs, piece_order(sum(out.shape[0] for out in outs)))


def first_kernel(
    owners, grad, partial, partial_other, first_unit, first_scale, vectors, attended, attended_far, second_sums,
    mixer_w, mixer_far, first_half, sums, mixer_grad, mixer_grad_far, attended_grad, attended_grad_far, held
):
    incoming = grad[...] + (partial[...] + partial_other[...])
    unit = first_unit[...]
    back = norm_back(unit, first_scale[:, 0:1], vectors[2:3], incoming)
    held[...] = back
    first_half[...] = held[half_of(owners, held.shape[0])]
    sums[...] = second_sums[...]
    sums[0:1] = sum_rows(back)
    sums[2:3] = sum_rows(incoming * unit)
    sums[3:4] = sum_rows(incoming)
    rounded = back.astype(low)
    attended_grad_far[...] = nt(mixer_far[...], rounded).astype(low)
    attended_grad[...] = nt(rounded, mixer_w[...]).astype(low)
    mixer_grad_far[...] = nn(attended_far[...], rounded).astype(low)
    mixer_grad[...] = tn(rounded, attended[...]).astype(low)


def entry_kernel(index, owners, lengths, packed, logs, outer, weights, packed_grad, kept, sent, partial):
    tall = weights.shape[1] // 4
    if outer.shape[0] == tall:
        outer = outer[...].T
    row = row_of(owners, index)
    same = same_segment(lengths, row, packed.shape[1])
    turned = logs[index].T
    scale = HD ** (-0.5)
    packed_grad[:, :tall] = jnp.zeros((outer.shape[0], tall), low)
    for head in range(tall // HD):
        at = tall + head * HD
        queries = packed[index, :, at : at + HD]
        keys = packed[index, :, tall + at : tall + at + HD]
        values = packed[index, :, 2 * tall + at : 2 * tall + at + HD]
        outward = outer[:, head * HD : head * HD + HD]
        probs = jnp.exp(scores(keys, queries, same) - turned[head : head + 1])
        probs_grad = nt(values, outward)
        rows = jnp.sum(probs * probs_grad, axis=0, keepdims=True)
        score_grad = (probs * (probs_grad - rows)).astype(low)
        packed_grad[:, at : at + HD] = (tn(keys, score_grad) * scale).astype(low).T
        packed_grad[:, tall + at : tall + at + HD] = (nn(score_grad, queries) * scale).astype(low)
        packed_grad[:, 2 * tall + at : 2 * tall + at + HD] = nn(probs.astype(low), outward).astype(low)
    partial[...] = nt(packed_grad[...], weights[...])
    kept[...] = partial[half_of(owners, partial.shape[0])]
    sent[...] = partial[half_of(owners, partial.shape[0], True)].astype(low)


def gather_kernel(
    owners, lengths, packed, logs, outer, weights, inputs, packed_grad, mixer_grad, mixer_grad_far, sums,
    sums_far, *refs
):
    outs, kept, sent, held, other_grad, partial = refs[:-5], *refs[-5:]
    entry_kernel(1, owners, lengths, packed, logs, outer, weights, other_grad, kept, sent, partial)
    tall = weights.shape[1] // 4
    done = packed_grad.shape[1]
    own, other = row_of(owners, 0), row_of(owners, 1)
    held[:, :done] = (
        tn(inputs[own], packed_grad[...]) + tn(inputs[other], other_grad[...])
    ).astype(low)
    held[:, :tall] = (mixer_grad[...].astype(wide) + mixer_grad_far[...].T.astype(wide)).astype(low)
    extra = held.shape[1] - done
    total = sums[...] + sums_far[...]
    lines = jnp.concatenate([total, jnp.zeros((extra - total.shape[0], total.shape[1]), wide)], axis=0)
    held[:, done:] = lines.T.astype(low)
    deal(owners, held, outs, piece_order(sum(out.shape[0] for out in outs)))


def fold(value):
    rows, columns = value.shape
    total = jnp.zeros((8, 128), wide)
    for i in range(rows // 8):
        for j in range(columns // 128):
            tile = value[8 * i : 8 * i + 8, 128 * j : 128 * j + 128]
            total = total + tile * tile
    return total


def total_kernel(inner, piece, load, crossed, others, pair, squares):
    pair[...] = piece[0].astype(wide) + load[0].astype(wide) + crossed[1].astype(wide)
    count = pair.shape[1] - 128
    squares[...] = others[...] + fold(pair[:, :count]) + fold(pair[:, count:]) * (1.0 / inner)


def adam_kernel(*refs):
    owners, attend, expand, shrink, squares, half, rest = refs[:7]
    sources, norm, targets, placed = refs[7:22], refs[23], refs[24:43], refs[43]
    held, made, other, sems = refs[44:59], refs[59:78], refs[78], refs[79]
    arriving = [
        pltpu.make_async_copy(s, h, sems.at[i]) for i, (s, h) in enumerate(zip(sources, held))
    ]
    for copy in arriving:
        copy.start()
    count = half.shape[0]
    other[half_of(owners, 2 * count)] = half[...].astype(wide)
    other[half_of(owners, 2 * count, True)] = rest[...].astype(wide)
    leaving = [pltpu.make_async_copy(other, placed.at[row_of(owners, 1)], sems.at[34])]
    leaving[0].start()
    found = jnp.sqrt(jnp.sum(squares[...], keepdims=True))
    norm[...] = found
    factor = jnp.minimum(1.0, clip_bound / (found + 1e-06))
    tall = held[0].shape[2]
    done = 4 * tall
    rounded = (tall + 127) // 128 * 128
    grads = [
        jnp.stack([attend[:, c * tall : (c + 1) * tall] for c in range(1, 4)]),
        attend[:, :rounded].T[:tall],
        expand[...],
        shrink[...],
        attend[:, done:].T[: held[12].shape[0]],
    ]
    rates = [rate_matrix, rate_mixer, rate_matrix, rate_matrix, rate_vector]
    for i, (grad, rate) in enumerate(zip(grads, rates)):
        settle(arriving[3 * i : 3 * i + 3])
        master, moment, square = (ref[...] for ref in held[3 * i : 3 * i + 3])
        decay = decay_matrix if i < 4 else 0.0
        new = adam_update(grad, moment, square, master, factor, rate, decay)
        new = (*new, new[2].astype(low)) if i < 4 else new
        for j, value in enumerate(new):
            k = 4 * i + j
            made[k][...] = value
            leaving.append(pltpu.make_async_copy(made[k], targets[k], sems.at[15 + k]))
            leaving[-1].start()
    settle(leaving)


def place_kernel(owners, own, half, rest, result):
    row = row_of(owners, 1)
    result[row_of(owners, 0)] = own[...]
    result[row, half_of(owners, own.shape[0])] = half[...]
    result[row, half_of(owners, own.shape[0], True)] = rest[...]


def own_kernel(owners, half, rest, result, sems):
    row = row_of(owners, 0)
    copies = [
        pltpu.make_async_copy(
            ref, result.at[row, half_of(owners, 2 * ref.shape[0], i == 1)], sems.at[i]
        )
        for i, ref in enumerate((half, rest))
    ]
    for copy in copies:
        copy.start()
    settle(copies)


def in_hbm(array):
    return pltpu.with_memory_space_constraint(array, pltpu.HBM)


def call(kernel, outs, *args, groups=None, owners=None, lengths=None, scratch=(), name=None):
    specs = [pl.BlockSpec(memory_space=pltpu.VMEM)] * len(args)
    if lengths is not None:
        args = (lengths, *args)
        specs = [pl.BlockSpec(memory_space=pltpu.SMEM), *specs]
    if owners is not None and groups is None:
        args = (owners, *args)
        specs = [pl.BlockSpec(memory_space=pltpu.SMEM), *specs]
    if groups is not None:
        picks = [[(index, distance) for _, index, distance in group] for group in groups]
        blocks = [in_hbm(array) if name in ('attend', 'mixer') else array for group in groups for array, _, _ in group]
        inner = kernel
        kernel = lambda *refs: inner(picks, *refs)
        args = (owners, *args, *blocks)
        specs = [pl.BlockSpec(memory_space=pltpu.SMEM), *specs]
        specs += [pl.BlockSpec(memory_space=pl.ANY)] * len(blocks)
    return pl.pallas_call(
        kernel,
        out_shape=tuple(jax.ShapeDtypeStruct(out[0], out[1]) for out in outs),
        in_specs=specs,
        out_specs=tuple(
            pl.BlockSpec(memory_space=pl.ANY if len(out) > 2 else pltpu.VMEM) for out in outs
        ),
        scratch_shapes=scratch,
        compiler_params=pltpu.CompilerParams(vmem_limit_bytes=VMEM_LIMIT),
        name=name,
    )(*args)


def shards(
    block_input,
    segment_lengths,
    entry_master,
    mixer_master,
    expand_master,
    shrink_master,
    block_vectors,
    block_cotangent,
    entry_moment,
    entry_square,
    mixer_moment,
    mixer_square,
    expand_moment,
    expand_square,
    shrink_moment,
    shrink_square,
    vector_moment,
    vector_square,
):
    rows, length, width = block_input.shape
    members = lax.axis_size("dp")
    place = lax.axis_index("dp")
    spot = lax.axis_index("tensor")
    core = spot % 2
    plane = spot // 2
    share = width // members
    tall = entry_master.shape[2]
    heads = 2 * tall // HD
    hidden = expand_master.shape[1]
    ringed = members <= RING_LIMIT

    if ringed:
        (attend_shard,) = call(
            pack_kernel, [((share, 4 * tall), low)], in_hbm(entry_master), in_hbm(mixer_master), name="pack"
        )
    else:
        attend_shard = jnp.concatenate([mixer_master.T, *entry_master], axis=1).astype(low)
    if ringed:
        (feed_shard,) = call(
            join_kernel, [((share, 2 * hidden), low)], in_hbm(expand_master), in_hbm(shrink_master.T), name="join"
        )
    else:
        feed_shard = jnp.concatenate([expand_master, shrink_master.T], axis=1).astype(low)

    def one_row(value):
        return lax.dynamic_index_in_dim(value, plane, 0, False)

    inputs = one_row(block_input)
    cotangent = one_row(block_cotangent)
    grid = (length, width)

    def mixer(blocks):
        rounded = (tall + 127) // 128 * 128
        return call(
            mixer_kernel, [((tall, width), low)], groups=[blocks], owners=owners, name="mixer",
            scratch=(
                pltpu.VMEM((width, rounded), low), pltpu.SemaphoreType.DMA((2 * len(blocks),))
            ),
        )[0]

    def attend(blocks, *gates):
        count = len(blocks)
        return call(
            attend_kernel,
            [
                ((2, length, 4 * tall), low),
                ((length, tall), low),
                ((tall, length), low),
                ((2, length, 128), wide),
                ((width, 4 * tall), low, "far"),
            ],
            after(block_input, *gates), groups=[blocks], owners=owners, lengths=segment_lengths, name="attend",
            scratch=(
                pltpu.VMEM((width, 4 * tall), low), pltpu.SemaphoreType.DMA((2 * count + 2,))
            ),
        )

    def mix(attended, attended_far, mixer_w, mixer_far, *gates):
        (mixed,) = call(
            mix_kernel, [(grid, low)], attended, after(attended_far, *gates), mixer_w, mixer_far, name="mix"
        )
        return mixed

    far = members // 2
    if ringed:
        owners = jnp.concatenate([owners_here(), core[None], plane[None]])
        attend_gather = Gather(attend_shard)
        feed_far = planes(feed_shard)
        for step in range(far):
            attend_gather.advance()
        mixer_w = mixer(attend_gather.blocks)
        packed, attended, attended_other, logs, attend_w = attend(attend_gather.blocks, mixer_w)
        feed_pair = jnp.concatenate([feed_shard, feed_far], axis=1)
        feed_gather = Twin(after(feed_pair, attend_gather.loads[1]))
        M, T = feed_gather.mine, feed_gather.theirs
        mixer_far = planes(mixer_w)
        attended_far = planes(after(attended_other, mixer_far))
        for step in range(far):
            feed_gather.advance(*({1: lambda: (*attend_gather.loads[3:], T[1]), 2: lambda: (T[2], attended), 3: lambda: (attended_far, mixer_far)}).get(step, tuple)())
            if step + 1 < far:
                feed_gather.follow(*({1: lambda: M[1:2], 2: lambda: M[2:3]}).get(step, tuple)())
            if step == far - 2:
                mixed = mix(attended, attended_far, mixer_w, mixer_far)
        feed_blocks = feed_gather.blocks
    else:
        owners = jnp.stack([jnp.zeros((), jnp.int32), core, plane])
        whole = lax.all_gather(attend_shard, "dp", axis=0, tiled=True)
        mixer_w = mixer([(whole, (), 0)])
        packed, attended, attended_other, logs, attend_w = attend([(whole, (), 0)])
        attended_far, mixer_far = planes(attended_other), planes(mixer_w)
        mixed = mix(attended, attended_far, mixer_w, mixer_far)
        whole = lax.all_gather(feed_shard, "dp", axis=0, tiled=True)
        feed_blocks = [(jnp.concatenate([whole, planes(whole)], axis=1), (), 0)]
    many = len(feed_blocks)

    mixed_other = cores(mixed)
    first_unit, first_scale, active, slope, shrunk, expand_w, shrink_w = call(
        feed_kernel,
        [
            (grid, wide),
            ((length, 128), wide),
            ((2, length, hidden), low),
            ((2, length, hidden), low),
            (grid, low),
            ((2, width, hidden), low, "far"),
            ((2, width, hidden), low, "far"),
        ],
        inputs, mixed, mixed_other, block_vectors,
        groups=[feed_blocks], owners=owners, name="feed",
        scratch=(
            pltpu.VMEM((2, width, hidden), low),
            pltpu.VMEM((2, width, hidden), low),
            pltpu.SemaphoreType.DMA((8 * many + 8,)),
        ),
    )
    shrunk_other = cores(shrunk)
    half = (length // 2, width)
    output, output_half, second_grad, second_low, second_sums = call(
        second_kernel,
        [(grid, low), (half, low), (grid, wide), (grid, low), ((8, width), wide)],
        first_unit, shrunk, shrunk_other, block_vectors, cotangent,
        owners=owners, name="second",
    )

    def pieces_of(columns, counts):
        return [((count, share if ringed else width, columns), low) for count in counts]

    singles = [1] * members if ringed else [1]

    def paired(pieces):
        middle = [tuple(pieces[i : i + 2]) for i in range(1, len(pieces) - 1, 2)]
        return [pieces[0], *middle, pieces[-1]]

    def swap(value):
        return planes(value.astype(low)).astype(wide)

    hidden_grad, partial = call(
        expand_kernel,
        [((2, length, hidden), low), (grid, wide)],
        second_low, slope, expand_w, shrink_w,
        name="expand",
    )
    partial_other = cores(partial)
    feed_pieces = call(
        weights_kernel,
        pieces_of(4 * hidden, singles),
        second_low, active, after(hidden_grad, partial), first_unit, block_vectors,
        owners=owners, scratch=(pltpu.VMEM((width, 4 * hidden), low),), name="weights",
    )
    feed_pieces = TwinPieces(paired(feed_pieces))
    partial_other = after(partial_other, feed_pieces.mine)
    first_half, sums, mixer_grad, mixer_grad_other, attended_grad, attended_grad_other = call(
        first_kernel,
        [
            (half, wide),
            ((8, width), wide),
            ((width, tall), low),
            ((tall, width), low),
            ((length, tall), low),
            ((tall, length), low),
        ],
        second_grad, partial, partial_other, first_unit, first_scale, block_vectors, attended, attended_far,
        second_sums, mixer_w, mixer_far, owners=owners, name="first", scratch=(pltpu.VMEM(grid, wide),),
    )

    def scattered(value):
        return lax.psum_scatter(value[0].astype(wide), "dp", scatter_dimension=0, tiled=True)

    attended_grad_far = planes(attended_grad_other)
    mixer_grad_far = planes(after(mixer_grad_other, attended_grad_far))
    sums_far = planes(after(sums, attended_grad_far))
    halves = [(half, wide), (half, low)]
    packed_grad, kept_own, sent_own = call(
        lambda *refs: entry_kernel(0, *refs),
        [((length, 4 * tall), low), *halves],
        packed, logs, after(attended_grad, attended_grad_far), attend_w,
        owners=owners, lengths=segment_lengths, name="entry", scratch=(pltpu.VMEM(grid, wide),),
    )
    if ringed:
        feed_pieces.advance(packed_grad, mixer_grad_far)
        feed_pieces.follow(packed_grad)
    columns = 4 * tall + 128
    *pieces, kept_other, sent_other = call(
        gather_kernel,
        [*pieces_of(columns, singles), *halves],
        packed, logs, after(attended_grad_far, packed_grad), attend_w, block_input,
        packed_grad, mixer_grad, mixer_grad_far, sums, sums_far, owners=owners, lengths=segment_lengths, name="gather",
        scratch=(
            pltpu.VMEM((width, columns), low),
            pltpu.VMEM((length, 4 * tall), low),
            pltpu.VMEM(grid, wide),
        ),
    )
    attend_pieces = Pieces(paired(pieces))
    output_half = planes(after(output_half, mixer_grad_far, sums_far))
    other_half = planes((kept_other + cores(sent_other).astype(wide)).astype(low))
    own_half = first_half + kept_own + cores(sent_own).astype(wide) + other_half.astype(wide)
    if ringed:
        feed_pieces.advance(attend_pieces.payload)
        feed_pieces.follow(attend_pieces.payload)
        fourth = feed_pieces.advance()
        others = feed_pieces.follow()
        attend_pieces.advance(fourth)
        third = attend_pieces.advance()
        feed_pieces.mine = after(feed_pieces.mine, others, third)
        feed_pair = feed_pieces.advance(output_half)
        attend_pieces.advance(other_half)
    else:
        feed_pair = scattered(feed_pieces.mine[None])
    (block_output,) = call(
        place_kernel, [((2, *grid), low)], output, output_half, cores(output_half), owners=owners, name="place"
    )
    (input_gradient,) = call(
        own_kernel,
        [((2, *grid), wide, "far")],
        own_half, cores(own_half), owners=owners, name="own", scratch=(pltpu.SemaphoreType.DMA((2,)),),
    )
    parts = [feed_pair[:, i * hidden : (i + 1) * hidden] for i in range(4)]
    feed_other = swap(jnp.concatenate([parts[1], parts[3]], axis=1))
    shrink_share = parts[0] + feed_other[:, :hidden]
    expand_share = parts[2] + feed_other[:, hidden:]
    other_squares = jnp.sum(shrink_share * shrink_share) + jnp.sum(expand_share * expand_share)
    if ringed:
        attend_pair = attend_pieces.advance(other_squares, block_output)
    else:
        attend_pair = scattered(pieces[0])
    inner = lax.axis_size("tensor")

    def near(squares):
        squares = squares + cores(squares)
        return squares + planes(squares)

    def reduced(squares):
        hop = 1
        while hop < members:
            squares = squares + lax.ppermute(squares, "dp", [(i, i ^ hop) for i in range(members)])
            hop *= 2
        return squares

    vector_width = width // members
    vector_master = lax.dynamic_slice_in_dim(block_vectors, place * vector_width, vector_width, 1)
    if ringed:
        others = jnp.where(lax.broadcasted_iota(jnp.int32, (8, 128), 1) == 0, other_squares / 8, 0.0)
        attend_pair, squares = call(
            lambda *refs: total_kernel(inner, *refs),
            [((share, columns), wide), ((8, 128), wide)],
            *attend_pair, others, name="total",
        )
        squares = near(squares)
        input_far = planes(after(own_half.astype(low), squares))
        squares = reduced(squares)
        input_far = after(input_far, squares)
        groups = [
            (entry_master, entry_moment, entry_square),
            (mixer_master, mixer_moment, mixer_square),
            (expand_master, expand_moment, expand_square),
            (shrink_master.T, shrink_moment.T, shrink_square.T),
            (vector_master, vector_moment, vector_square),
        ]
        sources = [array for group in groups for array in group]
        targets = []
        for i, group in enumerate(groups):
            targets += [(group[0].shape, wide)] * 3 + [(group[0].shape, low)] * (i < 4)
        in_place = pl.BlockSpec(memory_space=pltpu.HBM)
        held = pl.BlockSpec(memory_space=pltpu.VMEM)
        *rest, input_gradient = pl.pallas_call(
            adam_kernel,
            out_shape=[
                jax.ShapeDtypeStruct(shape, kind)
                for shape, kind in [((1, 1), wide), *targets, ((2, *grid), wide)]
            ],
            in_specs=[pl.BlockSpec(memory_space=pltpu.SMEM)] + [held] * 6 + [in_place] * 16,
            out_specs=[held] + [in_place] * 20,
            scratch_shapes=[
                *[pltpu.VMEM(array.shape, wide) for array in sources],
                *[pltpu.VMEM(shape, kind) for shape, kind in targets],
                pltpu.VMEM(grid, wide),
                pltpu.SemaphoreType.DMA((35,)),
            ],
            input_output_aliases={22: 20},
            compiler_params=pltpu.CompilerParams(vmem_limit_bytes=VMEM_LIMIT),
            name="adam",
        )(
            owners, attend_pair, expand_share, shrink_share, squares, input_far, cores(input_far),
            *map(in_hbm, sources), input_gradient,
        )
        norm, *news = rest
        news[12:16] = [array.T for array in news[12:16]]
        return (block_output, input_gradient, norm[0, 0], *news)

    attend_share = attend_pair[:, : 4 * tall]
    vector_sum = attend_pair[:, 4 * tall :]
    entry_share = jnp.stack([attend_share[:, c * tall : (c + 1) * tall] for c in range(1, 4)])
    mixer_share = attend_share[:, :tall].T
    vector_share = vector_sum[:, :6].T
    squares = other_squares + jnp.sum(attend_share * attend_share)
    squares = squares + jnp.sum(vector_share * vector_share) / inner
    squares = near(jnp.full((8, 128), squares))
    squares = reduced(squares)
    other = planes(own_half.astype(low))
    other, rest = other.astype(wide), cores(other).astype(wide)
    other = jnp.concatenate([jnp.where(core == 0, other, rest), jnp.where(core == 0, rest, other)], axis=0)
    input_gradient = lax.dynamic_update_index_in_dim(input_gradient, other, 1 - plane, 0)
    gradient_norm = jnp.sqrt(squares[0, 0])
    factor = jnp.minimum(1.0, clip_bound / (gradient_norm + 1e-06))
    results = []
    for grad, moment, square, master, rate in (
        (entry_share, entry_moment, entry_square, entry_master, rate_matrix),
        (mixer_share, mixer_moment, mixer_square, mixer_master, rate_mixer),
        (expand_share, expand_moment, expand_square, expand_master, rate_matrix),
        (shrink_share.T, shrink_moment, shrink_square, shrink_master, rate_matrix),
    ):
        new = adam_update(grad, moment, square, master, factor, rate, decay_matrix)
        results += [*new, new[2].astype(low)]
    results += adam_update(
        vector_share, vector_moment, vector_square, vector_master, factor, rate_vector, 0.0
    )
    return (block_output, input_gradient, gradient_norm, *results)


def solution(mesh):
    in_specs = (
        P("dp", None, None),
        P("dp", None),
        P(None, "dp", "tensor"),
        P("tensor", "dp"),
        P("dp", "tensor"),
        P("tensor", "dp"),
        P(),
        P("dp", None, None),
        P(None, "dp", "tensor"),
        P(None, "dp", "tensor"),
        P("tensor", "dp"),
        P("tensor", "dp"),
        P("dp", "tensor"),
        P("dp", "tensor"),
        P("tensor", "dp"),
        P("tensor", "dp"),
        P(None, "dp"),
        P(None, "dp"),
    )
    out_specs = (
        P("dp", None, None),
        P("dp", None, None),
        P(),
        P(None, "dp", "tensor"),
        P(None, "dp", "tensor"),
        P(None, "dp", "tensor"),
        P(None, "dp", "tensor"),
        P("tensor", "dp"),
        P("tensor", "dp"),
        P("tensor", "dp"),
        P("tensor", "dp"),
        P("dp", "tensor"),
        P("dp", "tensor"),
        P("dp", "tensor"),
        P("dp", "tensor"),
        P("tensor", "dp"),
        P("tensor", "dp"),
        P("tensor", "dp"),
        P("tensor", "dp"),
        P(None, "dp"),
        P(None, "dp"),
        P(None, "dp"),
    )
    return jax.shard_map(shards, mesh=mesh, in_specs=in_specs, out_specs=out_specs, check_vma=False)
```
